512 devices in a mesh: row: 32 (over x, z), col: 16 (over y, core).
Axes of the slice: x: 4, y: 8, z: 8, core: 2. Of those that a mesh axis runs over, the one named last changes fastest.
Arguments:
- object_field: float32 [2, 4096, 2048], P(None, 'row', 'col'), may hold values from -6 to 6
- amplitudes: bfloat16 [32, 16, 12, 128, 128], P('row', 'col'), may hold values from 0 to 2
- counts: int32 [32, 16], P('row', 'col'), may hold values from 1 to 12, as said below
- offsets: int32 [32, 16, 12, 2], P('row', 'col'), may hold values from 0 to 127
- mode_index: int32 [32, 16, 12], P('row', 'col'), may hold values from 0 to 15
- mix_table: float32 [16, 4], replicated, may hold values from -1 to 1
- probe_modes: float32 [4, 2, 128, 128], replicated, may hold values from -6 to 6
Outputs:
- new_object: float32 [2, 4096, 2048], P(None, 'row', 'col')
- new_modes: float32 [4, 2, 128, 128], replicated
The draws below stay inside these ranges and needn't reach their ends.
Inputs may be any that keep to these rules, and one draw needn't show every extreme that they name: `counts`: some tile lists exactly 12 positions and some tile exactly one; the others list between 6 and 12.
All inputs are finite; a program needn't handle non-finite values.
Results may differ from the reference program's by a relative error of at most 0.0009.
The reference program's roundings to bfloat16 on the way count: a program that leaves them out, or rounds other values in their place, can miss the bound.
Values sent between devices are 32-bit elements; how exact they have to be, the bound alone decides.
A program may use at most 64 MiB of HBM per device.

```python
import math
import jax
import jax.numpy as jnp
from jax import lax

FRAME = 128
TILE = 128
CAP = 12
MODES = 4
MIXES = 16
TILE_ROWS = 32
TILE_COLS = 16
OBJ_ROWS = 4096
OBJ_COLS = 2048


rank_weights = [160, 120, 100, 80, 40, 32, 26, 20, 8, 6, 5, 4, 2, 1, 1, 1]


def draw_counts(key, part):
    fill_key, spot_key, other_key = jax.random.split(jax.random.fold_in(key, 17), 3)
    total = TILE_ROWS * TILE_COLS
    listed = jax.random.randint(fill_key, (total,), (CAP + 1) // 2, CAP + 1)
    spot = jax.random.randint(spot_key, (), 0, total)
    other = (spot + jax.random.randint(other_key, (), 1, total)) % total
    listed = listed.at[spot].set(CAP)
    listed = listed.at[other].set(1)
    return listed.reshape(TILE_ROWS, TILE_COLS).astype(jnp.int32)


def ranking(key):
    row_key, group_key = jax.random.split(jax.random.fold_in(key, 29))
    rows_by_rank = jax.random.permutation(row_key, MIXES).astype(jnp.int32)
    group_mode = jax.random.permutation(group_key, MODES).astype(jnp.int32)
    return (rows_by_rank, group_mode)


def draw_mode_index(key, part):
    rows_by_rank, group_mode = ranking(key)
    ticket_key, spot_key, other_key = jax.random.split(jax.random.fold_in(key, 31), 3)
    limits = jnp.cumsum(jnp.array(rank_weights, dtype=jnp.int32))
    whole = sum(rank_weights)
    ticket = jax.random.randint(ticket_key, (TILE_ROWS, TILE_COLS, CAP), 0, whole)
    ranks = jnp.sum((ticket[..., None] >= limits).astype(jnp.int32), -1)
    chosen = rows_by_rank[ranks].reshape(-1)
    length = TILE_ROWS * TILE_COLS * CAP
    spot = jax.random.randint(spot_key, (), 0, length)
    other = (spot + jax.random.randint(other_key, (), 1, length)) % length
    chosen = chosen.at[spot].set(0)
    chosen = chosen.at[other].set(MIXES - 1)
    return chosen.reshape(TILE_ROWS, TILE_COLS, CAP).astype(jnp.int32)


def draw_mix_table(key, part):
    rows_by_rank, group_mode = ranking(key)
    rank_of_row = jnp.zeros((MIXES,), jnp.int32).at[rows_by_rank].set(jnp.arange(MIXES, dtype=jnp.int32))
    dominant = group_mode[rank_of_row // (MIXES // MODES)]
    small_key, size_key, sign_key = jax.random.split(jax.random.fold_in(key, 37), 3)
    minor = jax.random.uniform(small_key, (MIXES, MODES), jnp.float32, -0.15, 0.15)
    major = jax.random.uniform(size_key, (MIXES,), jnp.float32, 0.8, 1.0)
    signs = (jax.random.randint(sign_key, (MIXES,), 0, 2) * 2 - 1).astype(jnp.float32)
    picked = jnp.arange(MODES, dtype=jnp.int32)[None, :] == dominant[:, None]
    table = jnp.where(picked, (signs * major)[:, None], minor)
    return table.astype(jnp.float32)


def draw_object_field(key, part):
    base_key, scale_key = jax.random.split(jax.random.fold_in(key, 41), 2)
    shape = (2, OBJ_ROWS, OBJ_COLS)
    scales = jnp.exp(jax.random.uniform(scale_key, (OBJ_ROWS, OBJ_COLS), jnp.float32, math.log(0.25), math.log(2.0)))
    values = jax.random.normal(base_key, shape, jnp.float32) * scales[None]
    return jnp.clip(values, -6.0, 6.0).astype(jnp.float32)


def plant(entries, own_key, low, largest):
    extent = entries.shape
    index_at = [jax.random.randint(jax.random.fold_in(own_key, axis), (), 0, extent[axis]) for axis in range(len(extent))]
    entries = entries.at[tuple(index_at)].set(low)
    longest = extent.index(max(extent))
    index_at[longest] = (index_at[longest] + 1) % extent[longest]
    return entries.at[tuple(index_at)].set(largest)


def block_scale(own_key, dims, pieces, least, top_value):
    factor_of, own = 1.0, jax.random.fold_in(own_key, 6)
    for dim, shards_of in pieces:
        steps = jnp.exp(jax.random.uniform(jax.random.fold_in(own, dim), (shards_of,), jnp.float32, least / len(pieces), top_value / len(pieces)))
        factor_of = factor_of * jnp.repeat(steps, dims[dim] // shards_of).reshape([-1 if axis == dim else 1 for axis in range(len(dims))])
    return factor_of


def bell_draw(rng, extent, spread, bound, kind=jnp.bfloat16):
    return jnp.clip(spread * jax.random.normal(rng, extent, jnp.float32), -bound, bound).astype(kind)


def setup_inputs(seed: int = 0) -> dict:
    splits = jax.random.split(jax.random.key(seed), 8)
    return {
        "object_field": draw_object_field(jax.random.fold_in(splits[7], 71), 0),
        "amplitudes": jnp.clip(2.0 * jax.random.uniform(splits[1], (TILE_ROWS, TILE_COLS, CAP, FRAME, FRAME), jnp.float32) ** block_scale(splits[1], (TILE_ROWS, TILE_COLS, CAP, FRAME, FRAME), ((0, 32), (1, 16)), -0.2, 0.2), 0.0, 2.0).astype(jnp.bfloat16),
        "counts": draw_counts(jax.random.fold_in(splits[7], 71), 0),
        "offsets": plant(jax.random.randint(splits[3], (TILE_ROWS, TILE_COLS, CAP, 2), 0, TILE), jax.random.fold_in(splits[3], 1), 0, TILE - 1).astype(jnp.int32),
        "mode_index": draw_mode_index(jax.random.fold_in(splits[7], 71), 0),
        "mix_table": draw_mix_table(jax.random.fold_in(splits[7], 71), 0),
        "probe_modes": bell_draw(splits[6], (MODES, 2, FRAME, FRAME), 0.7, 6.0, jnp.float32),
    }


FLOOR = 0.25
RELAX = 0.5
EPSILON = 1e-06

def tables(size):
    index = jnp.arange(size, dtype=jnp.int32)
    product = index[:, None] * index[None, :] % size
    angle = product.astype(jnp.float32) * (2.0 * math.pi / size)
    factor = 1.0 / math.sqrt(size)
    return ((jnp.cos(angle) * factor).astype(jnp.bfloat16), (jnp.sin(angle) * factor).astype(jnp.bfloat16))

def left_apply(cosine, sine, real, imag, sign):
    size = real.shape[0]
    stacked = jnp.dot(jnp.concatenate([cosine, sine], 0), jnp.concatenate([real, imag], 1), preferred_element_type=jnp.float32)
    out_real = stacked[:size, :size] - sign * stacked[size:, size:]
    out_imag = stacked[:size, size:] + sign * stacked[size:, :size]
    return (out_real, out_imag)

def right_apply(cosine, sine, real, imag, sign):
    size = real.shape[0]
    stacked = jnp.dot(jnp.concatenate([real, imag], 0), jnp.concatenate([cosine, sine], 1), preferred_element_type=jnp.float32)
    out_real = stacked[:size, :size] - sign * stacked[size:, size:]
    out_imag = stacked[size:, :size] + sign * stacked[:size, size:]
    return (out_real, out_imag)

def mix_probe(weights, modes):
    real = weights[0] * modes[0, 0]
    imag = weights[0] * modes[0, 1]
    for k in range(1, modes.shape[0]):
        real = real + weights[k] * modes[k, 0]
        imag = imag + weights[k] * modes[k, 1]
    return (real, imag)

def exit_change(patch, probe_real, probe_imag, amp, cosine, sine):
    psi_real = probe_real * patch[0] - probe_imag * patch[1]
    psi_imag = probe_real * patch[1] + probe_imag * patch[0]
    front_real, front_imag = left_apply(cosine, sine, psi_real.astype(jnp.bfloat16), psi_imag.astype(jnp.bfloat16), -1.0)
    spec_real, spec_imag = right_apply(cosine, sine, front_real.astype(jnp.bfloat16), front_imag.astype(jnp.bfloat16), -1.0)
    magnitude = jnp.sqrt(spec_real * spec_real + spec_imag * spec_imag)
    ratio = amp.astype(jnp.float32) / jnp.maximum(magnitude, FLOOR)
    fixed_real = (spec_real * ratio).astype(jnp.bfloat16)
    fixed_imag = (spec_imag * ratio).astype(jnp.bfloat16)
    back_real, back_imag = left_apply(cosine, sine, fixed_real, fixed_imag, 1.0)
    out_real, out_imag = right_apply(cosine, sine, back_real.astype(jnp.bfloat16), back_imag.astype(jnp.bfloat16), 1.0)
    return (out_real - psi_real, out_imag - psi_imag)

def position_terms(patch, weights, modes, amp, cosine, sine):
    probe_real, probe_imag = mix_probe(weights, modes)
    delta_real, delta_imag = exit_change(patch, probe_real, probe_imag, amp, cosine, sine)
    object_piece = jnp.stack([probe_real * delta_real + probe_imag * delta_imag, probe_real * delta_imag - probe_imag * delta_real, probe_real * probe_real + probe_imag * probe_imag])
    mode_piece = jnp.stack([patch[0] * delta_real + patch[1] * delta_imag, patch[0] * delta_imag - patch[1] * delta_real, patch[0] * patch[0] + patch[1] * patch[1]])
    factor = jnp.stack([weights, weights, weights * weights], 1)
    return (object_piece, factor[:, :, None, None] * mode_piece[None])

def orthonormal_sequential(flat, reduce_value, count):
    basis = []
    for k in range(flat.shape[0]):
        vec_real, vec_imag = (flat[k, 0], flat[k, 1])
        if basis:
            parts = []
            for base_real, base_imag in basis:
                parts.append(jnp.sum(base_real * vec_real + base_imag * vec_imag))
                parts.append(jnp.sum(base_real * vec_imag - base_imag * vec_real))
            coeffs = reduce_value(jnp.stack(parts)) / count
            for j in range(len(basis)):
                base_real, base_imag = basis[j]
                coef_real, coef_imag = (coeffs[2 * j], coeffs[2 * j + 1])
                vec_real = vec_real - (coef_real * base_real - coef_imag * base_imag)
                vec_imag = vec_imag - (coef_real * base_imag + coef_imag * base_real)
        length = reduce_value(jnp.sum(vec_real * vec_real + vec_imag * vec_imag)) / count
        scale = 1.0 / jnp.sqrt(length + EPSILON)
        basis.append((vec_real * scale, vec_imag * scale))
    return jnp.stack([jnp.stack([pair[0], pair[1]]) for pair in basis])

def reference(object_field, amplitudes, counts, offsets, mode_index, mix_table, probe_modes):
    frame = probe_modes.shape[-1]
    half = frame // 2
    tile = TILE
    cosine, sine = tables(frame)
    padded = jnp.pad(object_field, ((0, 0), (half, half), (half, half)))
    margins = jnp.zeros((3, padded.shape[1], padded.shape[2]), jnp.float32)
    sums = jnp.zeros((probe_modes.shape[0], 3, frame, frame), jnp.float32)
    zero = jnp.zeros((), jnp.int32)

    def tile_step(flat, carry):
        flat = jnp.asarray(flat).astype(jnp.int32)
        tile_row = (flat // TILE_COLS).astype(jnp.int32)
        tile_col = (flat % TILE_COLS).astype(jnp.int32)

        def visit(slot, inner):
            margin_acc, sum_acc = inner
            slot = jnp.asarray(slot).astype(jnp.int32)
            top = (tile_row * tile + offsets[tile_row, tile_col, slot, 0]).astype(jnp.int32)
            left = (tile_col * tile + offsets[tile_row, tile_col, slot, 1]).astype(jnp.int32)
            patch = lax.dynamic_slice(padded, (zero, top, left), (2, frame, frame))
            weights = mix_table[mode_index[tile_row, tile_col, slot]]
            amp = amplitudes[tile_row, tile_col, slot]
            object_piece, mode_piece = position_terms(patch, weights, probe_modes, amp, cosine, sine)
            current = lax.dynamic_slice(margin_acc, (zero, top, left), (3, frame, frame))
            margin_acc = lax.dynamic_update_slice(margin_acc, current + object_piece, (zero, top, left))
            return (margin_acc, sum_acc + mode_piece)
        return lax.fori_loop(jnp.zeros((), jnp.int32), counts[tile_row, tile_col].astype(jnp.int32), visit, carry)
    margins, sums = lax.fori_loop(0, TILE_ROWS * TILE_COLS, tile_step, (margins, sums))
    inner = margins[:, half:half + object_field.shape[1], half:half + object_field.shape[2]]
    new_object = object_field + inner[:2] / (inner[2] + RELAX)
    fresh = probe_modes + sums[:, :2] / (sums[:, 2:3] + RELAX)
    flat = fresh.reshape(fresh.shape[0], 2, frame * frame)
    ortho = orthonormal_sequential(flat, lambda values: values, float(frame * frame))
    return (new_object, ortho.reshape(probe_modes.shape))
```

```python
import functools

import jax
import jax.numpy as jnp
import ml_dtypes
import numpy as np
from jax import lax
from jax.experimental import pallas as pl
from jax.experimental.pallas import tpu as pltpu
from jax.sharding import PartitionSpec as P

FLOOR = 0.25
RELAX = 0.5
EPSILON = 1e-06
GROUP = 2
MESH = pl.DeviceIdType.MESH
VMEM = pl.BlockSpec(memory_space=pltpu.VMEM)
SMEM = pl.BlockSpec(memory_space=pltpu.SMEM)


def tables(size):
    index = np.arange(size)
    angle = (index[:, None] * index[None, :] % size).astype(np.float32) * np.float32(2.0 * np.pi / size)
    factor = np.float32(1.0 / np.sqrt(size))
    c = (np.cos(angle) * factor).astype(ml_dtypes.bfloat16)
    s = (np.sin(angle) * factor).astype(ml_dtypes.bfloat16)
    p = np.concatenate([np.concatenate([c, s], 1), np.concatenate([-s, c], 1)], 0)
    q = np.concatenate([np.concatenate([c, -s], 1), np.concatenate([s, c], 1)], 0)
    return np.stack([p, q])


def lanes_iota(shape):
    return lax.broadcasted_iota(jnp.int32, shape, len(shape) - 1)


def pack_low(x):
    n = x.shape[1] // 2
    a, b = x[:, :n], x[:, n:]
    return jnp.where(lanes_iota(a.shape) < 64, a, pltpu.roll(b, 64, 2))


def pack_high(x):
    n = x.shape[1] // 2
    a, b = x[:, :n], x[:, n:]
    return jnp.where(lanes_iota(a.shape) < 64, pltpu.roll(a, 64, 2), b)


def unpack_low(x):
    return jnp.concatenate([x, pltpu.roll(x, 64, 2)], 1)


def unpack_high(x):
    return jnp.concatenate([pltpu.roll(x, 64, 2), x], 1)


def place(rows, cols):
    row, col = lax.axis_index("row"), lax.axis_index("col")
    around = {}
    for dr in (-1, 0, 1):
        for dc in (-1, 0, 1):
            if dr or dc:
                around[dr, dc] = (lax.rem(row + dr + rows, rows), lax.rem(col + dc + cols, cols))
    return row, col, around


def inside(row, col, rows, cols, dr, dc):
    ok = jnp.float32(1.0)
    if dr == -1:
        ok = ok * (row > 0).astype(jnp.float32)
    if dr == 1:
        ok = ok * (row < rows - 1).astype(jnp.float32)
    if dc == -1:
        ok = ok * (col > 0).astype(jnp.float32)
    if dc == 1:
        ok = ok * (col < cols - 1).astype(jnp.float32)
    return ok


SIDES = [(-1, 0), (1, 0), (0, -1), (0, 1), (-1, -1), (-1, 1), (1, -1), (1, 1)]


def greet(devices):
    barrier = pltpu.get_barrier_semaphore()
    for device in devices:
        pl.semaphore_signal(barrier, inc=1, device_id=device, device_id_type=MESH)
    pl.semaphore_wait(barrier, len(devices))


def halo_kernel(rows, cols, o_ref, t_ref, ps, pc, rv, rs, rc, send, recv):
    row, col, around = place(rows, cols)
    o = o_ref[...]
    ps[0] = pack_low(o)
    ps[1] = pack_high(o)
    pc[0] = pack_low(o[:, :64])
    pc[1] = pack_high(o[:, :64])
    pc[2] = pack_low(o[:, 64:])
    pc[3] = pack_high(o[:, 64:])
    greet([around[s] for s in SIDES])
    source = {
        (-1, 0): o_ref.at[:, 0:64],
        (1, 0): o_ref.at[:, 64:128],
        (0, -1): ps.at[0],
        (0, 1): ps.at[1],
        (-1, -1): pc.at[0],
        (-1, 1): pc.at[1],
        (1, -1): pc.at[2],
        (1, 1): pc.at[3],
    }
    target = {
        (-1, 0): rv.at[0],
        (1, 0): rv.at[1],
        (0, -1): rs.at[0],
        (0, 1): rs.at[1],
        (-1, -1): rc.at[0],
        (-1, 1): rc.at[1],
        (1, -1): rc.at[2],
        (1, 1): rc.at[3],
    }
    copies = []
    for i, s in enumerate(SIDES):
        copy = pltpu.make_async_remote_copy(
            src_ref=source[s], dst_ref=target[s], send_sem=send.at[i], recv_sem=recv.at[i],
            device_id=around[s], device_id_type=MESH,
        )
        copy.start()
        copies.append(copy)
    t_ref[:, 1, 64:192] = o
    for copy in copies:
        copy.wait()

    def ok(dr, dc):
        return inside(row, col, rows, cols, dr, dc)

    t_ref[:, 1, 192:256] = rv[0] * ok(1, 0)
    t_ref[:, 1, 0:64] = rv[1] * ok(-1, 0)
    t_ref[:, 2, 64:192] = unpack_low(rs[0] * ok(0, 1))
    t_ref[:, 0, 64:192] = unpack_high(rs[1] * ok(0, -1))
    t_ref[:, 2, 192:256] = unpack_low(rc[0] * ok(1, 1))
    t_ref[:, 0, 192:256] = unpack_high(rc[1] * ok(1, -1))
    t_ref[:, 2, 0:64] = unpack_low(rc[2] * ok(-1, 1))
    t_ref[:, 0, 0:64] = unpack_high(rc[3] * ok(-1, -1))


def work_kernel(cap, mixes, counts, offs, index, mix, t_ref, modes, amps, tab, m_ref, s_ref):
    n = 128
    m_ref[...] = jnp.zeros_like(m_ref)
    s_ref[...] = jnp.zeros_like(s_ref)
    count = counts[0, 0]
    fwd, inv = tab[0], tab[1]

    def dot(a, b):
        return jnp.dot(a, b, preferred_element_type=jnp.float32)

    def left(table, res, ims):
        out = dot(table, jnp.concatenate([jnp.concatenate(res, 1), jnp.concatenate(ims, 1)], 0))
        return (
            [out[:n, i * n : (i + 1) * n] for i in range(len(res))],
            [out[n:, i * n : (i + 1) * n] for i in range(len(res))],
        )

    def right(table, res, ims):
        out = dot(jnp.concatenate([jnp.concatenate([a, b], 1) for a, b in zip(res, ims)], 0), table)
        return (
            [out[i * n : (i + 1) * n, :n] for i in range(len(res))],
            [out[i * n : (i + 1) * n, n:] for i in range(len(res))],
        )

    def half(xs):
        return [x.astype(jnp.bfloat16) for x in xs]

    lane = lanes_iota((n, n))

    def visit(step, carry):
        slots = [step * GROUP + i for i in range(GROUP)]
        where, weights, patches, probes, psi = [], [], [], [], []
        for slot in slots:
            top = jnp.clip(offs[0, 0, slot, 0], 0, n - 1)
            left_px = jnp.clip(offs[0, 0, slot, 1], 0, n - 1)
            first = left_px // 64
            shift = lax.rem(left_px + 64, n)
            pick = jnp.clip(index[0, 0, slot], 0, mixes - 1)
            listed = slot < count
            w = [jnp.where(listed, mix[pick, k], 0.0) for k in range(4)]
            mask = lane >= shift
            patch = []
            for comp in range(2):
                a = t_ref[comp, first, pl.ds(top, n), :]
                b = t_ref[comp, first + 1, pl.ds(top, n), :]
                patch.append(pltpu.roll(jnp.where(mask, a, b), lax.rem(n - shift, n), 1))
            probe = []
            for comp in range(2):
                total = w[0] * modes[0, comp]
                for k in range(1, 4):
                    total = total + w[k] * modes[k, comp]
                probe.append(total)
            where.append((top, first, shift, mask))
            weights.append(w)
            patches.append(patch)
            probes.append(probe)
            psi.append(
                (
                    probe[0] * patch[0] - probe[1] * patch[1],
                    probe[0] * patch[1] + probe[1] * patch[0],
                )
            )
        re, im = left(fwd, half([p[0] for p in psi]), half([p[1] for p in psi]))
        re, im = right(inv, half(re), half(im))
        fixed_re, fixed_im = [], []
        for slot, a, b in zip(slots, re, im):
            ratio = amps[0, 0, slot].astype(jnp.float32) * lax.rsqrt(jnp.maximum(a * a + b * b, FLOOR * FLOOR))
            fixed_re.append((a * ratio).astype(jnp.bfloat16))
            fixed_im.append((b * ratio).astype(jnp.bfloat16))
        re, im = left(inv, fixed_re, fixed_im)
        re, im = right(fwd, half(re), half(im))
        pieces = []
        for i in range(GROUP):
            dr, di = re[i] - psi[i][0], im[i] - psi[i][1]
            pr, pi = probes[i]
            ar, ai = patches[i]
            top, first, shift, mask = where[i]
            for f, value in enumerate((pr * dr + pi * di, pr * di - pi * dr, pr * pr + pi * pi)):
                rolled = pltpu.roll(value, shift, 1)
                m_ref[f, first, pl.ds(top, n), :] += jnp.where(mask, rolled, 0.0)
                m_ref[f, first + 1, pl.ds(top, n), :] += jnp.where(mask, 0.0, rolled)
            pieces.append((ar * dr + ai * di, ar * di - ai * dr, ar * ar + ai * ai))
        for k in range(4):
            for f in range(3):
                total = s_ref[k, f]
                for i in range(GROUP):
                    w = weights[i][k]
                    total = total + (w if f < 2 else w * w) * pieces[i][f]
                s_ref[k, f] = total
        return carry

    lax.fori_loop(0, cap // GROUP, visit, 0)


def reduce_kernel(
    rows, cols, nx, n1,
    o_ref, m_ref, s_ref, modes, new_object, new_modes,
    op, oc, orv, ors, orc, got, half, r1, r2, r3, fresh, send, recv,
):
    nz = rows // nx
    row, col, around = place(rows, cols)
    x, z = row // nz, lax.rem(row, nz)
    y, core = col // 2, lax.rem(col, 2)
    p1 = z + core * (y - z)
    p2 = y + core * (z - y)
    sibling = (row, col + 1 - 2 * core)
    high = 2 * core

    def first_peer(a):
        return (x * nz + z + (1 - core) * (a - z), (y + core * (a - y)) * 2 + core)

    def second_peer(a):
        return (x * nz + z + core * (a - z), (y + (1 - core) * (a - y)) * 2 + core)

    def x_peer(a):
        return (a * nz + z, col)

    firsts = [lax.rem(p1 + d, n1) for d in range(1, n1)]
    seconds = [lax.rem(p2 + d, n1) for d in range(1, n1)]
    xs = [lax.rem(x + d, nx) for d in range(1, nx)]
    used = [0]

    def copy(src, dst, device):
        i = used[0]
        used[0] += 1
        made = pltpu.make_async_remote_copy(
            src_ref=src, dst_ref=dst, send_sem=send.at[i], recv_sem=recv.at[i],
            device_id=device, device_id_type=MESH,
        )
        made.start()
        return made

    thick = 128 // n1
    op[0] = pack_high(m_ref[:, 0, 64:192])
    op[1] = pack_low(m_ref[:, 2, 64:192])
    oc[0] = pack_high(m_ref[:, 0, 0:64])
    oc[1] = pack_low(m_ref[:, 2, 0:64])
    oc[2] = pack_high(m_ref[:, 0, 192:256])
    oc[3] = pack_low(m_ref[:, 2, 192:256])
    greet(
        [around[s] for s in SIDES]
        + [sibling]
        + [first_peer(a) for a in firsts]
        + [second_peer(a) for a in seconds]
        + [x_peer(a) for a in xs]
    )
    pending = []
    pair = copy(s_ref.at[pl.ds(2 - high, 2)], got, sibling)
    pair.wait_recv()
    half[...] = s_ref[pl.ds(high, 2)] + got[...]
    pending.append(pair)
    sent = [
        copy(half.at[:, :, pl.ds(pl.multiple_of(a * thick, thick), thick)], r1.at[d], first_peer(a))
        for d, a in enumerate(firsts)
    ]
    edge = [
        copy(m_ref.at[:, 1, 0:64], orv.at[0], around[-1, 0]),
        copy(m_ref.at[:, 1, 192:256], orv.at[1], around[1, 0]),
        copy(op.at[0], ors.at[0], around[0, -1]),
        copy(op.at[1], ors.at[1], around[0, 1]),
        copy(oc.at[0], orc.at[0], around[-1, -1]),
        copy(oc.at[1], orc.at[1], around[-1, 1]),
        copy(oc.at[2], orc.at[2], around[1, -1]),
        copy(oc.at[3], orc.at[3], around[1, 1]),
    ]
    mine = pl.ds(pl.multiple_of(p1 * thick, thick), thick)
    total = half[:, :, mine]
    for d, c in enumerate(sent):
        c.wait_recv()
        total = total + r1[d]
    pending += sent
    tiles = thick // 8
    for m in range(2):
        for t in range(tiles):
            r2[m * tiles + t] = total[m, :, t * 8 : (t + 1) * 8]
    sent = [copy(r2.at[a], r2.at[nx + d], x_peer(a)) for d, a in enumerate(xs)]
    total = r2[x]
    for d, c in enumerate(sent):
        c.wait_recv()
        total = total + r2[nx + d]
    pending += sent
    r3[p2] = total
    sent = [copy(r3.at[p2], r3.at[p2], second_peer(a)) for a in seconds]
    for c in sent:
        c.wait_recv()
    pending += sent
    total = r3[0]
    for a in range(1, n1):
        total = total + r3[a]
    mode, tile = high + x // tiles, lax.rem(x, tiles)
    unit = pl.ds(pl.multiple_of(p1 * thick + tile * 8, 8), 8)
    fresh[mode, :, unit] = modes[mode, :, unit] + total[:2] / (total[2:] + RELAX)
    sent = [copy(fresh.at[mode, :, unit], fresh.at[mode, :, unit], x_peer(a)) for a in xs]
    for c in sent:
        c.wait_recv()
    pending += sent
    both = pl.ds(high, 2)
    sent = [copy(fresh.at[both, :, mine], fresh.at[both, :, mine], first_peer(a)) for a in firsts]

    for c in edge:
        c.wait_recv()
    pending += edge

    def ok(dr, dc):
        return inside(row, col, rows, cols, dr, dc)

    lane = lanes_iota((3, 64, 128))
    west = unpack_low(ors[1] * ok(0, -1))
    east = unpack_high(ors[0] * ok(0, 1))
    for part, vertical, low, top in (
        (slice(0, 64), orv[1] * ok(-1, 0), orc[3] * ok(-1, -1), orc[2] * ok(-1, 1)),
        (slice(64, 128), orv[0] * ok(1, 0), orc[1] * ok(1, -1), orc[0] * ok(1, 1)),
    ):
        sums = m_ref[:, 1, 64 + part.start : 64 + part.stop] + vertical
        side = jnp.where(
            lane < 64, west[:, part] + unpack_low(low), east[:, part] + unpack_high(top)
        )
        sums = sums + side
        new_object[:, part] = o_ref[:, part] + sums[:2] / (sums[2:] + RELAX)

    for c in sent:
        c.wait_recv()
    pending += sent
    pair = copy(fresh.at[both], fresh.at[both], sibling)
    pair.wait_recv()
    pending.append(pair)

    scale = 1.0 / (128 * 128)

    def mean(v):
        return jnp.sum(jnp.sum(v, 0, keepdims=True), 1, keepdims=True) * scale

    basis = []
    coefs = {}
    for k in range(4):
        vr, vi = fresh[k, 0], fresh[k, 1]
        for j in range(k):
            cr, ci = coefs[j, k]
            br, bi = basis[j]
            vr = vr - (cr * br - ci * bi)
            vi = vi - (cr * bi + ci * br)
        norm = 1.0 / jnp.sqrt(mean(vr * vr + vi * vi) + EPSILON)
        qr, qi = vr * norm, vi * norm
        basis.append((qr, qi))
        new_modes[k, 0] = qr
        new_modes[k, 1] = qi
        for later in range(k + 1, 4):
            fr, fi = fresh[later, 0], fresh[later, 1]
            coefs[k, later] = (mean(qr * fr + qi * fi), mean(qr * fi - qi * fr))
    for c in pending:
        c.wait_send()


def halo(rows, cols, object_field):
    f32 = jnp.float32
    return pl.pallas_call(
        functools.partial(halo_kernel, rows, cols),
        out_shape=jax.ShapeDtypeStruct((2, 3, 256, 128), f32),
        in_specs=[VMEM],
        out_specs=VMEM,
        scratch_shapes=[
            pltpu.VMEM((2, 2, 64, 128), f32),
            pltpu.VMEM((4, 2, 32, 128), f32),
            pltpu.VMEM((2, 2, 64, 128), f32),
            pltpu.VMEM((2, 2, 64, 128), f32),
            pltpu.VMEM((4, 2, 32, 128), f32),
            pltpu.SemaphoreType.DMA((8,)),
            pltpu.SemaphoreType.DMA((8,)),
        ],
        compiler_params=pltpu.CompilerParams(collective_id=0, has_side_effects=True),
        name="halo",
    )(object_field)


def work(counts, offsets, mode_index, mix_table, tiles, probe_modes, amplitudes):
    f32 = jnp.float32
    return pl.pallas_call(
        functools.partial(work_kernel, amplitudes.shape[2], mix_table.shape[0]),
        out_shape=(
            jax.ShapeDtypeStruct((3, 3, 256, 128), f32),
            jax.ShapeDtypeStruct((4, 3, 128, 128), f32),
        ),
        in_specs=[SMEM] * 4 + [VMEM] * 4,
        out_specs=(VMEM, VMEM),
        compiler_params=pltpu.CompilerParams(vmem_limit_bytes=48 * 1024 * 1024),
        name="work",
    )(counts, offsets, mode_index, mix_table, tiles, probe_modes, amplitudes, jnp.asarray(tables(128)))


def reduce(rows, cols, nx, object_field, margins, sums, probe_modes):
    f32 = jnp.float32
    n1 = cols // 2
    count = 8 + 2 + 4 * (n1 - 1) + 2 * (nx - 1)
    return pl.pallas_call(
        functools.partial(reduce_kernel, rows, cols, nx, n1),
        out_shape=(
            jax.ShapeDtypeStruct((2, 128, 128), f32),
            jax.ShapeDtypeStruct((4, 2, 128, 128), f32),
        ),
        in_specs=[VMEM] * 4,
        out_specs=(VMEM, VMEM),
        scratch_shapes=[
            pltpu.VMEM((2, 3, 64, 128), f32),
            pltpu.VMEM((4, 3, 32, 128), f32),
            pltpu.VMEM((2, 3, 64, 128), f32),
            pltpu.VMEM((2, 3, 64, 128), f32),
            pltpu.VMEM((4, 3, 32, 128), f32),
            pltpu.VMEM((2, 3, 128, 128), f32),
            pltpu.VMEM((2, 3, 128, 128), f32),
            pltpu.VMEM((n1 - 1, 2, 3, 128 // n1, 128), f32),
            pltpu.VMEM((2 * nx, 3, 8, 128), f32),
            pltpu.VMEM((n1, 3, 8, 128), f32),
            pltpu.VMEM((4, 2, 128, 128), f32),
            pltpu.SemaphoreType.DMA((count,)),
            pltpu.SemaphoreType.DMA((count,)),
        ],
        compiler_params=pltpu.CompilerParams(
            collective_id=1, has_side_effects=True, vmem_limit_bytes=48 * 1024 * 1024
        ),
        name="reduce",
    )(object_field, margins, sums, probe_modes)


def solution(mesh):
    rows, cols = mesh.shape["row"], mesh.shape["col"]
    nx = 4

    def body(object_field, amplitudes, counts, offsets, mode_index, mix_table, probe_modes):
        tiles = halo(rows, cols, object_field)
        margins, sums = work(counts, offsets, mode_index, mix_table, tiles, probe_modes, amplitudes)
        return reduce(rows, cols, nx, object_field, margins, sums, probe_modes)

    return jax.shard_map(
        body,
        mesh=mesh,
        in_specs=(
            P(None, "row", "col"),
            P("row", "col", None, None, None),
            P("row", "col"),
            P("row", "col", None, None),
            P("row", "col", None),
            P(),
            P(),
        ),
        out_specs=(P(None, "row", "col"), P()),
        check_vma=False,
    )
```

```python
import functools

import jax
import jax.numpy as jnp
import ml_dtypes
import numpy as np
from jax import lax
from jax.experimental import pallas as pl
from jax.experimental.pallas import tpu as pltpu
from jax.sharding import PartitionSpec as P

FLOOR = 0.25
RELAX = 0.5
EPSILON = 1e-06
GROUP = 2
FAR = (4, 3, 5, 2, 6, 1, 7)
NEAR = (1, 7, 2, 6, 3, 5, 4)
MESH = pl.DeviceIdType.MESH
VMEM = pl.BlockSpec(memory_space=pltpu.VMEM)
HBM = pl.BlockSpec(memory_space=pltpu.HBM)


def tables(size):
    index = np.arange(size)
    angle = (index[:, None] * index[None, :] % size).astype(np.float32) * np.float32(2.0 * np.pi / size)
    factor = np.float32(1.0 / np.sqrt(size))
    c = (np.cos(angle) * factor).astype(ml_dtypes.bfloat16)
    s = (np.sin(angle) * factor).astype(ml_dtypes.bfloat16)
    p = np.concatenate([np.concatenate([c, s], 1), np.concatenate([-s, c], 1)], 0)
    q = np.concatenate([np.concatenate([c, -s], 1), np.concatenate([s, c], 1)], 0)
    return np.stack([p, q])


def lanes_iota(shape):
    return lax.broadcasted_iota(jnp.int32, shape, len(shape) - 1)


def pack_low(x):
    n = x.shape[1] // 2
    a, b = x[:, :n], x[:, n:]
    return jnp.where(lanes_iota(a.shape) < 64, a, pltpu.roll(b, 64, 2))


def pack_high(x):
    n = x.shape[1] // 2
    a, b = x[:, :n], x[:, n:]
    return jnp.where(lanes_iota(a.shape) < 64, pltpu.roll(a, 64, 2), b)


def unpack_low(x):
    return jnp.concatenate([x, pltpu.roll(x, 64, 2)], 1)


def unpack_high(x):
    return jnp.concatenate([pltpu.roll(x, 64, 2), x], 1)


def place(rows, cols):
    row, col = lax.axis_index("row"), lax.axis_index("col")
    around = {}
    for dr in (-1, 0, 1):
        for dc in (-1, 0, 1):
            if dr or dc:
                around[dr, dc] = (lax.rem(row + dr + rows, rows), lax.rem(col + dc + cols, cols))
    return row, col, around


def inside(row, col, rows, cols, dr, dc):
    ok = jnp.float32(1.0)
    if dr == -1:
        ok = ok * (row > 0).astype(jnp.float32)
    if dr == 1:
        ok = ok * (row < rows - 1).astype(jnp.float32)
    if dc == -1:
        ok = ok * (col > 0).astype(jnp.float32)
    if dc == 1:
        ok = ok * (col < cols - 1).astype(jnp.float32)
    return ok


SIDES = [(-1, 0), (1, 0), (0, -1), (0, 1), (-1, -1), (-1, 1), (1, -1), (1, 1)]


def kernel(
    rows, cols, nx, n1, cap, mixes,
    o_hbm, a_hbm, counts_hbm, offs_hbm, index_hbm, mix_hbm, modes_hbm, tab_hbm,
    new_object, new_modes,
    obj, amps, counts, offs, index, mix, modes, tab,
    ps, pc, rv, rs, rc, tiles, probes, patches, deltas, sums, pad, marg,
    on, op, oc, orv, ors, orc, got, half, r1, r2, r3, fresh,
    load, send, recv,
):
    n = 128
    nz = rows // nx
    row, col, around = place(rows, cols)
    x, z = row // nz, lax.rem(row, nz)
    y, core = col // 2, lax.rem(col, 2)
    p1 = z + core * (y - z)
    p2 = y + core * (z - y)
    sibling = (row, col + 1 - 2 * core)
    high = 2 * core
    other = 2 - high

    def first_peer(d):
        a = lax.rem(p1 + d, n1)
        return a, (x * nz + z + (1 - core) * (a - z), (y + core * (a - y)) * 2 + core)

    def second_peer(d):
        a = lax.rem(p2 + d, n1)
        return a, (x * nz + z + core * (a - z), (y + (1 - core) * (a - y)) * 2 + core)

    def x_peer(d):
        a = lax.rem(x + d, nx)
        return a, (a * nz + z, col)

    used = [0]
    pending = []

    def copy(src, dst, device):
        i = used[0]
        used[0] += 1
        made = pltpu.make_async_remote_copy(
            src_ref=src, dst_ref=dst, send_sem=send.at[i], recv_sem=recv.at[i],
            device_id=device, device_id_type=MESH,
        )
        made.start()
        pending.append(made)
        return made

    def ok(dr, dc):
        return inside(row, col, rows, cols, dr, dc)

    barrier = pltpu.get_barrier_semaphore()
    partners = (
        [around[s] for s in SIDES]
        + [sibling]
        + [first_peer(d)[1] for d in range(1, n1)]
        + [second_peer(d)[1] for d in range(1, n1)]
        + [x_peer(d)[1] for d in range(1, nx)]
    )
    for device in partners:
        pl.semaphore_signal(barrier, inc=1, device_id=device, device_id_type=MESH)
    loads = [
        pltpu.make_async_copy(src, dst, load.at[i])
        for i, (src, dst) in enumerate(
            (
                (o_hbm, obj), (modes_hbm, modes), (mix_hbm, mix), (index_hbm, index), (counts_hbm, counts),
                (offs_hbm, offs), (tab_hbm, tab), (a_hbm, amps),
            )
        )
    ]
    for c in loads:
        c.start()

    loads[0].wait()
    ps[0] = pack_low(obj[...])
    ps[1] = pack_high(obj[...])
    pc[0] = pack_low(obj[:, :64])
    pc[1] = pack_high(obj[:, :64])
    pc[2] = pack_low(obj[:, 64:])
    pc[3] = pack_high(obj[:, 64:])
    pl.semaphore_wait(barrier, len(partners))
    halo = [
        copy(pc.at[0], rc.at[0], around[-1, -1]),
        copy(pc.at[1], rc.at[1], around[-1, 1]),
        copy(pc.at[2], rc.at[2], around[1, -1]),
        copy(pc.at[3], rc.at[3], around[1, 1]),
        copy(obj.at[:, 0:64], rv.at[0], around[-1, 0]),
        copy(obj.at[:, 64:128], rv.at[1], around[1, 0]),
        copy(ps.at[0], rs.at[0], around[0, -1]),
        copy(ps.at[1], rs.at[1], around[0, 1]),
    ]

    for c in loads[1:]:
        c.wait()
    marg[...] = jnp.zeros_like(marg)
    sums[...] = jnp.zeros_like(sums)
    pad[...] = jnp.zeros_like(pad)
    count = counts[0, 0]

    def spot(slot):
        top = jnp.clip(offs[0, 0, 0, slot], 0, n - 1)
        left_px = jnp.clip(offs[0, 0, 1, slot], 0, n - 1)
        return top, left_px

    def weights_of(slot):
        pick = jnp.clip(index[0, 0, slot], 0, mixes - 1)
        return [jnp.where(slot < count, mix[k, pick], 0.0) for k in range(4)]

    def make_probe(slot, carry):
        w = weights_of(slot)
        for comp in range(2):
            total = w[0] * modes[0, comp]
            for k in range(1, 4):
                total = total + w[k] * modes[k, comp]
            probes[slot, comp] = total
        return carry

    lax.fori_loop(0, cap, make_probe, 0)
    for c in halo:
        c.wait_recv()

    def tile_rows(target, west, own, east):
        turned = pltpu.roll(own, 64, 2)
        low = lanes_iota(own.shape) < 64
        tiles[:, 0, target] = jnp.where(low, west, turned)
        tiles[:, 1, target] = jnp.where(low, turned, east)

    tile_rows(
        slice(0, 64), unpack_low(rc[3] * ok(-1, -1)), rv[1] * ok(-1, 0), unpack_high(rc[2] * ok(-1, 1))
    )
    tile_rows(slice(64, 192), unpack_low(rs[1] * ok(0, -1)), obj[...], unpack_high(rs[0] * ok(0, 1)))
    tile_rows(
        slice(192, 256), unpack_low(rc[1] * ok(1, -1)), rv[0] * ok(1, 0), unpack_high(rc[0] * ok(1, 1))
    )

    fwd, inv = tab[0], tab[1]

    def dot(a, b):
        return jnp.dot(a, b, preferred_element_type=jnp.float32)

    def left(table, res, ims):
        out = dot(table, jnp.concatenate([jnp.concatenate(res, 1), jnp.concatenate(ims, 1)], 0))
        return (
            [out[:n, i * n : (i + 1) * n] for i in range(len(res))],
            [out[n:, i * n : (i + 1) * n] for i in range(len(res))],
        )

    def right(table, res, ims):
        out = dot(jnp.concatenate([jnp.concatenate([a, b], 1) for a, b in zip(res, ims)], 0), table)
        return (
            [out[i * n : (i + 1) * n, :n] for i in range(len(res))],
            [out[i * n : (i + 1) * n, n:] for i in range(len(res))],
        )

    def lower(xs):
        return [v.astype(jnp.bfloat16) for v in xs]

    lane = lanes_iota((n, n))

    def visit(step, carry):
        slots = [step * GROUP + i for i in range(GROUP)]
        psi_r, psi_i = [], []
        for slot in slots:
            top, left_px = spot(slot)
            mask = lane >= left_px
            patch = []
            for comp in range(2):
                a = tiles[comp, 0, pl.ds(top, n), :]
                b = tiles[comp, 1, pl.ds(top, n), :]
                patch.append(pltpu.roll(jnp.where(mask, a, b), lax.rem(n - left_px, n), 1))
                patches[slot, comp] = patch[comp]
            pr, pi = probes[slot, 0], probes[slot, 1]
            psi_r.append(pr * patch[0] - pi * patch[1])
            psi_i.append(pr * patch[1] + pi * patch[0])
        re, im = left(fwd, lower(psi_r), lower(psi_i))
        re, im = right(inv, lower(re), lower(im))
        fixed_re, fixed_im = [], []
        for slot, a, b in zip(slots, re, im):
            ratio = amps[0, 0, slot].astype(jnp.float32) * lax.rsqrt(jnp.maximum(a * a + b * b, FLOOR * FLOOR))
            fixed_re.append((a * ratio).astype(jnp.bfloat16))
            fixed_im.append((b * ratio).astype(jnp.bfloat16))
        re, im = left(inv, fixed_re, fixed_im)
        re, im = right(fwd, lower(re), lower(im))
        pieces, weights = [], []
        for i, slot in enumerate(slots):
            dr, di = re[i] - psi_r[i], im[i] - psi_i[i]
            deltas[slot, 0] = dr
            deltas[slot, 1] = di
            ar, ai = patches[slot, 0], patches[slot, 1]
            pieces.append((ar * dr + ai * di, ar * di - ai * dr, ar * ar + ai * ai))
            weights.append(weights_of(slot))
        for k in range(4):
            for f in range(3):
                total = sums[k, f]
                for i in range(GROUP):
                    w = weights[i][k]
                    total = total + (w if f < 2 else w * w) * pieces[i][f]
                sums[k, f] = total
        return carry

    lax.fori_loop(0, cap // GROUP, visit, 0)

    thick = n // n1

    def chunk(a):
        return pl.ds(pl.multiple_of(a * thick, thick), thick)

    order = FAR + (0,)
    pair = []
    for d in order:
        piece = chunk(lax.rem(p2 + d, n1))
        pair.append(copy(sums.at[pl.ds(other, 2), :, piece], got.at[:, :, piece], sibling))
    sent = []
    for d, c in zip(order, pair):
        c.wait_recv()
        a, device = first_peer(d)
        half[:, :, chunk(a)] = sums[pl.ds(high, 2), :, chunk(a)] + got[:, :, chunk(a)]
        if d:
            sent.append(copy(half.at[:, :, chunk(a)], r1.at[d - 1], device))

    def spread(step, carry):
        slots = [step * GROUP + i for i in range(GROUP)]
        spots = [spot(slot) for slot in slots]
        for i, slot in enumerate(slots):
            pr, pi = probes[slot, 0], probes[slot, 1]
            dr, di = deltas[slot, 0], deltas[slot, 1]
            for f, value in enumerate((pr * dr + pi * di, pr * di - pi * dr, pr * pr + pi * pi)):
                pad[i, f, n : 2 * n] = pltpu.roll(value, spots[i][1], 1)
        for f in range(3):
            for h in range(4):
                part = slice(h * 64, (h + 1) * 64)
                low, up = marg[f, 0, part], marg[f, 1, part]
                for i, (top, left_px) in enumerate(spots):
                    value = pad[i, f, pl.ds(n - top + h * 64, 64), :]
                    mask = lanes_iota((64, n)) >= left_px
                    low = low + jnp.where(mask, value, 0.0)
                    up = up + jnp.where(mask, 0.0, value)
                marg[f, 0, part] = low
                marg[f, 1, part] = up
        return carry

    lax.fori_loop(0, cap // GROUP, spread, 0)
    low64 = lanes_iota((3, 64, n)) < 64

    def centre(part):
        return jnp.where(low64, pltpu.roll(marg[:, 0, part], 64, 2), pltpu.roll(marg[:, 1, part], 64, 2))

    on[0] = centre(slice(0, 64))
    on[1] = centre(slice(192, 256))
    op[0] = pack_low(marg[:, 0, 64:192])
    op[1] = pack_high(marg[:, 1, 64:192])
    oc[0] = pack_low(marg[:, 0, 0:64])
    oc[1] = pack_high(marg[:, 1, 0:64])
    oc[2] = pack_low(marg[:, 0, 192:256])
    oc[3] = pack_high(marg[:, 1, 192:256])

    mine = chunk(p1)
    total = half[:, :, mine]
    for d, c in zip(FAR[::-1], sent[::-1]):
        c.wait_recv()
        total = total + r1[d - 1]
    parts = thick // 8
    for m in range(2):
        for t in range(parts):
            r2[m * parts + t] = total[m, :, t * 8 : (t + 1) * 8]
    sent = []
    for d in range(1, nx):
        a, device = x_peer(d)
        sent.append(copy(r2.at[a], r2.at[nx + d - 1], device))
    edge = [
        copy(oc.at[0], orc.at[0], around[-1, -1]),
        copy(oc.at[1], orc.at[1], around[-1, 1]),
        copy(oc.at[2], orc.at[2], around[1, -1]),
        copy(oc.at[3], orc.at[3], around[1, 1]),
        copy(on.at[0], orv.at[0], around[-1, 0]),
        copy(on.at[1], orv.at[1], around[1, 0]),
        copy(op.at[0], ors.at[0], around[0, -1]),
        copy(op.at[1], ors.at[1], around[0, 1]),
    ]
    total = r2[x]
    for d, c in enumerate(sent):
        c.wait_recv()
        total = total + r2[nx + d]
    r3[p2] = total
    sent = []
    for d in FAR:
        _, device = second_peer(d)
        sent.append(copy(r3.at[p2], r3.at[p2], device))
    for c in sent:
        c.wait_recv()
    total = r3[0]
    for a in range(1, n1):
        total = total + r3[a]
    mode, tile = high + x // parts, lax.rem(x, parts)
    unit = pl.ds(pl.multiple_of(p1 * thick + tile * 8, 8), 8)
    fresh[mode, :, unit] = modes[mode, :, unit] + total[:2] / (total[2:] + RELAX)
    sent = []
    for d in range(1, nx):
        _, device = x_peer(d)
        sent.append(copy(fresh.at[mode, :, unit], fresh.at[mode, :, unit], device))
    for c in sent:
        c.wait_recv()
    both = pl.ds(high, 2)
    sent = {}
    for d in FAR:
        _, device = first_peer(d)
        sent[d] = copy(fresh.at[both, :, mine], fresh.at[both, :, mine], device)
    pair = [copy(fresh.at[both, :, mine], fresh.at[both, :, mine], sibling)]

    for c in edge:
        c.wait_recv()
    west = unpack_low(ors[1] * ok(0, -1))
    east = unpack_high(ors[0] * ok(0, 1))
    for part, inner, vertical, lo, up in (
        (slice(0, 64), slice(64, 128), orv[1] * ok(-1, 0), orc[3] * ok(-1, -1), orc[2] * ok(-1, 1)),
        (slice(64, 128), slice(128, 192), orv[0] * ok(1, 0), orc[1] * ok(1, -1), orc[0] * ok(1, 1)),
    ):
        side = jnp.where(low64, west[:, part] + unpack_low(lo), east[:, part] + unpack_high(up))
        both_sums = centre(inner) + vertical + side
        new_object[:, part] = obj[:, part] + both_sums[:2] / (both_sums[2:] + RELAX)

    for d in NEAR:
        sent[d].wait_recv()
        piece = chunk(lax.rem(p1 + n1 - d, n1))
        pair.append(copy(fresh.at[both, :, piece], fresh.at[both, :, piece], sibling))
    for c in pair:
        c.wait_recv()

    scale = 1.0 / (n * n)

    def mean(v):
        return jnp.sum(jnp.sum(v, 0, keepdims=True), 1, keepdims=True) * scale

    basis = []
    coefs = {}
    for k in range(4):
        vr, vi = fresh[k, 0], fresh[k, 1]
        for j in range(k):
            cr, ci = coefs[j, k]
            br, bi = basis[j]
            vr = vr - (cr * br - ci * bi)
            vi = vi - (cr * bi + ci * br)
        norm = 1.0 / jnp.sqrt(mean(vr * vr + vi * vi) + EPSILON)
        qr, qi = vr * norm, vi * norm
        basis.append((qr, qi))
        new_modes[k, 0] = qr
        new_modes[k, 1] = qi
        for later in range(k + 1, 4):
            fr, fi = fresh[later, 0], fresh[later, 1]
            coefs[k, later] = (mean(qr * fr + qi * fi), mean(qr * fi - qi * fr))
    for c in pending:
        c.wait_send()


def solution(mesh):
    rows, cols = mesh.shape["row"], mesh.shape["col"]
    nx = 4
    n1 = cols // 2
    f32, bf16, i32 = jnp.float32, jnp.bfloat16, jnp.int32

    def body(object_field, amplitudes, counts, offsets, mode_index, mix_table, probe_modes):
        cap, mixes = amplitudes.shape[2], mix_table.shape[0]
        number = 16 + 8 + 8 + 3 * (n1 - 1) + 2 * (nx - 1)
        return pl.pallas_call(
            functools.partial(kernel, rows, cols, nx, n1, cap, mixes),
            out_shape=(
                jax.ShapeDtypeStruct((2, 128, 128), f32),
                jax.ShapeDtypeStruct((4, 2, 128, 128), f32),
            ),
            in_specs=[HBM] * 8,
            out_specs=(VMEM, VMEM),
            scratch_shapes=[
                pltpu.VMEM((2, 128, 128), f32),
                pltpu.VMEM(amplitudes.shape, bf16),
                pltpu.SMEM((1, 1), i32),
                pltpu.SMEM((1, 1, 2, cap), i32),
                pltpu.SMEM((1, 1, cap), i32),
                pltpu.SMEM((4, mixes), f32),
                pltpu.VMEM((4, 2, 128, 128), f32),
                pltpu.VMEM((2, 256, 256), bf16),
                pltpu.VMEM((2, 2, 64, 128), f32),
                pltpu.VMEM((4, 2, 32, 128), f32),
                pltpu.VMEM((2, 2, 64, 128), f32),
                pltpu.VMEM((2, 2, 64, 128), f32),
                pltpu.VMEM((4, 2, 32, 128), f32),
                pltpu.VMEM((2, 2, 256, 128), f32),
                pltpu.VMEM((cap, 2, 128, 128), f32),
                pltpu.VMEM((cap, 2, 128, 128), f32),
                pltpu.VMEM((cap, 2, 128, 128), f32),
                pltpu.VMEM((4, 3, 128, 128), f32),
                pltpu.VMEM((GROUP, 3, 384, 128), f32),
                pltpu.VMEM((3, 2, 256, 128), f32),
                pltpu.VMEM((2, 3, 64, 128), f32),
                pltpu.VMEM((2, 3, 64, 128), f32),
                pltpu.VMEM((4, 3, 32, 128), f32),
                pltpu.VMEM((2, 3, 64, 128), f32),
                pltpu.VMEM((2, 3, 64, 128), f32),
                pltpu.VMEM((4, 3, 32, 128), f32),
                pltpu.VMEM((2, 3, 128, 128), f32),
                pltpu.VMEM((2, 3, 128, 128), f32),
                pltpu.VMEM((n1 - 1, 2, 3, 128 // n1, 128), f32),
                pltpu.VMEM((2 * nx, 3, 8, 128), f32),
                pltpu.VMEM((n1, 3, 8, 128), f32),
                pltpu.VMEM((4, 2, 128, 128), f32),
                pltpu.SemaphoreType.DMA((8,)),
                pltpu.SemaphoreType.DMA((number,)),
                pltpu.SemaphoreType.DMA((number,)),
            ],
            compiler_params=pltpu.CompilerParams(
                collective_id=0, has_side_effects=True, vmem_limit_bytes=56 * 1024 * 1024
            ),
            name="update",
        )(
            object_field, amplitudes, counts, jnp.swapaxes(offsets, 2, 3), mode_index, mix_table.T,
            probe_modes, jnp.asarray(tables(128)),
        )

    return jax.shard_map(
        body,
        mesh=mesh,
        in_specs=(
            P(None, "row", "col"),
            P("row", "col", None, None, None),
            P("row", "col"),
            P("row", "col", None, None),
            P("row", "col", None),
            P(),
            P(),
        ),
        out_specs=(P(None, "row", "col"), P()),
        check_vma=False,
    )
```

```python
import functools

import jax
import jax.numpy as jnp
import ml_dtypes
import numpy as np
from jax import lax
from jax.experimental import pallas as pl
from jax.experimental.pallas import tpu as pltpu
from jax.sharding import PartitionSpec as P

FLOOR = 0.25
RELAX = 0.5
EPSILON = 1e-06
GROUP = 2
FAR = (4, 3, 5, 2, 6, 1, 7)
NEAR = (1, 7, 2, 6, 3, 5, 4)
MESH = pl.DeviceIdType.MESH
VMEM = pl.BlockSpec(memory_space=pltpu.VMEM)
HBM = pl.BlockSpec(memory_space=pltpu.HBM)


def tables(size):
    index = np.arange(size)
    angle = (index[:, None] * index[None, :] % size).astype(np.float32) * np.float32(2.0 * np.pi / size)
    factor = np.float32(1.0 / np.sqrt(size))
    c = (np.cos(angle) * factor).astype(ml_dtypes.bfloat16)
    s = (np.sin(angle) * factor).astype(ml_dtypes.bfloat16)
    p = np.concatenate([np.concatenate([c, s], 1), np.concatenate([-s, c], 1)], 0)
    q = np.concatenate([np.concatenate([c, -s], 1), np.concatenate([s, c], 1)], 0)
    return np.stack([p, q])


def lanes_iota(shape):
    return lax.broadcasted_iota(jnp.int32, shape, len(shape) - 1)


def pack_low(x):
    n = x.shape[1] // 2
    a, b = x[:, :n], x[:, n:]
    return jnp.where(lanes_iota(a.shape) < 64, a, pltpu.roll(b, 64, 2))


def pack_high(x):
    n = x.shape[1] // 2
    a, b = x[:, :n], x[:, n:]
    return jnp.where(lanes_iota(a.shape) < 64, pltpu.roll(a, 64, 2), b)


def unpack_low(x):
    return jnp.concatenate([x, pltpu.roll(x, 64, 2)], 1)


def unpack_high(x):
    return jnp.concatenate([pltpu.roll(x, 64, 2), x], 1)


def place(rows, cols):
    row, col = lax.axis_index("row"), lax.axis_index("col")
    around = {}
    for dr in (-1, 0, 1):
        for dc in (-1, 0, 1):
            if dr or dc:
                around[dr, dc] = (lax.rem(row + dr + rows, rows), lax.rem(col + dc + cols, cols))
    return row, col, around


def inside(row, col, rows, cols, dr, dc):
    ok = jnp.float32(1.0)
    if dr == -1:
        ok = ok * (row > 0).astype(jnp.float32)
    if dr == 1:
        ok = ok * (row < rows - 1).astype(jnp.float32)
    if dc == -1:
        ok = ok * (col > 0).astype(jnp.float32)
    if dc == 1:
        ok = ok * (col < cols - 1).astype(jnp.float32)
    return ok


SIDES = [(-1, 0), (1, 0), (0, -1), (0, 1), (-1, -1), (-1, 1), (1, -1), (1, 1)]


def kernel(
    rows, cols, nx, n1, cap, mixes,
    o_hbm, a_hbm, counts_hbm, offs_hbm, index_hbm, mix_hbm, modes_hbm, tab_hbm,
    new_object, fresh,
    obj, amps, counts, offs, index, mix, modes, tab,
    ps, pc, rv, rs, rc, tiles, probes, patches, deltas, sums, pad, marg,
    on, op, oc, orv, ors, orc, got, half, r1, r2, r3,
    load, send, recv,
):
    n = 128
    nz = rows // nx
    row, col, around = place(rows, cols)
    x, z = row // nz, lax.rem(row, nz)
    y, core = col // 2, lax.rem(col, 2)
    p1 = z + core * (y - z)
    p2 = y + core * (z - y)
    sibling = (row, col + 1 - 2 * core)
    high = 2 * core
    other = 2 - high

    def first_peer(d):
        a = lax.rem(p1 + d, n1)
        return a, (x * nz + z + (1 - core) * (a - z), (y + core * (a - y)) * 2 + core)

    def second_peer(d):
        a = lax.rem(p2 + d, n1)
        return a, (x * nz + z + core * (a - z), (y + (1 - core) * (a - y)) * 2 + core)

    def x_peer(d):
        a = lax.rem(x + d, nx)
        return a, (a * nz + z, col)

    used = [0]
    pending = []

    def copy(src, dst, device):
        i = used[0]
        used[0] += 1
        made = pltpu.make_async_remote_copy(
            src_ref=src, dst_ref=dst, send_sem=send.at[i], recv_sem=recv.at[i],
            device_id=device, device_id_type=MESH,
        )
        made.start()
        pending.append(made)
        return made

    def ok(dr, dc):
        return inside(row, col, rows, cols, dr, dc)

    barrier = pltpu.get_barrier_semaphore()
    partners = (
        [around[s] for s in SIDES]
        + [sibling]
        + [first_peer(d)[1] for d in range(1, n1)]
        + [second_peer(d)[1] for d in range(1, n1)]
        + [x_peer(d)[1] for d in range(1, nx)]
    )
    for device in partners:
        pl.semaphore_signal(barrier, inc=1, device_id=device, device_id_type=MESH)
    loads = [
        pltpu.make_async_copy(src, dst, load.at[i])
        for i, (src, dst) in enumerate(
            (
                (o_hbm, obj), (modes_hbm, modes), (mix_hbm, mix), (index_hbm, index), (counts_hbm, counts),
                (offs_hbm, offs), (tab_hbm, tab), (a_hbm, amps),
            )
        )
    ]
    for c in loads:
        c.start()

    loads[0].wait()
    ps[0] = pack_low(obj[...])
    ps[1] = pack_high(obj[...])
    pc[0] = pack_low(obj[:, :64])
    pc[1] = pack_high(obj[:, :64])
    pc[2] = pack_low(obj[:, 64:])
    pc[3] = pack_high(obj[:, 64:])
    pl.semaphore_wait(barrier, len(partners))
    halo = [
        copy(pc.at[0], rc.at[0], around[-1, -1]),
        copy(pc.at[1], rc.at[1], around[-1, 1]),
        copy(pc.at[2], rc.at[2], around[1, -1]),
        copy(pc.at[3], rc.at[3], around[1, 1]),
        copy(obj.at[:, 0:64], rv.at[0], around[-1, 0]),
        copy(obj.at[:, 64:128], rv.at[1], around[1, 0]),
        copy(ps.at[0], rs.at[0], around[0, -1]),
        copy(ps.at[1], rs.at[1], around[0, 1]),
    ]

    for c in loads[1:]:
        c.wait()
    marg[...] = jnp.zeros_like(marg)
    sums[...] = jnp.zeros_like(sums)
    pad[...] = jnp.zeros_like(pad)
    count = counts[0, 0]

    def spot(slot):
        top = jnp.clip(offs[0, 0, 0, slot], 0, n - 1)
        left_px = jnp.clip(offs[0, 0, 1, slot], 0, n - 1)
        return top, left_px

    def weights_of(slot):
        pick = jnp.clip(index[0, 0, slot], 0, mixes - 1)
        return [jnp.where(slot < count, mix[k, pick], 0.0) for k in range(4)]

    def spread(frames, spots):
        for f in frames:
            for h in range(4):
                part = slice(h * 64, (h + 1) * 64)
                low, up = marg[f, 0, part], marg[f, 1, part]
                for i, (top, left_px) in enumerate(spots):
                    value = pad[i, f, pl.ds(n - top + h * 64, 64), :]
                    mask = lanes_iota((64, n)) >= left_px
                    low = low + jnp.where(mask, value, 0.0)
                    up = up + jnp.where(mask, 0.0, value)
                marg[f, 0, part] = low
                marg[f, 1, part] = up

    def centre(frames, part):
        own, end = marg[frames, 0, part], marg[frames, 1, part]
        return jnp.where(lanes_iota(own.shape) < 64, pltpu.roll(own, 64, 2), pltpu.roll(end, 64, 2))

    def send_edges(frames):
        top, middle, bottom = slice(0, 64), slice(64, 192), slice(192, 256)
        on[0, frames] = centre(frames, top)
        on[1, frames] = centre(frames, bottom)
        op[0, frames] = pack_low(marg[frames, 0, middle])
        op[1, frames] = pack_high(marg[frames, 1, middle])
        oc[0, frames] = pack_low(marg[frames, 0, top])
        oc[1, frames] = pack_high(marg[frames, 1, top])
        oc[2, frames] = pack_low(marg[frames, 0, bottom])
        oc[3, frames] = pack_high(marg[frames, 1, bottom])
        return [
            copy(oc.at[0, frames], orc.at[0, frames], around[-1, -1]),
            copy(oc.at[1, frames], orc.at[1, frames], around[-1, 1]),
            copy(oc.at[2, frames], orc.at[2, frames], around[1, -1]),
            copy(oc.at[3, frames], orc.at[3, frames], around[1, 1]),
            copy(on.at[0, frames], orv.at[0, frames], around[-1, 0]),
            copy(on.at[1, frames], orv.at[1, frames], around[1, 0]),
            copy(op.at[0, frames], ors.at[0, frames], around[0, -1]),
            copy(op.at[1, frames], ors.at[1, frames], around[0, 1]),
        ]

    def make_probes(step, carry):
        slots = [step * GROUP + i for i in range(GROUP)]
        spots = [spot(slot) for slot in slots]
        for i, slot in enumerate(slots):
            w = weights_of(slot)
            probe = []
            for comp in range(2):
                total = w[0] * modes[0, comp]
                for k in range(1, 4):
                    total = total + w[k] * modes[k, comp]
                probes[slot, comp] = total
                probe.append(total)
            value = probe[0] * probe[0] + probe[1] * probe[1]
            pad[i, 2, n : 2 * n] = pltpu.roll(value, spots[i][1], 1)
        spread((2,), spots)
        return carry

    lax.fori_loop(0, cap // GROUP, make_probes, 0)
    edge = send_edges(slice(2, 3))
    for c in halo:
        c.wait_recv()

    def tile_rows(target, west, own, east):
        turned = pltpu.roll(own, 64, 2)
        low = lanes_iota(own.shape) < 64
        tiles[:, 0, target] = jnp.where(low, west, turned)
        tiles[:, 1, target] = jnp.where(low, turned, east)

    tile_rows(
        slice(0, 64), unpack_low(rc[3] * ok(-1, -1)), rv[1] * ok(-1, 0), unpack_high(rc[2] * ok(-1, 1))
    )
    tile_rows(slice(64, 192), unpack_low(rs[1] * ok(0, -1)), obj[...], unpack_high(rs[0] * ok(0, 1)))
    tile_rows(
        slice(192, 256), unpack_low(rc[1] * ok(1, -1)), rv[0] * ok(1, 0), unpack_high(rc[0] * ok(1, 1))
    )

    fwd, inv = tab[0], tab[1]

    def dot(a, b):
        return jnp.dot(a, b, preferred_element_type=jnp.float32)

    def left(table, res, ims):
        out = dot(table, jnp.concatenate([jnp.concatenate(res, 1), jnp.concatenate(ims, 1)], 0))
        return (
            [out[:n, i * n : (i + 1) * n] for i in range(len(res))],
            [out[n:, i * n : (i + 1) * n] for i in range(len(res))],
        )

    def right(table, res, ims):
        out = dot(jnp.concatenate([jnp.concatenate([a, b], 1) for a, b in zip(res, ims)], 0), table)
        return (
            [out[i * n : (i + 1) * n, :n] for i in range(len(res))],
            [out[i * n : (i + 1) * n, n:] for i in range(len(res))],
        )

    def lower(xs):
        return [v.astype(jnp.bfloat16) for v in xs]

    lane = lanes_iota((n, n))

    def visit(step, carry):
        slots = [step * GROUP + i for i in range(GROUP)]
        psi_r, psi_i = [], []
        for slot in slots:
            top, left_px = spot(slot)
            mask = lane >= left_px
            patch = []
            for comp in range(2):
                a = tiles[comp, 0, pl.ds(top, n), :]
                b = tiles[comp, 1, pl.ds(top, n), :]
                patch.append(pltpu.roll(jnp.where(mask, a, b), lax.rem(n - left_px, n), 1))
                patches[slot, comp] = patch[comp]
            pr, pi = probes[slot, 0], probes[slot, 1]
            psi_r.append(pr * patch[0] - pi * patch[1])
            psi_i.append(pr * patch[1] + pi * patch[0])
        re, im = left(fwd, lower(psi_r), lower(psi_i))
        re, im = right(inv, lower(re), lower(im))
        fixed_re, fixed_im = [], []
        for slot, a, b in zip(slots, re, im):
            ratio = amps[0, 0, slot].astype(jnp.float32) * lax.rsqrt(jnp.maximum(a * a + b * b, FLOOR * FLOOR))
            fixed_re.append((a * ratio).astype(jnp.bfloat16))
            fixed_im.append((b * ratio).astype(jnp.bfloat16))
        re, im = left(inv, fixed_re, fixed_im)
        re, im = right(fwd, lower(re), lower(im))
        pieces, weights = [], []
        for i, slot in enumerate(slots):
            dr, di = re[i] - psi_r[i], im[i] - psi_i[i]
            deltas[slot, 0] = dr
            deltas[slot, 1] = di
            ar, ai = patches[slot, 0], patches[slot, 1]
            pieces.append((ar * dr + ai * di, ar * di - ai * dr, ar * ar + ai * ai))
            weights.append(weights_of(slot))
        for k in range(4):
            for f in range(3):
                total = sums[k, f]
                for i in range(GROUP):
                    w = weights[i][k]
                    total = total + (w if f < 2 else w * w) * pieces[i][f]
                sums[k, f] = total
        return carry

    lax.fori_loop(0, cap // GROUP, visit, 0)

    thick = n // n1

    def chunk(a):
        return pl.ds(pl.multiple_of(a * thick, thick), thick)

    order = FAR + (0,)
    pair = []
    for d in order:
        piece = chunk(lax.rem(p2 + d, n1))
        pair.append(copy(sums.at[pl.ds(other, 2), :, piece], got.at[:, :, piece], sibling))
    sent = []
    for d, c in zip(order, pair):
        c.wait_recv()
        a, device = first_peer(d)
        half[:, :, chunk(a)] = sums[pl.ds(high, 2), :, chunk(a)] + got[:, :, chunk(a)]
        if d:
            sent.append(copy(half.at[:, :, chunk(a)], r1.at[d - 1], device))

    def numerators(step, carry):
        slots = [step * GROUP + i for i in range(GROUP)]
        spots = [spot(slot) for slot in slots]
        for i, slot in enumerate(slots):
            pr, pi = probes[slot, 0], probes[slot, 1]
            dr, di = deltas[slot, 0], deltas[slot, 1]
            for f, value in enumerate((pr * dr + pi * di, pr * di - pi * dr)):
                pad[i, f, n : 2 * n] = pltpu.roll(value, spots[i][1], 1)
        spread((0, 1), spots)
        return carry

    lax.fori_loop(0, cap // GROUP, numerators, 0)

    mine = chunk(p1)
    total = half[:, :, mine]
    for d, c in zip(FAR[::-1], sent[::-1]):
        c.wait_recv()
        total = total + r1[d - 1]
    parts = thick // 8
    for m in range(2):
        for t in range(parts):
            r2[m * parts + t] = total[m, :, t * 8 : (t + 1) * 8]
    sent = []
    for d in range(1, nx):
        a, device = x_peer(d)
        sent.append(copy(r2.at[a], r2.at[nx + d - 1], device))
    total = r2[x]
    for d, c in enumerate(sent):
        c.wait_recv()
        total = total + r2[nx + d]
    r3[p2] = total
    sent = []
    for d in FAR:
        _, device = second_peer(d)
        sent.append(copy(r3.at[p2], r3.at[p2], device))
    edge += send_edges(slice(0, 2))
    for c in sent:
        c.wait_recv()
    total = r3[0]
    for a in range(1, n1):
        total = total + r3[a]
    mode, tile = high + x // parts, lax.rem(x, parts)
    unit = pl.ds(pl.multiple_of(p1 * thick + tile * 8, 8), 8)
    fresh[mode, :, unit] = modes[mode, :, unit] + total[:2] / (total[2:] + RELAX)
    sent = []
    for d in range(1, nx):
        _, device = x_peer(d)
        sent.append(copy(fresh.at[mode, :, unit], fresh.at[mode, :, unit], device))
    for c in sent:
        c.wait_recv()
    both = pl.ds(high, 2)
    sent = {}
    for d in FAR:
        _, device = first_peer(d)
        sent[d] = copy(fresh.at[both, :, mine], fresh.at[both, :, mine], device)
    pair = [copy(fresh.at[both, :, mine], fresh.at[both, :, mine], sibling)]

    for c in edge:
        c.wait_recv()
    west = unpack_low(ors[1] * ok(0, -1))
    east = unpack_high(ors[0] * ok(0, 1))
    for part, inner, vertical, lo, up in (
        (slice(0, 64), slice(64, 128), orv[1] * ok(-1, 0), orc[3] * ok(-1, -1), orc[2] * ok(-1, 1)),
        (slice(64, 128), slice(128, 192), orv[0] * ok(1, 0), orc[1] * ok(1, -1), orc[0] * ok(1, 1)),
    ):
        side = jnp.where(lanes_iota((3, 64, n)) < 64, west[:, part] + unpack_low(lo), east[:, part] + unpack_high(up))
        both_sums = centre(slice(0, 3), inner) + vertical + side
        new_object[:, part] = obj[:, part] + both_sums[:2] / (both_sums[2:] + RELAX)

    for d in NEAR:
        sent[d].wait_recv()
        piece = chunk(lax.rem(p1 + n1 - d, n1))
        pair.append(copy(fresh.at[both, :, piece], fresh.at[both, :, piece], sibling))
    for c in pair:
        c.wait_recv()

    for c in pending:
        c.wait_send()


def finish_kernel(object_in, fresh, object_out, modes_out, made, sem):
    first = pltpu.make_async_copy(object_in, object_out, sem.at[0])
    first.start()
    copies = [first]
    scale = 1.0 / (fresh.shape[2] * fresh.shape[3])

    def mean(v):
        return jnp.sum(jnp.sum(v, 0, keepdims=True), 1, keepdims=True) * scale

    basis = []
    coefs = {}
    for k in range(4):
        vr, vi = fresh[k, 0], fresh[k, 1]
        for j in range(k):
            cr, ci = coefs[j, k]
            br, bi = basis[j]
            vr = vr - (cr * br - ci * bi)
            vi = vi - (cr * bi + ci * br)
        norm = 1.0 / jnp.sqrt(mean(vr * vr + vi * vi) + EPSILON)
        qr, qi = vr * norm, vi * norm
        basis.append((qr, qi))
        made[k, 0] = qr
        made[k, 1] = qi
        write = pltpu.make_async_copy(made.at[k], modes_out.at[k], sem.at[k + 1])
        write.start()
        copies.append(write)
        for later in range(k + 1, 4):
            fr, fi = fresh[later, 0], fresh[later, 1]
            coefs[k, later] = (mean(qr * fr + qi * fi), mean(qr * fi - qi * fr))
    for c in copies:
        c.wait()


def solution(mesh):
    rows, cols = mesh.shape["row"], mesh.shape["col"]
    nx = 4
    n1 = cols // 2
    f32, bf16, i32 = jnp.float32, jnp.bfloat16, jnp.int32

    def body(object_field, amplitudes, counts, offsets, mode_index, mix_table, probe_modes):
        cap, mixes = amplitudes.shape[2], mix_table.shape[0]
        number = 16 + 16 + 8 + 3 * (n1 - 1) + 2 * (nx - 1)
        new_object, fresh = pl.pallas_call(
            functools.partial(kernel, rows, cols, nx, n1, cap, mixes),
            out_shape=(
                pltpu.VMEM((2, 128, 128), f32),
                pltpu.VMEM((4, 2, 128, 128), f32),
            ),
            in_specs=[HBM] * 8,
            out_specs=(VMEM, VMEM),
            scratch_shapes=[
                pltpu.VMEM((2, 128, 128), f32),
                pltpu.VMEM(amplitudes.shape, bf16),
                pltpu.SMEM((1, 1), i32),
                pltpu.SMEM((1, 1, 2, cap), i32),
                pltpu.SMEM((1, 1, cap), i32),
                pltpu.SMEM((4, mixes), f32),
                pltpu.VMEM((4, 2, 128, 128), f32),
                pltpu.VMEM((2, 256, 256), bf16),
                pltpu.VMEM((2, 2, 64, 128), f32),
                pltpu.VMEM((4, 2, 32, 128), f32),
                pltpu.VMEM((2, 2, 64, 128), f32),
                pltpu.VMEM((2, 2, 64, 128), f32),
                pltpu.VMEM((4, 2, 32, 128), f32),
                pltpu.VMEM((2, 2, 256, 128), f32),
                pltpu.VMEM((cap, 2, 128, 128), f32),
                pltpu.VMEM((cap, 2, 128, 128), f32),
                pltpu.VMEM((cap, 2, 128, 128), f32),
                pltpu.VMEM((4, 3, 128, 128), f32),
                pltpu.VMEM((GROUP, 3, 384, 128), f32),
                pltpu.VMEM((3, 2, 256, 128), f32),
                pltpu.VMEM((2, 3, 64, 128), f32),
                pltpu.VMEM((2, 3, 64, 128), f32),
                pltpu.VMEM((4, 3, 32, 128), f32),
                pltpu.VMEM((2, 3, 64, 128), f32),
                pltpu.VMEM((2, 3, 64, 128), f32),
                pltpu.VMEM((4, 3, 32, 128), f32),
                pltpu.VMEM((2, 3, 128, 128), f32),
                pltpu.VMEM((2, 3, 128, 128), f32),
                pltpu.VMEM((n1 - 1, 2, 3, 128 // n1, 128), f32),
                pltpu.VMEM((2 * nx, 3, 8, 128), f32),
                pltpu.VMEM((n1, 3, 8, 128), f32),
                pltpu.SemaphoreType.DMA((8,)),
                pltpu.SemaphoreType.DMA((number,)),
                pltpu.SemaphoreType.DMA((number,)),
            ],
            compiler_params=pltpu.CompilerParams(
                collective_id=0, has_side_effects=True, vmem_limit_bytes=56 * 1024 * 1024
            ),
            name="update",
        )(
            object_field, amplitudes, counts, jnp.swapaxes(offsets, 2, 3), mode_index, mix_table.T,
            probe_modes, jnp.asarray(tables(128)),
        )
        return pl.pallas_call(
            finish_kernel,
            out_shape=(
                jax.ShapeDtypeStruct((2, 128, 128), f32),
                jax.ShapeDtypeStruct((4, 2, 128, 128), f32),
            ),
            in_specs=[VMEM, VMEM],
            out_specs=(HBM, HBM),
            scratch_shapes=[pltpu.VMEM((4, 2, 128, 128), f32), pltpu.SemaphoreType.DMA((5,))],
            compiler_params=pltpu.CompilerParams(vmem_limit_bytes=8 * 1024 * 1024),
            name="finish",
        )(new_object, fresh)

    return jax.shard_map(
        body,
        mesh=mesh,
        in_specs=(
            P(None, "row", "col"),
            P("row", "col", None, None, None),
            P("row", "col"),
            P("row", "col", None, None),
            P("row", "col", None),
            P(),
            P(),
        ),
        out_specs=(P(None, "row", "col"), P()),
        check_vma=False,
    )
```

```python
import functools

import jax
import jax.numpy as jnp
import ml_dtypes
import numpy as np
from jax import lax
from jax.experimental import pallas as pl
from jax.experimental.pallas import tpu as pltpu
from jax.sharding import PartitionSpec as P

FLOOR = 0.25
RELAX = 0.5
EPSILON = 1e-06
GROUP = 2
TEAM = 6
FAR = (4, 3, 5, 2, 6, 1, 7)
NEAR = (1, 7, 2, 6, 3, 5, 4)
MESH = pl.DeviceIdType.MESH
VMEM = pl.BlockSpec(memory_space=pltpu.VMEM)
HBM = pl.BlockSpec(memory_space=pltpu.HBM)


def tables(size):
    index = np.arange(size)
    angle = (index[:, None] * index[None, :] % size).astype(np.float32) * np.float32(2.0 * np.pi / size)
    factor = np.float32(1.0 / np.sqrt(size))
    c = (np.cos(angle) * factor).astype(ml_dtypes.bfloat16)
    s = (np.sin(angle) * factor).astype(ml_dtypes.bfloat16)
    p = np.concatenate([np.concatenate([c, s], 1), np.concatenate([-s, c], 1)], 0)
    q = np.concatenate([np.concatenate([c, -s], 1), np.concatenate([s, c], 1)], 0)
    return np.stack([p, q])


def lanes_iota(shape):
    return lax.broadcasted_iota(jnp.int32, shape, len(shape) - 1)


def pack_low(x):
    n = x.shape[1] // 2
    a, b = x[:, :n], x[:, n:]
    return jnp.where(lanes_iota(a.shape) < 64, a, pltpu.roll(b, 64, 2))


def pack_high(x):
    n = x.shape[1] // 2
    a, b = x[:, :n], x[:, n:]
    return jnp.where(lanes_iota(a.shape) < 64, pltpu.roll(a, 64, 2), b)


def unpack_low(x):
    return jnp.concatenate([x, pltpu.roll(x, 64, 2)], 1)


def unpack_high(x):
    return jnp.concatenate([pltpu.roll(x, 64, 2), x], 1)


def place(rows, cols):
    row, col = lax.axis_index("row"), lax.axis_index("col")
    around = {}
    for dr in (-1, 0, 1):
        for dc in (-1, 0, 1):
            if dr or dc:
                around[dr, dc] = (lax.rem(row + dr + rows, rows), lax.rem(col + dc + cols, cols))
    return row, col, around


def inside(row, col, rows, cols, dr, dc):
    ok = jnp.float32(1.0)
    if dr == -1:
        ok = ok * (row > 0).astype(jnp.float32)
    if dr == 1:
        ok = ok * (row < rows - 1).astype(jnp.float32)
    if dc == -1:
        ok = ok * (col > 0).astype(jnp.float32)
    if dc == 1:
        ok = ok * (col < cols - 1).astype(jnp.float32)
    return ok


SIDES = [(-1, 0), (1, 0), (0, -1), (0, 1), (-1, -1), (-1, 1), (1, -1), (1, 1)]


def kernel(
    rows, cols, nx, n1, cap, mixes,
    o_hbm, a_hbm, counts_hbm, offs_hbm, index_hbm, mix_hbm, modes_hbm, tab_hbm,
    new_object, fresh,
    obj, amps, counts, offs, index, mix, modes, tab,
    ps, pc, rv, rs, rc, tiles, probes, patches, psis, backs, deltas, sums, pad, marg,
    on, op, oc, orv, ors, orc, got, half, r1, r2, r3,
    load, send, recv, pair_send, pair_recv,
):
    n = 128
    nz = rows // nx
    row, col, around = place(rows, cols)
    x, z = row // nz, lax.rem(row, nz)
    y, core = col // 2, lax.rem(col, 2)
    p1 = z + core * (y - z)
    p2 = y + core * (z - y)
    sibling = (row, col + 1 - 2 * core)
    high = 2 * core
    other = 2 - high

    def first_peer(d):
        a = lax.rem(p1 + d, n1)
        return a, (x * nz + z + (1 - core) * (a - z), (y + core * (a - y)) * 2 + core)

    def second_peer(d):
        a = lax.rem(p2 + d, n1)
        return a, (x * nz + z + core * (a - z), (y + (1 - core) * (a - y)) * 2 + core)

    def x_peer(d):
        a = lax.rem(x + d, nx)
        return a, (a * nz + z, col)

    used = [0]
    pending = []

    def copy(src, dst, device):
        i = used[0]
        used[0] += 1
        made = pltpu.make_async_remote_copy(
            src_ref=src, dst_ref=dst, send_sem=send.at[i], recv_sem=recv.at[i],
            device_id=device, device_id_type=MESH,
        )
        made.start()
        pending.append(made)
        return made

    def ok(dr, dc):
        return inside(row, col, rows, cols, dr, dc)

    barrier = pltpu.get_barrier_semaphore()
    partners = (
        [around[s] for s in SIDES]
        + [sibling]
        + [first_peer(d)[1] for d in range(1, n1)]
        + [second_peer(d)[1] for d in range(1, n1)]
        + [x_peer(d)[1] for d in range(1, nx)]
    )
    for device in partners:
        pl.semaphore_signal(barrier, inc=1, device_id=device, device_id_type=MESH)
    loads = [
        pltpu.make_async_copy(src, dst, load.at[i])
        for i, (src, dst) in enumerate(
            (
                (o_hbm, obj), (modes_hbm, modes), (mix_hbm, mix), (index_hbm, index), (counts_hbm, counts),
                (offs_hbm, offs), (tab_hbm, tab), (a_hbm, amps),
            )
        )
    ]
    for c in loads:
        c.start()

    loads[0].wait()
    ps[0] = pack_low(obj[...])
    ps[1] = pack_high(obj[...])
    pc[0] = pack_low(obj[:, :64])
    pc[1] = pack_high(obj[:, :64])
    pc[2] = pack_low(obj[:, 64:])
    pc[3] = pack_high(obj[:, 64:])
    pl.semaphore_wait(barrier, len(partners))
    halo = [
        copy(pc.at[0], rc.at[0], around[-1, -1]),
        copy(pc.at[1], rc.at[1], around[-1, 1]),
        copy(pc.at[2], rc.at[2], around[1, -1]),
        copy(pc.at[3], rc.at[3], around[1, 1]),
        copy(obj.at[:, 0:64], rv.at[0], around[-1, 0]),
        copy(obj.at[:, 64:128], rv.at[1], around[1, 0]),
        copy(ps.at[0], rs.at[0], around[0, -1]),
        copy(ps.at[1], rs.at[1], around[0, 1]),
    ]

    for c in loads[1:]:
        c.wait()
    marg[...] = jnp.zeros_like(marg)
    pad[...] = jnp.zeros_like(pad)
    count = counts[0, 0]

    def spot(slot):
        top = jnp.clip(offs[0, 0, 0, slot], 0, n - 1)
        left_px = jnp.clip(offs[0, 0, 1, slot], 0, n - 1)
        return top, left_px

    def weights_of(slot):
        pick = jnp.clip(index[0, 0, slot], 0, mixes - 1)
        return [jnp.where(slot < count, mix[k, pick], 0.0) for k in range(4)]

    def spread(frames, spots):
        for f in frames:
            for h in range(4):
                part = slice(h * 64, (h + 1) * 64)
                low, up = marg[f, 0, part], marg[f, 1, part]
                for i, (top, left_px) in enumerate(spots):
                    value = pad[i, f, pl.ds(n - top + h * 64, 64), :]
                    mask = lanes_iota((64, n)) >= left_px
                    low = low + jnp.where(mask, value, 0.0)
                    up = up + jnp.where(mask, 0.0, value)
                marg[f, 0, part] = low
                marg[f, 1, part] = up

    def centre(frames, part):
        own, end = marg[frames, 0, part], marg[frames, 1, part]
        return jnp.where(lanes_iota(own.shape) < 64, pltpu.roll(own, 64, 2), pltpu.roll(end, 64, 2))

    def send_edges(frames):
        top, middle, bottom = slice(0, 64), slice(64, 192), slice(192, 256)
        on[0, frames] = centre(frames, top)
        on[1, frames] = centre(frames, bottom)
        op[0, frames] = pack_low(marg[frames, 0, middle])
        op[1, frames] = pack_high(marg[frames, 1, middle])
        oc[0, frames] = pack_low(marg[frames, 0, top])
        oc[1, frames] = pack_high(marg[frames, 1, top])
        oc[2, frames] = pack_low(marg[frames, 0, bottom])
        oc[3, frames] = pack_high(marg[frames, 1, bottom])
        return [
            copy(oc.at[0, frames], orc.at[0, frames], around[-1, -1]),
            copy(oc.at[1, frames], orc.at[1, frames], around[-1, 1]),
            copy(oc.at[2, frames], orc.at[2, frames], around[1, -1]),
            copy(oc.at[3, frames], orc.at[3, frames], around[1, 1]),
            copy(on.at[0, frames], orv.at[0, frames], around[-1, 0]),
            copy(on.at[1, frames], orv.at[1, frames], around[1, 0]),
            copy(op.at[0, frames], ors.at[0, frames], around[0, -1]),
            copy(op.at[1, frames], ors.at[1, frames], around[0, 1]),
        ]

    def make_probes(step, carry):
        slots = [step * GROUP + i for i in range(GROUP)]
        spots = [spot(slot) for slot in slots]
        for i, slot in enumerate(slots):
            w = weights_of(slot)
            probe = []
            for comp in range(2):
                total = w[0] * modes[0, comp]
                for k in range(1, 4):
                    total = total + w[k] * modes[k, comp]
                probes[slot, comp] = total
                probe.append(total)
            value = probe[0] * probe[0] + probe[1] * probe[1]
            pad[i, 2, n : 2 * n] = pltpu.roll(value, spots[i][1], 1)
        spread((2,), spots)
        return carry

    lax.fori_loop(0, cap // GROUP, make_probes, 0)
    edge = send_edges(slice(2, 3))
    for c in halo:
        c.wait_recv()

    def tile_rows(target, west, own, east):
        turned = pltpu.roll(own, 64, 2)
        low = lanes_iota(own.shape) < 64
        tiles[:, 0, target] = jnp.where(low, west, turned)
        tiles[:, 1, target] = jnp.where(low, turned, east)

    tile_rows(
        slice(0, 64), unpack_low(rc[3] * ok(-1, -1)), rv[1] * ok(-1, 0), unpack_high(rc[2] * ok(-1, 1))
    )
    tile_rows(slice(64, 192), unpack_low(rs[1] * ok(0, -1)), obj[...], unpack_high(rs[0] * ok(0, 1)))
    tile_rows(
        slice(192, 256), unpack_low(rc[1] * ok(1, -1)), rv[0] * ok(1, 0), unpack_high(rc[0] * ok(1, 1))
    )

    fwd, inv = tab[0], tab[1]

    def dot(a, b):
        return jnp.dot(a, b, preferred_element_type=jnp.float32)

    def left(table, res, ims):
        out = dot(table, jnp.concatenate([jnp.concatenate(res, 1), jnp.concatenate(ims, 1)], 0))
        return (
            [out[:n, i * n : (i + 1) * n] for i in range(len(res))],
            [out[n:, i * n : (i + 1) * n] for i in range(len(res))],
        )

    def right(table, res, ims):
        out = dot(jnp.concatenate([jnp.concatenate([a, b], 1) for a, b in zip(res, ims)], 0), table)
        return (
            [out[i * n : (i + 1) * n, :n] for i in range(len(res))],
            [out[i * n : (i + 1) * n, n:] for i in range(len(res))],
        )

    def lower(xs):
        return [v.astype(jnp.bfloat16) for v in xs]

    lane = lanes_iota((n, n))

    def visit(step, carry):
        slots = [step * TEAM + i for i in range(TEAM)]
        psi_r, psi_i = [], []
        for slot in slots:
            top, left_px = spot(slot)
            mask = lane >= left_px
            patch = []
            for comp in range(2):
                a = tiles[comp, 0, pl.ds(top, n), :]
                b = tiles[comp, 1, pl.ds(top, n), :]
                patch.append(pltpu.roll(jnp.where(mask, a, b), lax.rem(n - left_px, n), 1))
                patches[slot, comp] = patch[comp]
            pr, pi = probes[slot, 0], probes[slot, 1]
            real = pr * patch[0] - pi * patch[1]
            imag = pr * patch[1] + pi * patch[0]
            psis[slot, 0] = real
            psis[slot, 1] = imag
            psi_r.append(real.astype(jnp.bfloat16))
            psi_i.append(imag.astype(jnp.bfloat16))
        re, im = left(fwd, psi_r, psi_i)
        re, im = right(inv, lower(re), lower(im))
        fixed_re, fixed_im = [], []
        for slot, a, b in zip(slots, re, im):
            ratio = amps[0, 0, slot].astype(jnp.float32) * lax.rsqrt(jnp.maximum(a * a + b * b, FLOOR * FLOOR))
            fixed_re.append((a * ratio).astype(jnp.bfloat16))
            fixed_im.append((b * ratio).astype(jnp.bfloat16))
        re, im = left(inv, fixed_re, fixed_im)
        for slot, a, b in zip(slots, lower(re), lower(im)):
            backs[slot, :, :n] = a
            backs[slot, :, n:] = b
        return carry

    lax.fori_loop(0, cap // TEAM, visit, 0)

    thick = n // n1

    def chunk(a):
        return pl.ds(pl.multiple_of(a * thick, thick), thick)

    def pair_copy(i, d):
        piece = chunk(lax.rem(p2 + d, n1))
        return pltpu.make_async_remote_copy(
            src_ref=sums.at[pl.ds(other, 2), :, piece], dst_ref=got.at[:, :, piece],
            send_sem=pair_send.at[i], recv_sem=pair_recv.at[i], device_id=sibling, device_id_type=MESH,
        )

    def finish_rows(i, carry):
        d = n1 // 2 + (1 - 2 * lax.rem(i, 2)) * ((i + 1) // 2)
        rows_here = chunk(lax.rem(p2 + d, n1))
        out = dot(backs[:, rows_here, :].reshape(cap * thick, 2 * n), fwd)
        totals = [[jnp.zeros((thick, n), jnp.float32) for _ in range(3)] for _ in range(4)]
        for slot in range(cap):
            part = slice(slot * thick, (slot + 1) * thick)
            dr = out[part, :n] - psis[slot, 0, rows_here]
            di = out[part, n:] - psis[slot, 1, rows_here]
            deltas[slot, 0, rows_here] = dr
            deltas[slot, 1, rows_here] = di
            ar, ai = patches[slot, 0, rows_here], patches[slot, 1, rows_here]
            pieces = (ar * dr + ai * di, ar * di - ai * dr, ar * ar + ai * ai)
            w = weights_of(slot)
            for k in range(4):
                totals[k][0] = totals[k][0] + w[k] * pieces[0]
                totals[k][1] = totals[k][1] + w[k] * pieces[1]
                totals[k][2] = totals[k][2] + (w[k] * w[k]) * pieces[2]
        for k in range(4):
            for f in range(3):
                sums[k, f, rows_here] = totals[k][f]
        pair_copy(i, d).start()
        return carry

    lax.fori_loop(0, n1, finish_rows, 0)
    order = FAR + (0,)
    pair_out = [pair_copy(i, d) for i, d in enumerate(order)]
    sent = []
    for d, c in zip(order, pair_out):
        c.wait_recv()
        a, device = first_peer(d)
        half[:, :, chunk(a)] = sums[pl.ds(high, 2), :, chunk(a)] + got[:, :, chunk(a)]
        if d:
            sent.append(copy(half.at[:, :, chunk(a)], r1.at[d - 1], device))

    def numerators(step, carry):
        slots = [step * GROUP + i for i in range(GROUP)]
        spots = [spot(slot) for slot in slots]
        for i, slot in enumerate(slots):
            pr, pi = probes[slot, 0], probes[slot, 1]
            dr, di = deltas[slot, 0], deltas[slot, 1]
            for f, value in enumerate((pr * dr + pi * di, pr * di - pi * dr)):
                pad[i, f, n : 2 * n] = pltpu.roll(value, spots[i][1], 1)
        spread((0, 1), spots)
        return carry

    lax.fori_loop(0, cap // GROUP, numerators, 0)

    mine = chunk(p1)
    total = half[:, :, mine]
    for d, c in zip(FAR[::-1], sent[::-1]):
        c.wait_recv()
        total = total + r1[d - 1]
    parts = thick // 8
    for m in range(2):
        for t in range(parts):
            r2[m * parts + t] = total[m, :, t * 8 : (t + 1) * 8]
    sent = []
    for d in range(1, nx):
        a, device = x_peer(d)
        sent.append(copy(r2.at[a], r2.at[nx + d - 1], device))
    total = r2[x]
    for d, c in enumerate(sent):
        c.wait_recv()
        total = total + r2[nx + d]
    r3[p2] = total
    sent = []
    for d in FAR:
        _, device = second_peer(d)
        sent.append(copy(r3.at[p2], r3.at[p2], device))
    edge += send_edges(slice(0, 2))
    for c in sent:
        c.wait_recv()
    total = r3[0]
    for a in range(1, n1):
        total = total + r3[a]
    mode, tile = high + x // parts, lax.rem(x, parts)
    unit = pl.ds(pl.multiple_of(p1 * thick + tile * 8, 8), 8)
    fresh[mode, :, unit] = modes[mode, :, unit] + total[:2] / (total[2:] + RELAX)
    sent = []
    for d in range(1, nx):
        _, device = x_peer(d)
        sent.append(copy(fresh.at[mode, :, unit], fresh.at[mode, :, unit], device))
    for c in sent:
        c.wait_recv()
    both = pl.ds(high, 2)
    sent = {}
    for d in FAR:
        _, device = first_peer(d)
        sent[d] = copy(fresh.at[both, :, mine], fresh.at[both, :, mine], device)
    pair = [copy(fresh.at[both, :, mine], fresh.at[both, :, mine], sibling)]

    for c in edge:
        c.wait_recv()
    west = unpack_low(ors[1] * ok(0, -1))
    east = unpack_high(ors[0] * ok(0, 1))
    for part, inner, vertical, lo, up in (
        (slice(0, 64), slice(64, 128), orv[1] * ok(-1, 0), orc[3] * ok(-1, -1), orc[2] * ok(-1, 1)),
        (slice(64, 128), slice(128, 192), orv[0] * ok(1, 0), orc[1] * ok(1, -1), orc[0] * ok(1, 1)),
    ):
        side = jnp.where(lanes_iota((3, 64, n)) < 64, west[:, part] + unpack_low(lo), east[:, part] + unpack_high(up))
        both_sums = centre(slice(0, 3), inner) + vertical + side
        new_object[:, part] = obj[:, part] + both_sums[:2] / (both_sums[2:] + RELAX)

    for d in NEAR:
        sent[d].wait_recv()
        piece = chunk(lax.rem(p1 + n1 - d, n1))
        pair.append(copy(fresh.at[both, :, piece], fresh.at[both, :, piece], sibling))
    for c in pair:
        c.wait_recv()

    for c in pending + pair_out:
        c.wait_send()


def finish_kernel(object_in, fresh, object_out, modes_out, made, sem):
    first = pltpu.make_async_copy(object_in, object_out, sem.at[0])
    first.start()
    copies = [first]
    scale = 1.0 / (fresh.shape[2] * fresh.shape[3])

    def mean(v):
        return jnp.sum(jnp.sum(v, 0, keepdims=True), 1, keepdims=True) * scale

    basis = []
    coefs = {}
    for k in range(4):
        vr, vi = fresh[k, 0], fresh[k, 1]
        for j in range(k):
            cr, ci = coefs[j, k]
            br, bi = basis[j]
            vr = vr - (cr * br - ci * bi)
            vi = vi - (cr * bi + ci * br)
        norm = 1.0 / jnp.sqrt(mean(vr * vr + vi * vi) + EPSILON)
        qr, qi = vr * norm, vi * norm
        basis.append((qr, qi))
        made[k, 0] = qr
        made[k, 1] = qi
        write = pltpu.make_async_copy(made.at[k], modes_out.at[k], sem.at[k + 1])
        write.start()
        copies.append(write)
        for later in range(k + 1, 4):
            fr, fi = fresh[later, 0], fresh[later, 1]
            coefs[k, later] = (mean(qr * fr + qi * fi), mean(qr * fi - qi * fr))
    for c in copies:
        c.wait()


def solution(mesh):
    rows, cols = mesh.shape["row"], mesh.shape["col"]
    nx = 4
    n1 = cols // 2
    f32, bf16, i32 = jnp.float32, jnp.bfloat16, jnp.int32

    def body(object_field, amplitudes, counts, offsets, mode_index, mix_table, probe_modes):
        cap, mixes = amplitudes.shape[2], mix_table.shape[0]
        number = 8 + 16 + 8 + 3 * (n1 - 1) + 2 * (nx - 1)
        new_object, fresh = pl.pallas_call(
            functools.partial(kernel, rows, cols, nx, n1, cap, mixes),
            out_shape=(
                pltpu.VMEM((2, 128, 128), f32),
                pltpu.VMEM((4, 2, 128, 128), f32),
            ),
            in_specs=[HBM] * 8,
            out_specs=(VMEM, VMEM),
            scratch_shapes=[
                pltpu.VMEM((2, 128, 128), f32),
                pltpu.VMEM(amplitudes.shape, bf16),
                pltpu.SMEM((1, 1), i32),
                pltpu.SMEM((1, 1, 2, cap), i32),
                pltpu.SMEM((1, 1, cap), i32),
                pltpu.SMEM((4, mixes), f32),
                pltpu.VMEM((4, 2, 128, 128), f32),
                pltpu.VMEM((2, 256, 256), bf16),
                pltpu.VMEM((2, 2, 64, 128), f32),
                pltpu.VMEM((4, 2, 32, 128), f32),
                pltpu.VMEM((2, 2, 64, 128), f32),
                pltpu.VMEM((2, 2, 64, 128), f32),
                pltpu.VMEM((4, 2, 32, 128), f32),
                pltpu.VMEM((2, 2, 256, 128), f32),
                pltpu.VMEM((cap, 2, 128, 128), f32),
                pltpu.VMEM((cap, 2, 128, 128), f32),
                pltpu.VMEM((cap, 2, 128, 128), f32),
                pltpu.VMEM((cap, 128, 256), bf16),
                pltpu.VMEM((cap, 2, 128, 128), f32),
                pltpu.VMEM((4, 3, 128, 128), f32),
                pltpu.VMEM((GROUP, 3, 384, 128), f32),
                pltpu.VMEM((3, 2, 256, 128), f32),
                pltpu.VMEM((2, 3, 64, 128), f32),
                pltpu.VMEM((2, 3, 64, 128), f32),
                pltpu.VMEM((4, 3, 32, 128), f32),
                pltpu.VMEM((2, 3, 64, 128), f32),
                pltpu.VMEM((2, 3, 64, 128), f32),
                pltpu.VMEM((4, 3, 32, 128), f32),
                pltpu.VMEM((2, 3, 128, 128), f32),
                pltpu.VMEM((2, 3, 128, 128), f32),
                pltpu.VMEM((n1 - 1, 2, 3, 128 // n1, 128), f32),
                pltpu.VMEM((2 * nx, 3, 8, 128), f32),
                pltpu.VMEM((n1, 3, 8, 128), f32),
                pltpu.SemaphoreType.DMA((8,)),
                pltpu.SemaphoreType.DMA((number,)),
                pltpu.SemaphoreType.DMA((number,)),
                pltpu.SemaphoreType.DMA((n1,)),
                pltpu.SemaphoreType.DMA((n1,)),
            ],
            compiler_params=pltpu.CompilerParams(
                collective_id=0, has_side_effects=True, vmem_limit_bytes=56 * 1024 * 1024
            ),
            name="update",
        )(
            object_field, amplitudes, counts, jnp.swapaxes(offsets, 2, 3), mode_index, mix_table.T,
            probe_modes, jnp.asarray(tables(128)),
        )
        return pl.pallas_call(
            finish_kernel,
            out_shape=(
                jax.ShapeDtypeStruct((2, 128, 128), f32),
                jax.ShapeDtypeStruct((4, 2, 128, 128), f32),
            ),
            in_specs=[VMEM, VMEM],
            out_specs=(HBM, HBM),
            scratch_shapes=[pltpu.VMEM((4, 2, 128, 128), f32), pltpu.SemaphoreType.DMA((5,))],
            compiler_params=pltpu.CompilerParams(vmem_limit_bytes=8 * 1024 * 1024),
            name="finish",
        )(new_object, fresh)

    return jax.shard_map(
        body,
        mesh=mesh,
        in_specs=(
            P(None, "row", "col"),
            P("row", "col", None, None, None),
            P("row", "col"),
            P("row", "col", None, None),
            P("row", "col", None),
            P(),
            P(),
        ),
        out_specs=(P(None, "row", "col"), P()),
        check_vma=False,
    )
```

```python
import functools

import jax
import jax.numpy as jnp
import ml_dtypes
import numpy as np
from jax import lax
from jax.experimental import pallas as pl
from jax.experimental.pallas import tpu as pltpu
from jax.sharding import PartitionSpec as P

FLOOR = 0.25
RELAX = 0.5
EPSILON = 1e-06
GROUP = 2
TEAM = 12
FAR = (4, 3, 5, 2, 6, 1, 7)
NEAR = (1, 7, 2, 6, 3, 5, 4)
MESH = pl.DeviceIdType.MESH
VMEM = pl.BlockSpec(memory_space=pltpu.VMEM)
HBM = pl.BlockSpec(memory_space=pltpu.HBM)


def tables(size):
    index = np.arange(size)
    angle = (index[:, None] * index[None, :] % size).astype(np.float32) * np.float32(2.0 * np.pi / size)
    factor = np.float32(1.0 / np.sqrt(size))
    c = (np.cos(angle) * factor).astype(ml_dtypes.bfloat16)
    s = (np.sin(angle) * factor).astype(ml_dtypes.bfloat16)
    p = np.concatenate([np.concatenate([c, s], 1), np.concatenate([-s, c], 1)], 0)
    q = np.concatenate([np.concatenate([c, -s], 1), np.concatenate([s, c], 1)], 0)
    return np.stack([p, q])


def lanes_iota(shape):
    return lax.broadcasted_iota(jnp.int32, shape, len(shape) - 1)


def pack_low(x):
    n = x.shape[1] // 2
    a, b = x[:, :n], x[:, n:]
    return jnp.where(lanes_iota(a.shape) < 64, a, pltpu.roll(b, 64, 2))


def pack_high(x):
    n = x.shape[1] // 2
    a, b = x[:, :n], x[:, n:]
    return jnp.where(lanes_iota(a.shape) < 64, pltpu.roll(a, 64, 2), b)


def unpack_low(x):
    return jnp.concatenate([x, pltpu.roll(x, 64, 2)], 1)


def unpack_high(x):
    return jnp.concatenate([pltpu.roll(x, 64, 2), x], 1)


def place(rows, cols):
    row, col = lax.axis_index("row"), lax.axis_index("col")
    around = {}
    for dr in (-1, 0, 1):
        for dc in (-1, 0, 1):
            if dr or dc:
                around[dr, dc] = (lax.rem(row + dr + rows, rows), lax.rem(col + dc + cols, cols))
    return row, col, around


def inside(row, col, rows, cols, dr, dc):
    ok = jnp.float32(1.0)
    if dr == -1:
        ok = ok * (row > 0).astype(jnp.float32)
    if dr == 1:
        ok = ok * (row < rows - 1).astype(jnp.float32)
    if dc == -1:
        ok = ok * (col > 0).astype(jnp.float32)
    if dc == 1:
        ok = ok * (col < cols - 1).astype(jnp.float32)
    return ok


SIDES = [(-1, 0), (1, 0), (0, -1), (0, 1), (-1, -1), (-1, 1), (1, -1), (1, 1)]


def kernel(
    rows, cols, nx, n1, cap, mixes,
    o_hbm, a_hbm, counts_hbm, offs_hbm, index_hbm, mix_hbm, modes_hbm, tab_hbm,
    new_object, fresh,
    obj, amps, counts, offs, index, mix, modes, tab,
    ps, pc, rv, rs, rc, tiles, probes, patches, psis, backs, deltas, sums, pad, marg,
    on, op, oc, orv, ors, orc, got, half, r1, r2, r3,
    load, send, recv, pair_send, pair_recv,
):
    n = 128
    nz = rows // nx
    row, col, around = place(rows, cols)
    x, z = row // nz, lax.rem(row, nz)
    y, core = col // 2, lax.rem(col, 2)
    p1 = z + core * (y - z)
    p2 = y + core * (z - y)
    sibling = (row, col + 1 - 2 * core)
    high = 2 * core
    other = 2 - high

    def first_peer(d):
        a = lax.rem(p1 + d, n1)
        return a, (x * nz + z + (1 - core) * (a - z), (y + core * (a - y)) * 2 + core)

    def second_peer(d):
        a = lax.rem(p2 + d, n1)
        return a, (x * nz + z + core * (a - z), (y + (1 - core) * (a - y)) * 2 + core)

    def x_peer(d):
        a = lax.rem(x + d, nx)
        return a, (a * nz + z, col)

    used = [0]
    pending = []

    def copy(src, dst, device):
        i = used[0]
        used[0] += 1
        made = pltpu.make_async_remote_copy(
            src_ref=src, dst_ref=dst, send_sem=send.at[i], recv_sem=recv.at[i],
            device_id=device, device_id_type=MESH,
        )
        made.start()
        pending.append(made)
        return made

    def ok(dr, dc):
        return inside(row, col, rows, cols, dr, dc)

    barrier = pltpu.get_barrier_semaphore()
    partners = (
        [around[s] for s in SIDES]
        + [sibling]
        + [first_peer(d)[1] for d in range(1, n1)]
        + [second_peer(d)[1] for d in range(1, n1)]
        + [x_peer(d)[1] for d in range(1, nx)]
    )
    for device in partners:
        pl.semaphore_signal(barrier, inc=1, device_id=device, device_id_type=MESH)
    loads = [
        pltpu.make_async_copy(src, dst, load.at[i])
        for i, (src, dst) in enumerate(
            (
                (o_hbm, obj), (modes_hbm, modes), (mix_hbm, mix), (index_hbm, index), (counts_hbm, counts),
                (offs_hbm, offs), (tab_hbm, tab), (a_hbm, amps),
            )
        )
    ]
    for c in loads:
        c.start()

    loads[0].wait()
    ps[0] = pack_low(obj[...])
    ps[1] = pack_high(obj[...])
    pc[0] = pack_low(obj[:, :64])
    pc[1] = pack_high(obj[:, :64])
    pc[2] = pack_low(obj[:, 64:])
    pc[3] = pack_high(obj[:, 64:])
    pl.semaphore_wait(barrier, len(partners))
    halo = [
        copy(pc.at[0], rc.at[0], around[-1, -1]),
        copy(pc.at[1], rc.at[1], around[-1, 1]),
        copy(pc.at[2], rc.at[2], around[1, -1]),
        copy(pc.at[3], rc.at[3], around[1, 1]),
        copy(obj.at[:, 0:64], rv.at[0], around[-1, 0]),
        copy(obj.at[:, 64:128], rv.at[1], around[1, 0]),
        copy(ps.at[0], rs.at[0], around[0, -1]),
        copy(ps.at[1], rs.at[1], around[0, 1]),
    ]

    for c in loads[1:]:
        c.wait()
    marg[...] = jnp.zeros_like(marg)
    pad[...] = jnp.zeros_like(pad)
    count = counts[0, 0]

    def spot(slot):
        top = jnp.clip(offs[0, 0, 0, slot], 0, n - 1)
        left_px = jnp.clip(offs[0, 0, 1, slot], 0, n - 1)
        return top, left_px

    def weights_of(slot):
        pick = jnp.clip(index[0, 0, slot], 0, mixes - 1)
        return [jnp.where(slot < count, mix[k, pick], 0.0) for k in range(4)]

    def spread(frames, spots):
        for f in frames:
            for h in range(4):
                part = slice(h * 64, (h + 1) * 64)
                low, up = marg[f, 0, part], marg[f, 1, part]
                for i, (top, left_px) in enumerate(spots):
                    value = pad[i, f, pl.ds(n - top + h * 64, 64), :]
                    mask = lanes_iota((64, n)) >= left_px
                    low = low + jnp.where(mask, value, 0.0)
                    up = up + jnp.where(mask, 0.0, value)
                marg[f, 0, part] = low
                marg[f, 1, part] = up

    def centre(frames, part):
        own, end = marg[frames, 0, part], marg[frames, 1, part]
        return jnp.where(lanes_iota(own.shape) < 64, pltpu.roll(own, 64, 2), pltpu.roll(end, 64, 2))

    def send_edges(frames):
        top, middle, bottom = slice(0, 64), slice(64, 192), slice(192, 256)
        on[0, frames] = centre(frames, top)
        on[1, frames] = centre(frames, bottom)
        op[0, frames] = pack_low(marg[frames, 0, middle])
        op[1, frames] = pack_high(marg[frames, 1, middle])
        oc[0, frames] = pack_low(marg[frames, 0, top])
        oc[1, frames] = pack_high(marg[frames, 1, top])
        oc[2, frames] = pack_low(marg[frames, 0, bottom])
        oc[3, frames] = pack_high(marg[frames, 1, bottom])
        return [
            copy(oc.at[0, frames], orc.at[0, frames], around[-1, -1]),
            copy(oc.at[1, frames], orc.at[1, frames], around[-1, 1]),
            copy(oc.at[2, frames], orc.at[2, frames], around[1, -1]),
            copy(oc.at[3, frames], orc.at[3, frames], around[1, 1]),
            copy(on.at[0, frames], orv.at[0, frames], around[-1, 0]),
            copy(on.at[1, frames], orv.at[1, frames], around[1, 0]),
            copy(op.at[0, frames], ors.at[0, frames], around[0, -1]),
            copy(op.at[1, frames], ors.at[1, frames], around[0, 1]),
        ]

    def make_probes(step, carry):
        slots = [step * GROUP + i for i in range(GROUP)]
        spots = [spot(slot) for slot in slots]
        for i, slot in enumerate(slots):
            w = weights_of(slot)
            probe = []
            for comp in range(2):
                total = w[0] * modes[0, comp]
                for k in range(1, 4):
                    total = total + w[k] * modes[k, comp]
                probes[slot, comp] = total
                probe.append(total)
            value = probe[0] * probe[0] + probe[1] * probe[1]
            pad[i, 2, n : 2 * n] = pltpu.roll(value, spots[i][1], 1)
        spread((2,), spots)
        return carry

    lax.fori_loop(0, cap // GROUP, make_probes, 0)
    edge = send_edges(slice(2, 3))
    for c in halo:
        c.wait_recv()

    def tile_rows(target, west, own, east):
        turned = pltpu.roll(own, 64, 2)
        low = lanes_iota(own.shape) < 64
        tiles[:, 0, target] = jnp.where(low, west, turned)
        tiles[:, 1, target] = jnp.where(low, turned, east)

    tile_rows(
        slice(0, 64), unpack_low(rc[3] * ok(-1, -1)), rv[1] * ok(-1, 0), unpack_high(rc[2] * ok(-1, 1))
    )
    tile_rows(slice(64, 192), unpack_low(rs[1] * ok(0, -1)), obj[...], unpack_high(rs[0] * ok(0, 1)))
    tile_rows(
        slice(192, 256), unpack_low(rc[1] * ok(1, -1)), rv[0] * ok(1, 0), unpack_high(rc[0] * ok(1, 1))
    )

    fwd, inv = tab[0], tab[1]

    def dot(a, b):
        return jnp.dot(a, b, preferred_element_type=jnp.float32)

    def left(table, res, ims):
        out = dot(table, jnp.concatenate([jnp.concatenate(res, 1), jnp.concatenate(ims, 1)], 0))
        return (
            [out[:n, i * n : (i + 1) * n] for i in range(len(res))],
            [out[n:, i * n : (i + 1) * n] for i in range(len(res))],
        )

    def right(table, res, ims):
        out = dot(jnp.concatenate([jnp.concatenate([a, b], 1) for a, b in zip(res, ims)], 0), table)
        return (
            [out[i * n : (i + 1) * n, :n] for i in range(len(res))],
            [out[i * n : (i + 1) * n, n:] for i in range(len(res))],
        )

    def lower(xs):
        return [v.astype(jnp.bfloat16) for v in xs]

    lane = lanes_iota((n, n))

    def visit(step, carry):
        slots = [step * TEAM + i for i in range(TEAM)]
        psi_r, psi_i = [], []
        for slot in slots:
            top, left_px = spot(slot)
            mask = lane >= left_px
            patch = []
            for comp in range(2):
                a = tiles[comp, 0, pl.ds(top, n), :]
                b = tiles[comp, 1, pl.ds(top, n), :]
                patch.append(pltpu.roll(jnp.where(mask, a, b), lax.rem(n - left_px, n), 1))
                patches[slot, comp] = patch[comp]
            pr, pi = probes[slot, 0], probes[slot, 1]
            real = pr * patch[0] - pi * patch[1]
            imag = pr * patch[1] + pi * patch[0]
            psis[slot, 0] = real
            psis[slot, 1] = imag
            psi_r.append(real.astype(jnp.bfloat16))
            psi_i.append(imag.astype(jnp.bfloat16))
        re, im = left(fwd, psi_r, psi_i)
        re, im = right(inv, lower(re), lower(im))
        fixed_re, fixed_im = [], []
        for slot, a, b in zip(slots, re, im):
            ratio = amps[0, 0, slot].astype(jnp.float32) * lax.rsqrt(jnp.maximum(a * a + b * b, FLOOR * FLOOR))
            fixed_re.append((a * ratio).astype(jnp.bfloat16))
            fixed_im.append((b * ratio).astype(jnp.bfloat16))
        re, im = left(inv, fixed_re, fixed_im)
        for slot, a, b in zip(slots, lower(re), lower(im)):
            backs[slot, :, :n] = a
            backs[slot, :, n:] = b
        return carry

    lax.fori_loop(0, cap // TEAM, visit, 0)

    thick = n // n1

    def chunk(a):
        return pl.ds(pl.multiple_of(a * thick, thick), thick)

    def pair_copy(i, d):
        piece = chunk(lax.rem(p2 + d, n1))
        return pltpu.make_async_remote_copy(
            src_ref=sums.at[pl.ds(other, 2), :, piece], dst_ref=got.at[:, :, piece],
            send_sem=pair_send.at[i], recv_sem=pair_recv.at[i], device_id=sibling, device_id_type=MESH,
        )

    def finish_rows(i, carry):
        d = n1 // 2 + (1 - 2 * lax.rem(i, 2)) * ((i + 1) // 2)
        rows_here = chunk(lax.rem(p2 + d, n1))
        out = dot(backs[:, rows_here, :].reshape(cap * thick, 2 * n), fwd)
        totals = [[jnp.zeros((thick, n), jnp.float32) for _ in range(3)] for _ in range(4)]
        for slot in range(cap):
            part = slice(slot * thick, (slot + 1) * thick)
            dr = out[part, :n] - psis[slot, 0, rows_here]
            di = out[part, n:] - psis[slot, 1, rows_here]
            deltas[slot, 0, rows_here] = dr
            deltas[slot, 1, rows_here] = di
            ar, ai = patches[slot, 0, rows_here], patches[slot, 1, rows_here]
            pieces = (ar * dr + ai * di, ar * di - ai * dr, ar * ar + ai * ai)
            w = weights_of(slot)
            for k in range(4):
                totals[k][0] = totals[k][0] + w[k] * pieces[0]
                totals[k][1] = totals[k][1] + w[k] * pieces[1]
                totals[k][2] = totals[k][2] + (w[k] * w[k]) * pieces[2]
        for k in range(4):
            for f in range(3):
                sums[k, f, rows_here] = totals[k][f]
        pair_copy(i, d).start()
        return carry

    lax.fori_loop(0, n1, finish_rows, 0)
    order = FAR + (0,)
    pair_out = [pair_copy(i, d) for i, d in enumerate(order)]
    streams = (0, 1)
    sent = [[], []]

    def send_first(m, d):
        a, device = first_peer(d)
        sent[m].append(copy(half.at[m, :, chunk(a)], r1.at[m, d - 1], device))

    for d, c in zip(order, pair_out):
        c.wait_recv()
        a, _ = first_peer(d)
        half[:, :, chunk(a)] = sums[pl.ds(high, 2), :, chunk(a)] + got[:, :, chunk(a)]
        if d:
            send_first(0, d)
    for d in FAR:
        send_first(1, d)

    def numerators(step, carry):
        slots = [step * GROUP + i for i in range(GROUP)]
        spots = [spot(slot) for slot in slots]
        for i, slot in enumerate(slots):
            pr, pi = probes[slot, 0], probes[slot, 1]
            dr, di = deltas[slot, 0], deltas[slot, 1]
            for f, value in enumerate((pr * dr + pi * di, pr * di - pi * dr)):
                pad[i, f, n : 2 * n] = pltpu.roll(value, spots[i][1], 1)
        spread((0, 1), spots)
        return carry

    lax.fori_loop(0, cap // GROUP, numerators, 0)

    mine = chunk(p1)
    parity = lax.rem(x, 2)
    x_sent = [[], []]
    for m in streams:
        total = half[m, :, mine]
        for d, c in zip(FAR[::-1], sent[m][::-1]):
            c.wait_recv()
            total = total + r1[m, d - 1]
        for t in range(2):
            r2[m, t] = total[:, t * 8 : (t + 1) * 8]
        r2[m, 2 + x] = r2[m, parity]
        for d in range(1, nx):
            a, device = x_peer(d)
            x_sent[m].append(copy(r2.at[m, lax.rem(a, 2)], r2.at[m, 2 + x], device))
    second_sent = [[], []]
    for m in streams:
        for c in x_sent[m]:
            c.wait_recv()
        total = r2[m, 2]
        for a in range(1, nx):
            total = total + r2[m, 2 + a]
        r3[m, p2] = total
        for d in FAR:
            _, device = second_peer(d)
            second_sent[m].append(copy(r3.at[m, p2], r3.at[m, p2], device))
    edge += send_edges(slice(0, 2))
    unit = pl.ds(pl.multiple_of(p1 * thick + parity * 8, 8), 8)
    back_sent = []
    partner = ((x + 1 - 2 * parity) * nz + z, col)
    for m in streams:
        for c in second_sent[m]:
            c.wait_recv()
        total = r3[m, 0]
        for a in range(1, n1):
            total = total + r3[m, a]
        fresh[high + m, :, unit] = modes[high + m, :, unit] + total[:2] / (total[2:] + RELAX)
        here = fresh.at[high + m, :, unit]
        back_sent.append(copy(here, here, partner))
    gather = []
    for m in streams:
        back_sent[m].wait_recv()
        here = fresh.at[high + m, :, mine]
        to_peers = {}
        for d in FAR:
            _, device = first_peer(d)
            to_peers[d] = copy(here, here, device)
        gather.append(to_peers)
    here = fresh.at[high + 1, :, mine]
    pair = [copy(here, here, sibling)]

    for c in edge:
        c.wait_recv()
    west = unpack_low(ors[1] * ok(0, -1))
    east = unpack_high(ors[0] * ok(0, 1))
    for part, inner, vertical, lo, up in (
        (slice(0, 64), slice(64, 128), orv[1] * ok(-1, 0), orc[3] * ok(-1, -1), orc[2] * ok(-1, 1)),
        (slice(64, 128), slice(128, 192), orv[0] * ok(1, 0), orc[1] * ok(1, -1), orc[0] * ok(1, 1)),
    ):
        side = jnp.where(lanes_iota((3, 64, n)) < 64, west[:, part] + unpack_low(lo), east[:, part] + unpack_high(up))
        both_sums = centre(slice(0, 3), inner) + vertical + side
        new_object[:, part] = obj[:, part] + both_sums[:2] / (both_sums[2:] + RELAX)

    for d in NEAR:
        gather[0][d].wait_recv()
    pair.append(copy(fresh.at[high], fresh.at[high], sibling))
    for d in NEAR:
        gather[1][d].wait_recv()
        here = fresh.at[high + 1, :, chunk(lax.rem(p1 + n1 - d, n1))]
        pair.append(copy(here, here, sibling))
    for c in pair:
        c.wait_recv()

    for c in pending + pair_out:
        c.wait_send()


def finish_kernel(object_in, fresh, object_out, modes_out, made, sem):
    first = pltpu.make_async_copy(object_in, object_out, sem.at[0])
    first.start()
    copies = [first]
    scale = 1.0 / (fresh.shape[2] * fresh.shape[3])

    def mean(v):
        return jnp.sum(jnp.sum(v, 0, keepdims=True), 1, keepdims=True) * scale

    basis = []
    coefs = {}
    for k in range(4):
        vr, vi = fresh[k, 0], fresh[k, 1]
        for j in range(k):
            cr, ci = coefs[j, k]
            br, bi = basis[j]
            vr = vr - (cr * br - ci * bi)
            vi = vi - (cr * bi + ci * br)
        norm = 1.0 / jnp.sqrt(mean(vr * vr + vi * vi) + EPSILON)
        qr, qi = vr * norm, vi * norm
        basis.append((qr, qi))
        made[k, 0] = qr
        made[k, 1] = qi
        write = pltpu.make_async_copy(made.at[k], modes_out.at[k], sem.at[k + 1])
        write.start()
        copies.append(write)
        for later in range(k + 1, 4):
            fr, fi = fresh[later, 0], fresh[later, 1]
            coefs[k, later] = (mean(qr * fr + qi * fi), mean(qr * fi - qi * fr))
    for c in copies:
        c.wait()


def solution(mesh):
    rows, cols = mesh.shape["row"], mesh.shape["col"]
    nx = 4
    n1 = cols // 2
    f32, bf16, i32 = jnp.float32, jnp.bfloat16, jnp.int32

    def body(object_field, amplitudes, counts, offsets, mode_index, mix_table, probe_modes):
        cap, mixes = amplitudes.shape[2], mix_table.shape[0]
        number = 24 + 6 * (n1 - 1) + 2 * (nx - 1) + 2 + n1 + 1
        new_object, fresh = pl.pallas_call(
            functools.partial(kernel, rows, cols, nx, n1, cap, mixes),
            out_shape=(
                pltpu.VMEM((2, 128, 128), f32),
                pltpu.VMEM((4, 2, 128, 128), f32),
            ),
            in_specs=[HBM] * 8,
            out_specs=(VMEM, VMEM),
            scratch_shapes=[
                pltpu.VMEM((2, 128, 128), f32),
                pltpu.VMEM(amplitudes.shape, bf16),
                pltpu.SMEM((1, 1), i32),
                pltpu.SMEM((1, 1, 2, cap), i32),
                pltpu.SMEM((1, 1, cap), i32),
                pltpu.SMEM((4, mixes), f32),
                pltpu.VMEM((4, 2, 128, 128), f32),
                pltpu.VMEM((2, 256, 256), bf16),
                pltpu.VMEM((2, 2, 64, 128), f32),
                pltpu.VMEM((4, 2, 32, 128), f32),
                pltpu.VMEM((2, 2, 64, 128), f32),
                pltpu.VMEM((2, 2, 64, 128), f32),
                pltpu.VMEM((4, 2, 32, 128), f32),
                pltpu.VMEM((2, 2, 256, 128), f32),
                pltpu.VMEM((cap, 2, 128, 128), f32),
                pltpu.VMEM((cap, 2, 128, 128), f32),
                pltpu.VMEM((cap, 2, 128, 128), f32),
                pltpu.VMEM((cap, 128, 256), bf16),
                pltpu.VMEM((cap, 2, 128, 128), f32),
                pltpu.VMEM((4, 3, 128, 128), f32),
                pltpu.VMEM((GROUP, 3, 384, 128), f32),
                pltpu.VMEM((3, 2, 256, 128), f32),
                pltpu.VMEM((2, 3, 64, 128), f32),
                pltpu.VMEM((2, 3, 64, 128), f32),
                pltpu.VMEM((4, 3, 32, 128), f32),
                pltpu.VMEM((2, 3, 64, 128), f32),
                pltpu.VMEM((2, 3, 64, 128), f32),
                pltpu.VMEM((4, 3, 32, 128), f32),
                pltpu.VMEM((2, 3, 128, 128), f32),
                pltpu.VMEM((2, 3, 128, 128), f32),
                pltpu.VMEM((2, n1 - 1, 3, 128 // n1, 128), f32),
                pltpu.VMEM((2, 2 + nx, 3, 8, 128), f32),
                pltpu.VMEM((2, n1, 3, 8, 128), f32),
                pltpu.SemaphoreType.DMA((8,)),
                pltpu.SemaphoreType.DMA((number,)),
                pltpu.SemaphoreType.DMA((number,)),
                pltpu.SemaphoreType.DMA((n1,)),
                pltpu.SemaphoreType.DMA((n1,)),
            ],
            compiler_params=pltpu.CompilerParams(
                collective_id=0, has_side_effects=True, vmem_limit_bytes=56 * 1024 * 1024
            ),
            name="update",
        )(
            object_field, amplitudes, counts, jnp.swapaxes(offsets, 2, 3), mode_index, mix_table.T,
            probe_modes, jnp.asarray(tables(128)),
        )
        return pl.pallas_call(
            finish_kernel,
            out_shape=(
                jax.ShapeDtypeStruct((2, 128, 128), f32),
                jax.ShapeDtypeStruct((4, 2, 128, 128), f32),
            ),
            in_specs=[VMEM, VMEM],
            out_specs=(HBM, HBM),
            scratch_shapes=[pltpu.VMEM((4, 2, 128, 128), f32), pltpu.SemaphoreType.DMA((5,))],
            compiler_params=pltpu.CompilerParams(vmem_limit_bytes=8 * 1024 * 1024),
            name="finish",
        )(new_object, fresh)

    return jax.shard_map(
        body,
        mesh=mesh,
        in_specs=(
            P(None, "row", "col"),
            P("row", "col", None, None, None),
            P("row", "col"),
            P("row", "col", None, None),
            P("row", "col", None),
            P(),
            P(),
        ),
        out_specs=(P(None, "row", "col"), P()),
        check_vma=False,
    )
```

```python
import functools

import jax
import jax.numpy as jnp
import ml_dtypes
import numpy as np
from jax import lax
from jax.experimental import pallas as pl
from jax.experimental.pallas import tpu as pltpu
from jax.sharding import PartitionSpec as P

FLOOR = 0.25
RELAX = 0.5
EPSILON = 1e-06
GROUP = 2
TEAM = 12
FAR = (4, 3, 5, 2, 6, 1, 7)
NEAR = (1, 7, 2, 6, 3, 5, 4)
MESH = pl.DeviceIdType.MESH
VMEM = pl.BlockSpec(memory_space=pltpu.VMEM)
HBM = pl.BlockSpec(memory_space=pltpu.HBM)


def tables(size):
    index = np.arange(size)
    angle = (index[:, None] * index[None, :] % size).astype(np.float32) * np.float32(2.0 * np.pi / size)
    factor = np.float32(1.0 / np.sqrt(size))
    c = (np.cos(angle) * factor).astype(ml_dtypes.bfloat16)
    s = (np.sin(angle) * factor).astype(ml_dtypes.bfloat16)
    p = np.concatenate([np.concatenate([c, s], 1), np.concatenate([-s, c], 1)], 0)
    q = np.concatenate([np.concatenate([c, -s], 1), np.concatenate([s, c], 1)], 0)
    return np.stack([p, q])


def lanes_iota(shape):
    return lax.broadcasted_iota(jnp.int32, shape, len(shape) - 1)


def pack_low(x):
    n = x.shape[1] // 2
    a, b = x[:, :n], x[:, n:]
    return jnp.where(lanes_iota(a.shape) < 64, a, pltpu.roll(b, 64, 2))


def pack_high(x):
    n = x.shape[1] // 2
    a, b = x[:, :n], x[:, n:]
    return jnp.where(lanes_iota(a.shape) < 64, pltpu.roll(a, 64, 2), b)


def unpack_low(x):
    return jnp.concatenate([x, pltpu.roll(x, 64, 2)], 1)


def unpack_high(x):
    return jnp.concatenate([pltpu.roll(x, 64, 2), x], 1)


def place(rows, cols):
    row, col = lax.axis_index("row"), lax.axis_index("col")
    around = {}
    for dr in (-1, 0, 1):
        for dc in (-1, 0, 1):
            if dr or dc:
                around[dr, dc] = (lax.rem(row + dr + rows, rows), lax.rem(col + dc + cols, cols))
    return row, col, around


def inside(row, col, rows, cols, dr, dc):
    ok = jnp.float32(1.0)
    if dr == -1:
        ok = ok * (row > 0).astype(jnp.float32)
    if dr == 1:
        ok = ok * (row < rows - 1).astype(jnp.float32)
    if dc == -1:
        ok = ok * (col > 0).astype(jnp.float32)
    if dc == 1:
        ok = ok * (col < cols - 1).astype(jnp.float32)
    return ok


SIDES = [(-1, 0), (1, 0), (0, -1), (0, 1), (-1, -1), (-1, 1), (1, -1), (1, 1)]


def kernel(
    rows, cols, nx, n1, cap, mixes,
    o_hbm, a_hbm, counts_hbm, offs_hbm, index_hbm, mix_hbm, modes_hbm, tab_hbm,
    new_object, fresh,
    obj, amps, counts, offs, index, mix, modes, tab,
    ps, pc, rv, rs, rc, tiles, probes, patches, deltas, splats, sums, pad, marg,
    on, op, oc, orv, ors, orc, got, half, r1, r2, r3,
    load, send, recv, pair_send, pair_recv,
):
    n = 128
    nz = rows // nx
    row, col, around = place(rows, cols)
    x, z = row // nz, lax.rem(row, nz)
    y, core = col // 2, lax.rem(col, 2)
    p1 = z + core * (y - z)
    p2 = y + core * (z - y)
    sibling = (row, col + 1 - 2 * core)
    high = 2 * core
    other = 2 - high

    def first_peer(d):
        a = lax.rem(p1 + d, n1)
        return a, (x * nz + z + (1 - core) * (a - z), (y + core * (a - y)) * 2 + core)

    def second_peer(d):
        a = lax.rem(p2 + d, n1)
        return a, (x * nz + z + core * (a - z), (y + (1 - core) * (a - y)) * 2 + core)

    def x_peer(d):
        a = lax.rem(x + d, nx)
        return a, (a * nz + z, col)

    used = [0]
    pending = []

    def copy(src, dst, device):
        i = used[0]
        used[0] += 1
        made = pltpu.make_async_remote_copy(
            src_ref=src, dst_ref=dst, send_sem=send.at[i], recv_sem=recv.at[i],
            device_id=device, device_id_type=MESH,
        )
        made.start()
        pending.append(made)
        return made

    def ok(dr, dc):
        return inside(row, col, rows, cols, dr, dc)

    barrier = pltpu.get_barrier_semaphore()
    partners = (
        [around[s] for s in SIDES]
        + [sibling]
        + [first_peer(d)[1] for d in range(1, n1)]
        + [second_peer(d)[1] for d in range(1, n1)]
        + [x_peer(d)[1] for d in range(1, nx)]
    )
    for device in partners:
        pl.semaphore_signal(barrier, inc=1, device_id=device, device_id_type=MESH)
    loads = [
        pltpu.make_async_copy(src, dst, load.at[i])
        for i, (src, dst) in enumerate(
            (
                (o_hbm, obj), (modes_hbm, modes), (mix_hbm, mix), (index_hbm, index), (counts_hbm, counts),
                (offs_hbm, offs), (tab_hbm, tab), (a_hbm, amps),
            )
        )
    ]
    for c in loads:
        c.start()

    loads[0].wait()
    ps[0] = pack_low(obj[...])
    ps[1] = pack_high(obj[...])
    pc[0] = pack_low(obj[:, :64])
    pc[1] = pack_high(obj[:, :64])
    pc[2] = pack_low(obj[:, 64:])
    pc[3] = pack_high(obj[:, 64:])
    pl.semaphore_wait(barrier, len(partners))
    halo = [
        copy(pc.at[0], rc.at[0], around[-1, -1]),
        copy(pc.at[1], rc.at[1], around[-1, 1]),
        copy(pc.at[2], rc.at[2], around[1, -1]),
        copy(pc.at[3], rc.at[3], around[1, 1]),
        copy(obj.at[:, 0:64], rv.at[0], around[-1, 0]),
        copy(obj.at[:, 64:128], rv.at[1], around[1, 0]),
        copy(ps.at[0], rs.at[0], around[0, -1]),
        copy(ps.at[1], rs.at[1], around[0, 1]),
    ]

    for c in loads[1:]:
        c.wait()
    marg[...] = jnp.zeros_like(marg)
    pad[...] = jnp.zeros_like(pad)
    count = counts[0, 0]

    def spot(slot):
        top = jnp.clip(offs[0, 0, 0, slot], 0, n - 1)
        left_px = jnp.clip(offs[0, 0, 1, slot], 0, n - 1)
        return top, left_px

    def weights_of(slot):
        pick = jnp.clip(index[0, 0, slot], 0, mixes - 1)
        return [jnp.where(slot < count, mix[k, pick], 0.0) for k in range(4)]

    def spread(frames, spots):
        for f in frames:
            for h in range(4):
                part = slice(h * 64, (h + 1) * 64)
                low, up = marg[f, 0, part], marg[f, 1, part]
                for i, (top, left_px) in enumerate(spots):
                    value = pad[i, f, pl.ds(n - top + h * 64, 64), :]
                    mask = lanes_iota((64, n)) >= left_px
                    low = low + jnp.where(mask, value, 0.0)
                    up = up + jnp.where(mask, 0.0, value)
                marg[f, 0, part] = low
                marg[f, 1, part] = up

    def centre(frames, part):
        own, end = marg[frames, 0, part], marg[frames, 1, part]
        return jnp.where(lanes_iota(own.shape) < 64, pltpu.roll(own, 64, 2), pltpu.roll(end, 64, 2))

    def send_edges(frames):
        top, middle, bottom = slice(0, 64), slice(64, 192), slice(192, 256)
        on[0, frames] = centre(frames, top)
        on[1, frames] = centre(frames, bottom)
        op[0, frames] = pack_low(marg[frames, 0, middle])
        op[1, frames] = pack_high(marg[frames, 1, middle])
        oc[0, frames] = pack_low(marg[frames, 0, top])
        oc[1, frames] = pack_high(marg[frames, 1, top])
        oc[2, frames] = pack_low(marg[frames, 0, bottom])
        oc[3, frames] = pack_high(marg[frames, 1, bottom])
        return [
            copy(oc.at[0, frames], orc.at[0, frames], around[-1, -1]),
            copy(oc.at[1, frames], orc.at[1, frames], around[-1, 1]),
            copy(oc.at[2, frames], orc.at[2, frames], around[1, -1]),
            copy(oc.at[3, frames], orc.at[3, frames], around[1, 1]),
            copy(on.at[0, frames], orv.at[0, frames], around[-1, 0]),
            copy(on.at[1, frames], orv.at[1, frames], around[1, 0]),
            copy(op.at[0, frames], ors.at[0, frames], around[0, -1]),
            copy(op.at[1, frames], ors.at[1, frames], around[0, 1]),
        ]

    def make_probes(step, carry):
        slots = [step * GROUP + i for i in range(GROUP)]
        spots = [spot(slot) for slot in slots]
        for i, slot in enumerate(slots):
            w = weights_of(slot)
            for k in range(4):
                splats[slot, k : k + 1] = jnp.broadcast_to(w[k], (1, n))
                splats[slot, 4 + k : 5 + k] = jnp.broadcast_to(w[k] * w[k], (1, n))
            probe = []
            for comp in range(2):
                total = w[0] * modes[0, comp]
                for k in range(1, 4):
                    total = total + w[k] * modes[k, comp]
                probes[slot, comp] = total
                probe.append(total)
            value = probe[0] * probe[0] + probe[1] * probe[1]
            pad[i, 2, n : 2 * n] = pltpu.roll(value, spots[i][1], 1)
        spread((2,), spots)
        return carry

    lax.fori_loop(0, cap // GROUP, make_probes, 0)
    edge = send_edges(slice(2, 3))
    for c in halo:
        c.wait_recv()

    def tile_rows(target, west, own, east):
        turned = pltpu.roll(own, 64, 2)
        low = lanes_iota(own.shape) < 64
        tiles[:, 0, target] = jnp.where(low, west, turned)
        tiles[:, 1, target] = jnp.where(low, turned, east)

    tile_rows(
        slice(0, 64), unpack_low(rc[3] * ok(-1, -1)), rv[1] * ok(-1, 0), unpack_high(rc[2] * ok(-1, 1))
    )
    tile_rows(slice(64, 192), unpack_low(rs[1] * ok(0, -1)), obj[...], unpack_high(rs[0] * ok(0, 1)))
    tile_rows(
        slice(192, 256), unpack_low(rc[1] * ok(1, -1)), rv[0] * ok(1, 0), unpack_high(rc[0] * ok(1, 1))
    )

    fwd, inv = tab[0], tab[1]

    def dot(a, b):
        return jnp.dot(a, b, preferred_element_type=jnp.float32)

    def left(table, res, ims):
        out = dot(table, jnp.concatenate([jnp.concatenate(res, 1), jnp.concatenate(ims, 1)], 0))
        return (
            [out[:n, i * n : (i + 1) * n] for i in range(len(res))],
            [out[n:, i * n : (i + 1) * n] for i in range(len(res))],
        )

    def right(table, res, ims):
        out = dot(jnp.concatenate([jnp.concatenate([a, b], 1) for a, b in zip(res, ims)], 0), table)
        return (
            [out[i * n : (i + 1) * n, :n] for i in range(len(res))],
            [out[i * n : (i + 1) * n, n:] for i in range(len(res))],
        )

    def lower(xs):
        return [v.astype(jnp.bfloat16) for v in xs]

    lane = lanes_iota((n, n))

    def visit(step, carry):
        slots = [step * TEAM + i for i in range(TEAM)]
        psi_r, psi_i = [], []
        for slot in slots:
            top, left_px = spot(slot)
            mask = lane >= left_px
            patch = []
            for comp in range(2):
                a = tiles[comp, 0, pl.ds(top, n), :]
                b = tiles[comp, 1, pl.ds(top, n), :]
                patch.append(pltpu.roll(jnp.where(mask, a, b), lax.rem(n - left_px, n), 1))
                patches[slot, comp] = patch[comp]
            pr, pi = probes[slot, 0], probes[slot, 1]
            real = pr * patch[0] - pi * patch[1]
            imag = pr * patch[1] + pi * patch[0]
            psi_r.append(real)
            psi_i.append(imag)
        re, im = left(fwd, lower(psi_r), lower(psi_i))
        re, im = right(inv, lower(re), lower(im))
        fixed_re, fixed_im = [], []
        for slot, a, b in zip(slots, re, im):
            ratio = amps[0, 0, slot].astype(jnp.float32) * lax.rsqrt(jnp.maximum(a * a + b * b, FLOOR * FLOOR))
            fixed_re.append((a * ratio).astype(jnp.bfloat16))
            fixed_im.append((b * ratio).astype(jnp.bfloat16))
        re, im = left(inv, fixed_re, fixed_im)
        re, im = right(fwd, lower(re), lower(im))
        for i, slot in enumerate(slots):
            deltas[slot, 0] = re[i] - psi_r[i]
            deltas[slot, 1] = im[i] - psi_i[i]
        return carry

    lax.fori_loop(0, cap // TEAM, visit, 0)

    thick = n // n1

    def chunk(a):
        return pl.ds(pl.multiple_of(a * thick, thick), thick)

    def pair_copy(i, d):
        piece = chunk(lax.rem(p2 + d, n1))
        return pltpu.make_async_remote_copy(
            src_ref=sums.at[pl.ds(other, 2), :, piece], dst_ref=got.at[:, :, piece],
            send_sem=pair_send.at[i], recv_sem=pair_recv.at[i], device_id=sibling, device_id_type=MESH,
        )

    def finish_rows(i, carry):
        d = n1 // 2 + (1 - 2 * lax.rem(i, 2)) * ((i + 1) // 2)
        rows_here = chunk(lax.rem(p2 + d, n1))
        totals = [[jnp.zeros((thick, n), jnp.float32) for _ in range(3)] for _ in range(4)]
        for slot in range(cap):
            dr, di = deltas[slot, 0, rows_here], deltas[slot, 1, rows_here]
            ar, ai = patches[slot, 0, rows_here], patches[slot, 1, rows_here]
            pieces = (ar * dr + ai * di, ar * di - ai * dr, ar * ar + ai * ai)
            for k in range(4):
                w, square = splats[slot, k : k + 1], splats[slot, 4 + k : 5 + k]
                totals[k][0] = totals[k][0] + w * pieces[0]
                totals[k][1] = totals[k][1] + w * pieces[1]
                totals[k][2] = totals[k][2] + square * pieces[2]
        for k in range(4):
            for f in range(3):
                sums[k, f, rows_here] = totals[k][f]
        pair_copy(i, d).start()
        return carry

    lax.fori_loop(0, n1, finish_rows, 0)
    order = FAR + (0,)
    pair_out = [pair_copy(i, d) for i, d in enumerate(order)]
    streams = (0, 1)
    sent = [[], []]

    def send_first(m, d):
        a, device = first_peer(d)
        sent[m].append(copy(half.at[m, :, chunk(a)], r1.at[m, d - 1], device))

    for d, c in zip(order, pair_out):
        c.wait_recv()
        a, _ = first_peer(d)
        half[:, :, chunk(a)] = sums[pl.ds(high, 2), :, chunk(a)] + got[:, :, chunk(a)]
        if d:
            send_first(0, d)
    for d in FAR:
        send_first(1, d)

    def numerators(step, carry):
        slots = [step * GROUP + i for i in range(GROUP)]
        spots = [spot(slot) for slot in slots]
        for i, slot in enumerate(slots):
            pr, pi = probes[slot, 0], probes[slot, 1]
            dr, di = deltas[slot, 0], deltas[slot, 1]
            for f, value in enumerate((pr * dr + pi * di, pr * di - pi * dr)):
                pad[i, f, n : 2 * n] = pltpu.roll(value, spots[i][1], 1)
        spread((0, 1), spots)
        return carry

    lax.fori_loop(0, cap // GROUP, numerators, 0)

    mine = chunk(p1)
    parity = lax.rem(x, 2)
    x_sent = [[], []]
    for m in streams:
        total = half[m, :, mine]
        for d, c in zip(FAR[::-1], sent[m][::-1]):
            c.wait_recv()
            total = total + r1[m, d - 1]
        for t in range(2):
            r2[m, t] = total[:, t * 8 : (t + 1) * 8]
        r2[m, 2 + x] = r2[m, parity]
        for d in range(1, nx):
            a, device = x_peer(d)
            x_sent[m].append(copy(r2.at[m, lax.rem(a, 2)], r2.at[m, 2 + x], device))
    second_sent = [[], []]
    for m in streams:
        for c in x_sent[m]:
            c.wait_recv()
        total = r2[m, 2]
        for a in range(1, nx):
            total = total + r2[m, 2 + a]
        r3[m, p2] = total
        for d in FAR:
            _, device = second_peer(d)
            second_sent[m].append(copy(r3.at[m, p2], r3.at[m, p2], device))
    edge += send_edges(slice(0, 2))
    unit = pl.ds(pl.multiple_of(p1 * thick + parity * 8, 8), 8)
    back_sent = []
    partner = ((x + 1 - 2 * parity) * nz + z, col)
    for m in streams:
        for c in second_sent[m]:
            c.wait_recv()
        total = r3[m, 0]
        for a in range(1, n1):
            total = total + r3[m, a]
        fresh[high + m, :, unit] = modes[high + m, :, unit] + total[:2] / (total[2:] + RELAX)
        here = fresh.at[high + m, :, unit]
        back_sent.append(copy(here, here, partner))
    gather = []
    for m in streams:
        back_sent[m].wait_recv()
        here = fresh.at[high + m, :, mine]
        to_peers = {}
        for d in FAR:
            _, device = first_peer(d)
            to_peers[d] = copy(here, here, device)
        gather.append(to_peers)
    here = fresh.at[high + 1, :, mine]
    pair = [copy(here, here, sibling)]

    for c in edge:
        c.wait_recv()
    west = unpack_low(ors[1] * ok(0, -1))
    east = unpack_high(ors[0] * ok(0, 1))
    for part, inner, vertical, lo, up in (
        (slice(0, 64), slice(64, 128), orv[1] * ok(-1, 0), orc[3] * ok(-1, -1), orc[2] * ok(-1, 1)),
        (slice(64, 128), slice(128, 192), orv[0] * ok(1, 0), orc[1] * ok(1, -1), orc[0] * ok(1, 1)),
    ):
        side = jnp.where(lanes_iota((3, 64, n)) < 64, west[:, part] + unpack_low(lo), east[:, part] + unpack_high(up))
        both_sums = centre(slice(0, 3), inner) + vertical + side
        new_object[:, part] = obj[:, part] + both_sums[:2] / (both_sums[2:] + RELAX)

    for d in NEAR:
        gather[0][d].wait_recv()
    pair.append(copy(fresh.at[high], fresh.at[high], sibling))
    for d in NEAR:
        gather[1][d].wait_recv()
        here = fresh.at[high + 1, :, chunk(lax.rem(p1 + n1 - d, n1))]
        pair.append(copy(here, here, sibling))
    for c in pair:
        c.wait_recv()

    for c in pending + pair_out:
        c.wait_send()


def finish_kernel(object_in, fresh, object_out, modes_out, made, sem):
    first = pltpu.make_async_copy(object_in, object_out, sem.at[0])
    first.start()
    copies = [first]
    scale = 1.0 / (fresh.shape[2] * fresh.shape[3])

    def mean(v):
        return jnp.sum(jnp.sum(v, 0, keepdims=True), 1, keepdims=True) * scale

    basis = []
    coefs = {}
    for k in range(4):
        vr, vi = fresh[k, 0], fresh[k, 1]
        for j in range(k):
            cr, ci = coefs[j, k]
            br, bi = basis[j]
            vr = vr - (cr * br - ci * bi)
            vi = vi - (cr * bi + ci * br)
        norm = 1.0 / jnp.sqrt(mean(vr * vr + vi * vi) + EPSILON)
        qr, qi = vr * norm, vi * norm
        basis.append((qr, qi))
        made[k, 0] = qr
        made[k, 1] = qi
        write = pltpu.make_async_copy(made.at[k], modes_out.at[k], sem.at[k + 1])
        write.start()
        copies.append(write)
        for later in range(k + 1, 4):
            fr, fi = fresh[later, 0], fresh[later, 1]
            coefs[k, later] = (mean(qr * fr + qi * fi), mean(qr * fi - qi * fr))
    for c in copies:
        c.wait()


def solution(mesh):
    rows, cols = mesh.shape["row"], mesh.shape["col"]
    nx = 4
    n1 = cols // 2
    f32, bf16, i32 = jnp.float32, jnp.bfloat16, jnp.int32

    def body(object_field, amplitudes, counts, offsets, mode_index, mix_table, probe_modes):
        cap, mixes = amplitudes.shape[2], mix_table.shape[0]
        number = 24 + 6 * (n1 - 1) + 2 * (nx - 1) + 2 + n1 + 1
        new_object, fresh = pl.pallas_call(
            functools.partial(kernel, rows, cols, nx, n1, cap, mixes),
            out_shape=(
                pltpu.VMEM((2, 128, 128), f32),
                pltpu.VMEM((4, 2, 128, 128), f32),
            ),
            in_specs=[HBM] * 8,
            out_specs=(VMEM, VMEM),
            scratch_shapes=[
                pltpu.VMEM((2, 128, 128), f32),
                pltpu.VMEM(amplitudes.shape, bf16),
                pltpu.SMEM((1, 1), i32),
                pltpu.SMEM((1, 1, 2, cap), i32),
                pltpu.SMEM((1, 1, cap), i32),
                pltpu.SMEM((4, mixes), f32),
                pltpu.VMEM((4, 2, 128, 128), f32),
                pltpu.VMEM((2, 256, 256), bf16),
                pltpu.VMEM((2, 2, 64, 128), f32),
                pltpu.VMEM((4, 2, 32, 128), f32),
                pltpu.VMEM((2, 2, 64, 128), f32),
                pltpu.VMEM((2, 2, 64, 128), f32),
                pltpu.VMEM((4, 2, 32, 128), f32),
                pltpu.VMEM((2, 2, 256, 128), f32),
                pltpu.VMEM((cap, 2, 128, 128), f32),
                pltpu.VMEM((cap, 2, 128, 128), f32),
                pltpu.VMEM((cap, 2, 128, 128), f32),
                pltpu.VMEM((cap, 8, 128), f32),
                pltpu.VMEM((4, 3, 128, 128), f32),
                pltpu.VMEM((GROUP, 3, 384, 128), f32),
                pltpu.VMEM((3, 2, 256, 128), f32),
                pltpu.VMEM((2, 3, 64, 128), f32),
                pltpu.VMEM((2, 3, 64, 128), f32),
                pltpu.VMEM((4, 3, 32, 128), f32),
                pltpu.VMEM((2, 3, 64, 128), f32),
                pltpu.VMEM((2, 3, 64, 128), f32),
                pltpu.VMEM((4, 3, 32, 128), f32),
                pltpu.VMEM((2, 3, 128, 128), f32),
                pltpu.VMEM((2, 3, 128, 128), f32),
                pltpu.VMEM((2, n1 - 1, 3, 128 // n1, 128), f32),
                pltpu.VMEM((2, 2 + nx, 3, 8, 128), f32),
                pltpu.VMEM((2, n1, 3, 8, 128), f32),
                pltpu.SemaphoreType.DMA((8,)),
                pltpu.SemaphoreType.DMA((number,)),
                pltpu.SemaphoreType.DMA((number,)),
                pltpu.SemaphoreType.DMA((n1,)),
                pltpu.SemaphoreType.DMA((n1,)),
            ],
            compiler_params=pltpu.CompilerParams(
                collective_id=0, has_side_effects=True, vmem_limit_bytes=56 * 1024 * 1024
            ),
            name="update",
        )(
            object_field, amplitudes, counts, jnp.swapaxes(offsets, 2, 3), mode_index, mix_table.T,
            probe_modes, jnp.asarray(tables(128)),
        )
        return pl.pallas_call(
            finish_kernel,
            out_shape=(
                jax.ShapeDtypeStruct((2, 128, 128), f32),
                jax.ShapeDtypeStruct((4, 2, 128, 128), f32),
            ),
            in_specs=[VMEM, VMEM],
            out_specs=(HBM, HBM),
            scratch_shapes=[pltpu.VMEM((4, 2, 128, 128), f32), pltpu.SemaphoreType.DMA((5,))],
            compiler_params=pltpu.CompilerParams(vmem_limit_bytes=8 * 1024 * 1024),
            name="finish",
        )(new_object, fresh)

    return jax.shard_map(
        body,
        mesh=mesh,
        in_specs=(
            P(None, "row", "col"),
            P("row", "col", None, None, None),
            P("row", "col"),
            P("row", "col", None, None),
            P("row", "col", None),
            P(),
            P(),
        ),
        out_specs=(P(None, "row", "col"), P()),
        check_vma=False,
    )
```

```python
import functools

import jax
import jax.numpy as jnp
import ml_dtypes
import numpy as np
from jax import lax
from jax.experimental import pallas as pl
from jax.experimental.pallas import tpu as pltpu
from jax.sharding import PartitionSpec as P

FLOOR = 0.25
RELAX = 0.5
EPSILON = 1e-06
GROUP = 2
TEAM = 12
FAR = (4, 3, 5, 2, 6, 1, 7)
NEAR = (1, 7, 2, 6, 3, 5, 4)
MESH = pl.DeviceIdType.MESH
VMEM = pl.BlockSpec(memory_space=pltpu.VMEM)
HBM = pl.BlockSpec(memory_space=pltpu.HBM)


def tables(size):
    index = np.arange(size)
    angle = (index[:, None] * index[None, :] % size).astype(np.float32) * np.float32(2.0 * np.pi / size)
    factor = np.float32(1.0 / np.sqrt(size))
    c = (np.cos(angle) * factor).astype(ml_dtypes.bfloat16)
    s = (np.sin(angle) * factor).astype(ml_dtypes.bfloat16)
    p = np.concatenate([np.concatenate([c, s], 1), np.concatenate([-s, c], 1)], 0)
    q = np.concatenate([np.concatenate([c, -s], 1), np.concatenate([s, c], 1)], 0)
    return np.stack([p, q])


def lanes_iota(shape):
    return lax.broadcasted_iota(jnp.int32, shape, len(shape) - 1)


def pack_low(x):
    n = x.shape[1] // 2
    a, b = x[:, :n], x[:, n:]
    return jnp.where(lanes_iota(a.shape) < 64, a, pltpu.roll(b, 64, 2))


def pack_high(x):
    n = x.shape[1] // 2
    a, b = x[:, :n], x[:, n:]
    return jnp.where(lanes_iota(a.shape) < 64, pltpu.roll(a, 64, 2), b)


def unpack_low(x):
    return jnp.concatenate([x, pltpu.roll(x, 64, 2)], 1)


def unpack_high(x):
    return jnp.concatenate([pltpu.roll(x, 64, 2), x], 1)


def place(rows, cols):
    row, col = lax.axis_index("row"), lax.axis_index("col")
    around = {}
    for dr in (-1, 0, 1):
        for dc in (-1, 0, 1):
            if dr or dc:
                around[dr, dc] = (lax.rem(row + dr + rows, rows), lax.rem(col + dc + cols, cols))
    return row, col, around


def inside(row, col, rows, cols, dr, dc):
    ok = jnp.float32(1.0)
    if dr == -1:
        ok = ok * (row > 0).astype(jnp.float32)
    if dr == 1:
        ok = ok * (row < rows - 1).astype(jnp.float32)
    if dc == -1:
        ok = ok * (col > 0).astype(jnp.float32)
    if dc == 1:
        ok = ok * (col < cols - 1).astype(jnp.float32)
    return ok


SIDES = [(-1, 0), (1, 0), (0, -1), (0, 1), (-1, -1), (-1, 1), (1, -1), (1, 1)]


def kernel(
    rows, cols, nx, n1, cap, mixes,
    o_hbm, a_hbm, counts_hbm, offs_hbm, index_hbm, mix_hbm, modes_hbm, tab_hbm,
    new_object, fresh,
    obj, amps, counts, offs, index, mix, modes, tab,
    ps, pc, rv, rs, rc, tiles, probes, patches, deltas, splats, sums, pad, marg,
    on, op, oc, orv, ors, orc, got, half, r1, r2, r3,
    load, send, recv, pair_send, pair_recv,
):
    n = 128
    nz = rows // nx
    row, col, around = place(rows, cols)
    x, z = row // nz, lax.rem(row, nz)
    y, core = col // 2, lax.rem(col, 2)
    p1 = z + core * (y - z)
    p2 = y + core * (z - y)
    sibling = (row, col + 1 - 2 * core)
    high = 2 * core
    other = 2 - high

    def first_peer(d):
        a = lax.rem(p1 + d, n1)
        return a, (x * nz + z + (1 - core) * (a - z), (y + core * (a - y)) * 2 + core)

    def second_peer(d):
        a = lax.rem(p2 + d, n1)
        return a, (x * nz + z + core * (a - z), (y + (1 - core) * (a - y)) * 2 + core)

    def x_peer(d):
        a = lax.rem(x + d, nx)
        return a, (a * nz + z, col)

    used = [0]
    pending = []

    def copy(src, dst, device):
        i = used[0]
        used[0] += 1
        made = pltpu.make_async_remote_copy(
            src_ref=src, dst_ref=dst, send_sem=send.at[i], recv_sem=recv.at[i],
            device_id=device, device_id_type=MESH,
        )
        made.start()
        pending.append(made)
        return made

    def flush(copies):
        for c in copies:
            c.wait_send()
        done = [id(c) for c in copies]
        pending[:] = [c for c in pending if id(c) not in done]

    def ok(dr, dc):
        return inside(row, col, rows, cols, dr, dc)

    barrier = pltpu.get_barrier_semaphore()
    partners = (
        [around[s] for s in SIDES]
        + [sibling]
        + [first_peer(d)[1] for d in range(1, n1)]
        + [second_peer(d)[1] for d in range(1, n1)]
        + [x_peer(d)[1] for d in range(1, nx)]
    )
    for device in partners:
        pl.semaphore_signal(barrier, inc=1, device_id=device, device_id_type=MESH)
    loads = [
        pltpu.make_async_copy(src, dst, load.at[i])
        for i, (src, dst) in enumerate(
            (
                (o_hbm, obj), (modes_hbm, modes), (mix_hbm, mix), (index_hbm, index), (counts_hbm, counts),
                (offs_hbm, offs), (tab_hbm, tab), (a_hbm, amps),
            )
        )
    ]
    for c in loads:
        c.start()

    loads[0].wait()
    ps[0] = pack_low(obj[...])
    ps[1] = pack_high(obj[...])
    pc[0] = pack_low(obj[:, :64])
    pc[1] = pack_high(obj[:, :64])
    pc[2] = pack_low(obj[:, 64:])
    pc[3] = pack_high(obj[:, 64:])
    pl.semaphore_wait(barrier, len(partners))
    halo = [
        copy(pc.at[0], rc.at[0], around[-1, -1]),
        copy(pc.at[1], rc.at[1], around[-1, 1]),
        copy(pc.at[2], rc.at[2], around[1, -1]),
        copy(pc.at[3], rc.at[3], around[1, 1]),
        copy(obj.at[:, 0:64], rv.at[0], around[-1, 0]),
        copy(obj.at[:, 64:128], rv.at[1], around[1, 0]),
        copy(ps.at[0], rs.at[0], around[0, -1]),
        copy(ps.at[1], rs.at[1], around[0, 1]),
    ]

    for c in loads[1:]:
        c.wait()
    marg[...] = jnp.zeros_like(marg)
    pad[...] = jnp.zeros_like(pad)
    count = counts[0, 0]

    def spot(slot):
        top = jnp.clip(offs[0, 0, 0, slot], 0, n - 1)
        left_px = jnp.clip(offs[0, 0, 1, slot], 0, n - 1)
        return top, left_px

    def weights_of(slot):
        pick = jnp.clip(index[0, 0, slot], 0, mixes - 1)
        return [jnp.where(slot < count, mix[k, pick], 0.0) for k in range(4)]

    def spread(frames, spots):
        for f in frames:
            for h in range(4):
                part = slice(h * 64, (h + 1) * 64)
                low, up = marg[f, 0, part], marg[f, 1, part]
                for i, (top, left_px) in enumerate(spots):
                    value = pad[i, f, pl.ds(n - top + h * 64, 64), :]
                    mask = lanes_iota((64, n)) >= left_px
                    low = low + jnp.where(mask, value, 0.0)
                    up = up + jnp.where(mask, 0.0, value)
                marg[f, 0, part] = low
                marg[f, 1, part] = up

    def centre(frames, part):
        own, end = marg[frames, 0, part], marg[frames, 1, part]
        return jnp.where(lanes_iota(own.shape) < 64, pltpu.roll(own, 64, 2), pltpu.roll(end, 64, 2))

    def send_edges(frames):
        top, middle, bottom = slice(0, 64), slice(64, 192), slice(192, 256)
        on[0, frames] = centre(frames, top)
        on[1, frames] = centre(frames, bottom)
        op[0, frames] = pack_low(marg[frames, 0, middle])
        op[1, frames] = pack_high(marg[frames, 1, middle])
        oc[0, frames] = pack_low(marg[frames, 0, top])
        oc[1, frames] = pack_high(marg[frames, 1, top])
        oc[2, frames] = pack_low(marg[frames, 0, bottom])
        oc[3, frames] = pack_high(marg[frames, 1, bottom])
        return [
            copy(oc.at[0, frames], orc.at[0, frames], around[-1, -1]),
            copy(oc.at[1, frames], orc.at[1, frames], around[-1, 1]),
            copy(oc.at[2, frames], orc.at[2, frames], around[1, -1]),
            copy(oc.at[3, frames], orc.at[3, frames], around[1, 1]),
            copy(on.at[0, frames], orv.at[0, frames], around[-1, 0]),
            copy(on.at[1, frames], orv.at[1, frames], around[1, 0]),
            copy(op.at[0, frames], ors.at[0, frames], around[0, -1]),
            copy(op.at[1, frames], ors.at[1, frames], around[0, 1]),
        ]

    def make_probes(step, carry):
        slots = [step * GROUP + i for i in range(GROUP)]
        spots = [spot(slot) for slot in slots]
        for i, slot in enumerate(slots):
            w = weights_of(slot)
            for k in range(4):
                splats[slot, k : k + 1] = jnp.broadcast_to(w[k], (1, n))
                splats[slot, 4 + k : 5 + k] = jnp.broadcast_to(w[k] * w[k], (1, n))
            probe = []
            for comp in range(2):
                total = w[0] * modes[0, comp]
                for k in range(1, 4):
                    total = total + w[k] * modes[k, comp]
                probes[slot, comp] = total
                probe.append(total)
            value = probe[0] * probe[0] + probe[1] * probe[1]
            pad[i, 2, n : 2 * n] = pltpu.roll(value, spots[i][1], 1)
        spread((2,), spots)
        return carry

    lax.fori_loop(0, cap // GROUP, make_probes, 0)
    edge = send_edges(slice(2, 3))
    for c in halo:
        c.wait_recv()

    def tile_rows(target, west, own, east):
        turned = pltpu.roll(own, 64, 2)
        low = lanes_iota(own.shape) < 64
        tiles[:, 0, target] = jnp.where(low, west, turned)
        tiles[:, 1, target] = jnp.where(low, turned, east)

    tile_rows(
        slice(0, 64), unpack_low(rc[3] * ok(-1, -1)), rv[1] * ok(-1, 0), unpack_high(rc[2] * ok(-1, 1))
    )
    tile_rows(slice(64, 192), unpack_low(rs[1] * ok(0, -1)), obj[...], unpack_high(rs[0] * ok(0, 1)))
    tile_rows(
        slice(192, 256), unpack_low(rc[1] * ok(1, -1)), rv[0] * ok(1, 0), unpack_high(rc[0] * ok(1, 1))
    )

    fwd, inv = tab[0], tab[1]

    def dot(a, b):
        return jnp.dot(a, b, preferred_element_type=jnp.float32)

    def left(table, res, ims):
        out = dot(table, jnp.concatenate([jnp.concatenate(res, 1), jnp.concatenate(ims, 1)], 0))
        return (
            [out[:n, i * n : (i + 1) * n] for i in range(len(res))],
            [out[n:, i * n : (i + 1) * n] for i in range(len(res))],
        )

    def right(table, res, ims):
        out = dot(jnp.concatenate([jnp.concatenate([a, b], 1) for a, b in zip(res, ims)], 0), table)
        return (
            [out[i * n : (i + 1) * n, :n] for i in range(len(res))],
            [out[i * n : (i + 1) * n, n:] for i in range(len(res))],
        )

    def lower(xs):
        return [v.astype(jnp.bfloat16) for v in xs]

    lane = lanes_iota((n, n))

    def visit(step, carry):
        slots = [step * TEAM + i for i in range(TEAM)]
        psi_r, psi_i = [], []
        for slot in slots:
            top, left_px = spot(slot)
            mask = lane >= left_px
            patch = []
            for comp in range(2):
                a = tiles[comp, 0, pl.ds(top, n), :]
                b = tiles[comp, 1, pl.ds(top, n), :]
                patch.append(pltpu.roll(jnp.where(mask, a, b), lax.rem(n - left_px, n), 1))
                patches[slot, comp] = patch[comp]
            pr, pi = probes[slot, 0], probes[slot, 1]
            real = pr * patch[0] - pi * patch[1]
            imag = pr * patch[1] + pi * patch[0]
            psi_r.append(real)
            psi_i.append(imag)
        re, im = left(fwd, lower(psi_r), lower(psi_i))
        re, im = right(inv, lower(re), lower(im))
        fixed_re, fixed_im = [], []
        for slot, a, b in zip(slots, re, im):
            ratio = amps[0, 0, slot].astype(jnp.float32) * lax.rsqrt(jnp.maximum(a * a + b * b, FLOOR * FLOOR))
            fixed_re.append((a * ratio).astype(jnp.bfloat16))
            fixed_im.append((b * ratio).astype(jnp.bfloat16))
        re, im = left(inv, fixed_re, fixed_im)
        re, im = right(fwd, lower(re), lower(im))
        for i, slot in enumerate(slots):
            deltas[slot, 0] = re[i] - psi_r[i]
            deltas[slot, 1] = im[i] - psi_i[i]
        return carry

    lax.fori_loop(0, cap // TEAM, visit, 0)

    thick = n // n1

    def chunk(a):
        return pl.ds(pl.multiple_of(a * thick, thick), thick)

    def pair_copy(i, d):
        piece = chunk(lax.rem(p2 + d, n1))
        return pltpu.make_async_remote_copy(
            src_ref=sums.at[pl.ds(other, 2), :, piece], dst_ref=got.at[:, :, piece],
            send_sem=pair_send.at[i], recv_sem=pair_recv.at[i], device_id=sibling, device_id_type=MESH,
        )

    def finish_rows(i, carry):
        d = n1 // 2 + (1 - 2 * lax.rem(i, 2)) * ((i + 1) // 2)
        rows_here = chunk(lax.rem(p2 + d, n1))
        totals = [[jnp.zeros((thick, n), jnp.float32) for _ in range(3)] for _ in range(4)]
        for slot in range(cap):
            dr, di = deltas[slot, 0, rows_here], deltas[slot, 1, rows_here]
            ar, ai = patches[slot, 0, rows_here], patches[slot, 1, rows_here]
            pieces = (ar * dr + ai * di, ar * di - ai * dr, ar * ar + ai * ai)
            for k in range(4):
                w, square = splats[slot, k : k + 1], splats[slot, 4 + k : 5 + k]
                totals[k][0] = totals[k][0] + w * pieces[0]
                totals[k][1] = totals[k][1] + w * pieces[1]
                totals[k][2] = totals[k][2] + square * pieces[2]
        for k in range(4):
            for f in range(3):
                sums[k, f, rows_here] = totals[k][f]
        pair_copy(i, d).start()
        return carry

    lax.fori_loop(0, n1, finish_rows, 0)
    order = FAR + (0,)
    pair_out = [pair_copy(i, d) for i, d in enumerate(order)]
    streams = (0, 1)
    sent = [[], []]

    def send_first(m, d):
        a, device = first_peer(d)
        sent[m].append(copy(half.at[m, :, chunk(a)], r1.at[m, d - 1], device))

    for d, c in zip(order, pair_out):
        c.wait_recv()
        a, _ = first_peer(d)
        half[:, :, chunk(a)] = sums[pl.ds(high, 2), :, chunk(a)] + got[:, :, chunk(a)]
        if d:
            send_first(0, d)
    for d in FAR:
        send_first(1, d)

    def numerators(step, carry):
        slots = [step * GROUP + i for i in range(GROUP)]
        spots = [spot(slot) for slot in slots]
        for i, slot in enumerate(slots):
            pr, pi = probes[slot, 0], probes[slot, 1]
            dr, di = deltas[slot, 0], deltas[slot, 1]
            for f, value in enumerate((pr * dr + pi * di, pr * di - pi * dr)):
                pad[i, f, n : 2 * n] = pltpu.roll(value, spots[i][1], 1)
        spread((0, 1), spots)
        return carry

    lax.fori_loop(0, cap // GROUP, numerators, 0)
    flush(pair_out + halo + edge)

    mine = chunk(p1)
    x_sent = [[], []]
    for m in streams:
        total = half[m, :, mine]
        for d, c in zip(FAR[::-1], sent[m][::-1]):
            c.wait_recv()
            total = total + r1[m, d - 1]
        r2[m, x] = total
        for d in range(1, nx):
            _, device = x_peer(d)
            x_sent[m].append(copy(r2.at[m, x], r2.at[m, x], device))
    second_sent = [[], []]
    for m in streams:
        for c in x_sent[m]:
            c.wait_recv()
        total = r2[m, 0]
        for a in range(1, nx):
            total = total + r2[m, a]
        r3[m, p2] = total
        for d in FAR:
            _, device = second_peer(d)
            second_sent[m].append(copy(r3.at[m, p2], r3.at[m, p2], device))
    edge += send_edges(slice(0, 2))
    gather = []
    for m in streams:
        for c in second_sent[m]:
            c.wait_recv()
        total = r3[m, 0]
        for a in range(1, n1):
            total = total + r3[m, a]
        fresh[high + m, :, mine] = modes[high + m, :, mine] + total[:2] / (total[2:] + RELAX)
        here = fresh.at[high + m, :, mine]
        to_peers = {}
        for d in FAR:
            _, device = first_peer(d)
            to_peers[d] = copy(here, here, device)
        gather.append(to_peers)
    late = [id(c) for to_peers in gather for c in to_peers.values()]
    early = [c for c in pending if id(c) not in late]
    here = fresh.at[high + 1, :, mine]
    pair = [copy(here, here, sibling)]

    for c in edge:
        c.wait_recv()
    west = unpack_low(ors[1] * ok(0, -1))
    east = unpack_high(ors[0] * ok(0, 1))
    for part, inner, vertical, lo, up in (
        (slice(0, 64), slice(64, 128), orv[1] * ok(-1, 0), orc[3] * ok(-1, -1), orc[2] * ok(-1, 1)),
        (slice(64, 128), slice(128, 192), orv[0] * ok(1, 0), orc[1] * ok(1, -1), orc[0] * ok(1, 1)),
    ):
        side = jnp.where(lanes_iota((3, 64, n)) < 64, west[:, part] + unpack_low(lo), east[:, part] + unpack_high(up))
        both_sums = centre(slice(0, 3), inner) + vertical + side
        new_object[:, part] = obj[:, part] + both_sums[:2] / (both_sums[2:] + RELAX)

    flush(early)
    for d in NEAR:
        gather[0][d].wait_recv()
    pair.append(copy(fresh.at[high], fresh.at[high], sibling))
    for d in NEAR:
        gather[1][d].wait_recv()
        here = fresh.at[high + 1, :, chunk(lax.rem(p1 + n1 - d, n1))]
        pair.append(copy(here, here, sibling))
    flush(list(gather[0].values()) + list(gather[1].values()))
    for c in pair:
        c.wait_recv()
    flush(list(pair))


def finish_kernel(object_in, fresh, object_out, modes_out, made, sem):
    first = pltpu.make_async_copy(object_in, object_out, sem.at[0])
    first.start()
    copies = [first]
    scale = 1.0 / (fresh.shape[2] * fresh.shape[3])

    def mean(v):
        return jnp.sum(jnp.sum(v, 0, keepdims=True), 1, keepdims=True) * scale

    basis = []
    coefs = {}
    for k in range(4):
        vr, vi = fresh[k, 0], fresh[k, 1]
        for j in range(k):
            cr, ci = coefs[j, k]
            br, bi = basis[j]
            vr = vr - (cr * br - ci * bi)
            vi = vi - (cr * bi + ci * br)
        inner = {}
        for later in range(k + 1, 4):
            fr, fi = fresh[later, 0], fresh[later, 1]
            inner[later] = (mean(vr * fr + vi * fi), mean(vr * fi - vi * fr))
        norm = 1.0 / jnp.sqrt(mean(vr * vr + vi * vi) + EPSILON)
        qr, qi = vr * norm, vi * norm
        for later in range(k + 1, 4):
            coefs[k, later] = (norm * inner[later][0], norm * inner[later][1])
        basis.append((qr, qi))
        made[k, 0] = qr
        made[k, 1] = qi
        write = pltpu.make_async_copy(made.at[k], modes_out.at[k], sem.at[k + 1])
        write.start()
        copies.append(write)
    for c in copies:
        c.wait()


def solution(mesh):
    rows, cols = mesh.shape["row"], mesh.shape["col"]
    nx = 4
    n1 = cols // 2
    f32, bf16, i32 = jnp.float32, jnp.bfloat16, jnp.int32

    def body(object_field, amplitudes, counts, offsets, mode_index, mix_table, probe_modes):
        cap, mixes = amplitudes.shape[2], mix_table.shape[0]
        number = 24 + 6 * (n1 - 1) + 2 * (nx - 1) + n1 + 1
        new_object, fresh = pl.pallas_call(
            functools.partial(kernel, rows, cols, nx, n1, cap, mixes),
            out_shape=(
                pltpu.VMEM((2, 128, 128), f32),
                pltpu.VMEM((4, 2, 128, 128), f32),
            ),
            in_specs=[HBM] * 8,
            out_specs=(VMEM, VMEM),
            scratch_shapes=[
                pltpu.VMEM((2, 128, 128), f32),
                pltpu.VMEM(amplitudes.shape, bf16),
                pltpu.SMEM((1, 1), i32),
                pltpu.SMEM((1, 1, 2, cap), i32),
                pltpu.SMEM((1, 1, cap), i32),
                pltpu.SMEM((4, mixes), f32),
                pltpu.VMEM((4, 2, 128, 128), f32),
                pltpu.VMEM((2, 256, 256), bf16),
                pltpu.VMEM((2, 2, 64, 128), f32),
                pltpu.VMEM((4, 2, 32, 128), f32),
                pltpu.VMEM((2, 2, 64, 128), f32),
                pltpu.VMEM((2, 2, 64, 128), f32),
                pltpu.VMEM((4, 2, 32, 128), f32),
                pltpu.VMEM((2, 2, 256, 128), f32),
                pltpu.VMEM((cap, 2, 128, 128), f32),
                pltpu.VMEM((cap, 2, 128, 128), f32),
                pltpu.VMEM((cap, 2, 128, 128), f32),
                pltpu.VMEM((cap, 8, 128), f32),
                pltpu.VMEM((4, 3, 128, 128), f32),
                pltpu.VMEM((GROUP, 3, 384, 128), f32),
                pltpu.VMEM((3, 2, 256, 128), f32),
                pltpu.VMEM((2, 3, 64, 128), f32),
                pltpu.VMEM((2, 3, 64, 128), f32),
                pltpu.VMEM((4, 3, 32, 128), f32),
                pltpu.VMEM((2, 3, 64, 128), f32),
                pltpu.VMEM((2, 3, 64, 128), f32),
                pltpu.VMEM((4, 3, 32, 128), f32),
                pltpu.VMEM((2, 3, 128, 128), f32),
                pltpu.VMEM((2, 3, 128, 128), f32),
                pltpu.VMEM((2, n1 - 1, 3, 128 // n1, 128), f32),
                pltpu.VMEM((2, nx, 3, 128 // n1, 128), f32),
                pltpu.VMEM((2, n1, 3, 128 // n1, 128), f32),
                pltpu.SemaphoreType.DMA((8,)),
                pltpu.SemaphoreType.DMA((number,)),
                pltpu.SemaphoreType.DMA((number,)),
                pltpu.SemaphoreType.DMA((n1,)),
                pltpu.SemaphoreType.DMA((n1,)),
            ],
            compiler_params=pltpu.CompilerParams(
                collective_id=0, has_side_effects=True, vmem_limit_bytes=56 * 1024 * 1024
            ),
            name="update",
        )(
            object_field, amplitudes, counts, jnp.swapaxes(offsets, 2, 3), mode_index, mix_table.T,
            probe_modes, jnp.asarray(tables(128)),
        )
        return pl.pallas_call(
            finish_kernel,
            out_shape=(
                jax.ShapeDtypeStruct((2, 128, 128), f32),
                jax.ShapeDtypeStruct((4, 2, 128, 128), f32),
            ),
            in_specs=[VMEM, VMEM],
            out_specs=(HBM, HBM),
            scratch_shapes=[pltpu.VMEM((4, 2, 128, 128), f32), pltpu.SemaphoreType.DMA((5,))],
            compiler_params=pltpu.CompilerParams(vmem_limit_bytes=8 * 1024 * 1024),
            name="finish",
        )(new_object, fresh)

    return jax.shard_map(
        body,
        mesh=mesh,
        in_specs=(
            P(None, "row", "col"),
            P("row", "col", None, None, None),
            P("row", "col"),
            P("row", "col", None, None),
            P("row", "col", None),
            P(),
            P(),
        ),
        out_specs=(P(None, "row", "col"), P()),
        check_vma=False,
    )
```

```python
import functools

import jax
import jax.numpy as jnp
import ml_dtypes
import numpy as np
from jax import lax
from jax.experimental import pallas as pl
from jax.experimental.pallas import tpu as pltpu
from jax.sharding import PartitionSpec as P

FLOOR = 0.25
RELAX = 0.5
EPSILON = 1e-06
GROUP = 2
TEAM = 12
FAR = (4, 3, 5, 2, 6, 1, 7)
NEAR = (1, 7, 2, 6, 3, 5, 4)
MESH = pl.DeviceIdType.MESH
VMEM = pl.BlockSpec(memory_space=pltpu.VMEM)
HBM = pl.BlockSpec(memory_space=pltpu.HBM)


def tables(size):
    index = np.arange(size)
    angle = (index[:, None] * index[None, :] % size).astype(np.float32) * np.float32(2.0 * np.pi / size)
    factor = np.float32(1.0 / np.sqrt(size))
    c = (np.cos(angle) * factor).astype(ml_dtypes.bfloat16)
    s = (np.sin(angle) * factor).astype(ml_dtypes.bfloat16)
    p = np.concatenate([np.concatenate([c, s], 1), np.concatenate([-s, c], 1)], 0)
    q = np.concatenate([np.concatenate([c, -s], 1), np.concatenate([s, c], 1)], 0)
    return np.stack([p, q])


def lanes_iota(shape):
    return lax.broadcasted_iota(jnp.int32, shape, len(shape) - 1)


def pack_low(x):
    n = x.shape[1] // 2
    a, b = x[:, :n], x[:, n:]
    return jnp.where(lanes_iota(a.shape) < 64, a, pltpu.roll(b, 64, 2))


def pack_high(x):
    n = x.shape[1] // 2
    a, b = x[:, :n], x[:, n:]
    return jnp.where(lanes_iota(a.shape) < 64, pltpu.roll(a, 64, 2), b)


def unpack_low(x):
    return jnp.concatenate([x, pltpu.roll(x, 64, 2)], 1)


def unpack_high(x):
    return jnp.concatenate([pltpu.roll(x, 64, 2), x], 1)


def place(rows, cols):
    row, col = lax.axis_index("row"), lax.axis_index("col")
    around = {}
    for dr in (-1, 0, 1):
        for dc in (-1, 0, 1):
            if dr or dc:
                around[dr, dc] = (lax.rem(row + dr + rows, rows), lax.rem(col + dc + cols, cols))
    return row, col, around


def inside(row, col, rows, cols, dr, dc):
    ok = jnp.float32(1.0)
    if dr == -1:
        ok = ok * (row > 0).astype(jnp.float32)
    if dr == 1:
        ok = ok * (row < rows - 1).astype(jnp.float32)
    if dc == -1:
        ok = ok * (col > 0).astype(jnp.float32)
    if dc == 1:
        ok = ok * (col < cols - 1).astype(jnp.float32)
    return ok


SIDES = [(-1, 0), (1, 0), (0, -1), (0, 1), (-1, -1), (-1, 1), (1, -1), (1, 1)]


def kernel(
    rows, cols, nx, n1, cap, mixes,
    o_hbm, a_hbm, counts_hbm, offs_hbm, index_hbm, mix_hbm, modes_hbm, tab_hbm,
    new_object, fresh,
    obj, amps, counts, offs, index, mix, modes, tab,
    ps, pc, rv, rs, rc, tiles, probes, patches, deltas, splats, sums, pad, marg,
    on, op, oc, orv, ors, orc, got, half, r1, r2, r3,
    load, send, recv, pair_send, pair_recv,
):
    n = 128
    nz = rows // nx
    row, col, around = place(rows, cols)
    x, z = row // nz, lax.rem(row, nz)
    y, core = col // 2, lax.rem(col, 2)
    p1 = z + core * (y - z)
    p2 = y + core * (z - y)
    sibling = (row, col + 1 - 2 * core)
    high = 2 * core
    other = 2 - high

    def first_peer(d):
        a = lax.rem(p1 + d, n1)
        return a, (x * nz + z + (1 - core) * (a - z), (y + core * (a - y)) * 2 + core)

    def second_peer(d):
        a = lax.rem(p2 + d, n1)
        return a, (x * nz + z + core * (a - z), (y + (1 - core) * (a - y)) * 2 + core)

    def x_peer(d):
        a = lax.rem(x + d, nx)
        return a, (a * nz + z, col)

    used = [0]
    pending = []

    def copy(src, dst, device):
        i = used[0]
        used[0] += 1
        made = pltpu.make_async_remote_copy(
            src_ref=src, dst_ref=dst, send_sem=send.at[i], recv_sem=recv.at[i],
            device_id=device, device_id_type=MESH,
        )
        made.start()
        pending.append(made)
        return made

    def flush(copies):
        for c in copies:
            c.wait_send()
        done = [id(c) for c in copies]
        pending[:] = [c for c in pending if id(c) not in done]

    def ok(dr, dc):
        return inside(row, col, rows, cols, dr, dc)

    barrier = pltpu.get_barrier_semaphore()
    partners = (
        [around[s] for s in SIDES]
        + [sibling]
        + [first_peer(d)[1] for d in range(1, n1)]
        + [second_peer(d)[1] for d in range(1, n1)]
        + [x_peer(d)[1] for d in range(1, nx)]
    )
    for device in partners:
        pl.semaphore_signal(barrier, inc=1, device_id=device, device_id_type=MESH)
    loads = [
        pltpu.make_async_copy(src, dst, load.at[i])
        for i, (src, dst) in enumerate(
            (
                (o_hbm, obj), (modes_hbm, modes), (mix_hbm, mix), (index_hbm, index), (counts_hbm, counts),
                (offs_hbm, offs), (tab_hbm, tab), (a_hbm, amps),
            )
        )
    ]
    for c in loads:
        c.start()

    loads[0].wait()
    ps[0] = pack_low(obj[...])
    ps[1] = pack_high(obj[...])
    pc[0] = pack_low(obj[:, :64])
    pc[1] = pack_high(obj[:, :64])
    pc[2] = pack_low(obj[:, 64:])
    pc[3] = pack_high(obj[:, 64:])
    pl.semaphore_wait(barrier, len(partners))
    halo = [
        copy(pc.at[0], rc.at[0], around[-1, -1]),
        copy(pc.at[1], rc.at[1], around[-1, 1]),
        copy(pc.at[2], rc.at[2], around[1, -1]),
        copy(pc.at[3], rc.at[3], around[1, 1]),
        copy(obj.at[:, 0:64], rv.at[0], around[-1, 0]),
        copy(obj.at[:, 64:128], rv.at[1], around[1, 0]),
        copy(ps.at[0], rs.at[0], around[0, -1]),
        copy(ps.at[1], rs.at[1], around[0, 1]),
    ]

    for c in loads[1:]:
        c.wait()
    marg[...] = jnp.zeros_like(marg)
    pad[...] = jnp.zeros_like(pad)
    count = counts[0, 0]

    def spot(slot):
        top = jnp.clip(offs[0, 0, 0, slot], 0, n - 1)
        left_px = jnp.clip(offs[0, 0, 1, slot], 0, n - 1)
        return top, left_px

    def weights_of(slot):
        pick = jnp.clip(index[0, 0, slot], 0, mixes - 1)
        return [jnp.where(slot < count, mix[k, pick], 0.0) for k in range(4)]

    def spread(frames, spots):
        for f in frames:
            for h in range(4):
                part = slice(h * 64, (h + 1) * 64)
                low, up = marg[f, 0, part], marg[f, 1, part]
                for i, (top, left_px) in enumerate(spots):
                    value = pad[i, f, pl.ds(n - top + h * 64, 64), :]
                    mask = lanes_iota((64, n)) >= left_px
                    low = low + jnp.where(mask, value, 0.0)
                    up = up + jnp.where(mask, 0.0, value)
                marg[f, 0, part] = low
                marg[f, 1, part] = up

    def centre(frames, part):
        own, end = marg[frames, 0, part], marg[frames, 1, part]
        return jnp.where(lanes_iota(own.shape) < 64, pltpu.roll(own, 64, 2), pltpu.roll(end, 64, 2))

    def send_edges(frames):
        top, middle, bottom = slice(0, 64), slice(64, 192), slice(192, 256)
        on[0, frames] = centre(frames, top)
        on[1, frames] = centre(frames, bottom)
        op[0, frames] = pack_low(marg[frames, 0, middle])
        op[1, frames] = pack_high(marg[frames, 1, middle])
        oc[0, frames] = pack_low(marg[frames, 0, top])
        oc[1, frames] = pack_high(marg[frames, 1, top])
        oc[2, frames] = pack_low(marg[frames, 0, bottom])
        oc[3, frames] = pack_high(marg[frames, 1, bottom])
        return [
            copy(oc.at[0, frames], orc.at[0, frames], around[-1, -1]),
            copy(oc.at[1, frames], orc.at[1, frames], around[-1, 1]),
            copy(oc.at[2, frames], orc.at[2, frames], around[1, -1]),
            copy(oc.at[3, frames], orc.at[3, frames], around[1, 1]),
            copy(on.at[0, frames], orv.at[0, frames], around[-1, 0]),
            copy(on.at[1, frames], orv.at[1, frames], around[1, 0]),
            copy(op.at[0, frames], ors.at[0, frames], around[0, -1]),
            copy(op.at[1, frames], ors.at[1, frames], around[0, 1]),
        ]

    def make_probes(step, carry):
        slots = [step * GROUP + i for i in range(GROUP)]
        spots = [spot(slot) for slot in slots]
        for i, slot in enumerate(slots):
            w = weights_of(slot)
            for k in range(4):
                splats[slot, k : k + 1] = jnp.broadcast_to(w[k], (1, n))
                splats[slot, 4 + k : 5 + k] = jnp.broadcast_to(w[k] * w[k], (1, n))
            probe = []
            for comp in range(2):
                total = w[0] * modes[0, comp]
                for k in range(1, 4):
                    total = total + w[k] * modes[k, comp]
                probes[slot, comp] = total
                probe.append(total)
            value = probe[0] * probe[0] + probe[1] * probe[1]
            pad[i, 2, n : 2 * n] = pltpu.roll(value, spots[i][1], 1)
        spread((2,), spots)
        return carry

    lax.fori_loop(0, cap // GROUP, make_probes, 0)
    edge = send_edges(slice(2, 3))
    for c in halo:
        c.wait_recv()

    def tile_rows(target, west, own, east):
        turned = pltpu.roll(own, 64, 2)
        low = lanes_iota(own.shape) < 64
        tiles[:, 0, target] = jnp.where(low, west, turned)
        tiles[:, 1, target] = jnp.where(low, turned, east)

    tile_rows(
        slice(0, 64), unpack_low(rc[3] * ok(-1, -1)), rv[1] * ok(-1, 0), unpack_high(rc[2] * ok(-1, 1))
    )
    tile_rows(slice(64, 192), unpack_low(rs[1] * ok(0, -1)), obj[...], unpack_high(rs[0] * ok(0, 1)))
    tile_rows(
        slice(192, 256), unpack_low(rc[1] * ok(1, -1)), rv[0] * ok(1, 0), unpack_high(rc[0] * ok(1, 1))
    )

    fwd, inv = tab[0], tab[1]

    def dot(a, b):
        return jnp.dot(a, b, preferred_element_type=jnp.float32)

    def left(table, res, ims):
        out = dot(table, jnp.concatenate([jnp.concatenate(res, 1), jnp.concatenate(ims, 1)], 0))
        return (
            [out[:n, i * n : (i + 1) * n] for i in range(len(res))],
            [out[n:, i * n : (i + 1) * n] for i in range(len(res))],
        )

    def right(table, res, ims):
        out = dot(jnp.concatenate([jnp.concatenate([a, b], 1) for a, b in zip(res, ims)], 0), table)
        return (
            [out[i * n : (i + 1) * n, :n] for i in range(len(res))],
            [out[i * n : (i + 1) * n, n:] for i in range(len(res))],
        )

    def lower(xs):
        return [v.astype(jnp.bfloat16) for v in xs]

    lane = lanes_iota((n, n))

    thick = n // n1

    def chunk(a):
        return pl.ds(pl.multiple_of(a * thick, thick), thick)

    def cut(step, carry):
        for i in range(GROUP):
            slot = step * GROUP + i
            top, left_px = spot(slot)
            mask = lane >= left_px
            for comp in range(2):
                a = tiles[comp, 0, pl.ds(top, n), :]
                b = tiles[comp, 1, pl.ds(top, n), :]
                patches[slot, comp] = pltpu.roll(jnp.where(mask, a, b), lax.rem(n - left_px, n), 1)
        return carry

    lax.fori_loop(0, cap // GROUP, cut, 0)

    def weigh_rows(i, carry):
        totals = [jnp.zeros((thick, n), jnp.float32) for _ in range(4)]
        for slot in range(cap):
            ar, ai = patches[slot, 0, chunk(i)], patches[slot, 1, chunk(i)]
            value = ar * ar + ai * ai
            for k in range(4):
                totals[k] = totals[k] + splats[slot, 4 + k : 5 + k] * value
        for k in range(4):
            sums[k, 2, chunk(i)] = totals[k]
        return carry

    lax.fori_loop(0, n1, weigh_rows, 0)
    dens_pair = copy(sums.at[pl.ds(other, 2), 2], got.at[:, 2], sibling)

    def visit(step, carry):
        slots = [step * TEAM + i for i in range(TEAM)]
        psi_r, psi_i = [], []
        for slot in slots:
            patch = (patches[slot, 0], patches[slot, 1])
            pr, pi = probes[slot, 0], probes[slot, 1]
            real = pr * patch[0] - pi * patch[1]
            imag = pr * patch[1] + pi * patch[0]
            psi_r.append(real)
            psi_i.append(imag)
        re, im = left(fwd, lower(psi_r), lower(psi_i))
        re, im = right(inv, lower(re), lower(im))
        fixed_re, fixed_im = [], []
        for slot, a, b in zip(slots, re, im):
            ratio = amps[0, 0, slot].astype(jnp.float32) * lax.rsqrt(jnp.maximum(a * a + b * b, FLOOR * FLOOR))
            fixed_re.append((a * ratio).astype(jnp.bfloat16))
            fixed_im.append((b * ratio).astype(jnp.bfloat16))
        re, im = left(inv, fixed_re, fixed_im)
        re, im = right(fwd, lower(re), lower(im))
        for i, slot in enumerate(slots):
            deltas[slot, 0] = re[i] - psi_r[i]
            deltas[slot, 1] = im[i] - psi_i[i]
        return carry

    lax.fori_loop(0, cap // TEAM, visit, 0)

    dens_pair.wait_recv()
    half[:, 2] = sums[pl.ds(high, 2), 2] + got[:, 2]
    dens_first = []
    for d in FAR:
        a, device = first_peer(d)
        dens_first.append(copy(half.at[:, 2, chunk(a)], r1.at[:, d - 1, 2], device))

    def pair_copy(i, d):
        piece = chunk(lax.rem(p2 + d, n1))
        return pltpu.make_async_remote_copy(
            src_ref=sums.at[pl.ds(other, 2), 0:2, piece], dst_ref=got.at[:, 0:2, piece],
            send_sem=pair_send.at[i], recv_sem=pair_recv.at[i], device_id=sibling, device_id_type=MESH,
        )

    def finish_rows(i, carry):
        d = n1 // 2 + (1 - 2 * lax.rem(i, 2)) * ((i + 1) // 2)
        rows_here = chunk(lax.rem(p2 + d, n1))
        totals = [[jnp.zeros((thick, n), jnp.float32) for _ in range(2)] for _ in range(4)]
        for slot in range(cap):
            dr, di = deltas[slot, 0, rows_here], deltas[slot, 1, rows_here]
            ar, ai = patches[slot, 0, rows_here], patches[slot, 1, rows_here]
            pieces = (ar * dr + ai * di, ar * di - ai * dr)
            for k in range(4):
                w = splats[slot, k : k + 1]
                totals[k][0] = totals[k][0] + w * pieces[0]
                totals[k][1] = totals[k][1] + w * pieces[1]
        for k in range(4):
            for f in range(2):
                sums[k, f, rows_here] = totals[k][f]
        pair_copy(i, d).start()
        return carry

    lax.fori_loop(0, n1, finish_rows, 0)
    order = FAR + (0,)
    pair_out = [pair_copy(i, d) for i, d in enumerate(order)]
    streams = (0, 1)
    sent = [[], []]

    def send_first(m, d):
        a, device = first_peer(d)
        sent[m].append(copy(half.at[m, 0:2, chunk(a)], r1.at[m, d - 1, 0:2], device))

    for d, c in zip(order, pair_out):
        c.wait_recv()
        a, _ = first_peer(d)
        half[:, 0:2, chunk(a)] = sums[pl.ds(high, 2), 0:2, chunk(a)] + got[:, 0:2, chunk(a)]
        if d:
            send_first(0, d)
    for d in FAR:
        send_first(1, d)

    def numerators(step, carry):
        slots = [step * GROUP + i for i in range(GROUP)]
        spots = [spot(slot) for slot in slots]
        for i, slot in enumerate(slots):
            pr, pi = probes[slot, 0], probes[slot, 1]
            dr, di = deltas[slot, 0], deltas[slot, 1]
            for f, value in enumerate((pr * dr + pi * di, pr * di - pi * dr)):
                pad[i, f, n : 2 * n] = pltpu.roll(value, spots[i][1], 1)
        spread((0, 1), spots)
        return carry

    lax.fori_loop(0, cap // GROUP, numerators, 0)
    flush(pair_out + halo + edge)

    mine = chunk(p1)
    parity = lax.rem(x, 2)
    total = half[:, 2, mine]
    for d, c in zip(FAR[::-1], dens_first[::-1]):
        c.wait_recv()
        total = total + r1[:, d - 1, 2]
    for t in range(2):
        r2[:, t, 2] = total[:, t * 8 : (t + 1) * 8]
    r2[:, 2 + x, 2] = r2[:, parity, 2]
    dens_x = []
    for d in range(1, nx):
        a, device = x_peer(d)
        dens_x.append(copy(r2.at[:, lax.rem(a, 2), 2], r2.at[:, 2 + x, 2], device))
    x_sent = [[], []]
    for m in streams:
        total = half[m, 0:2, mine]
        for d, c in zip(FAR[::-1], sent[m][::-1]):
            c.wait_recv()
            total = total + r1[m, d - 1, 0:2]
        for t in range(2):
            r2[m, t, 0:2] = total[:, t * 8 : (t + 1) * 8]
        r2[m, 2 + x, 0:2] = r2[m, parity, 0:2]
        for d in range(1, nx):
            a, device = x_peer(d)
            x_sent[m].append(copy(r2.at[m, lax.rem(a, 2), 0:2], r2.at[m, 2 + x, 0:2], device))
    for c in dens_x:
        c.wait_recv()
    second_sent = [[], []]
    for m in streams:
        for c in x_sent[m]:
            c.wait_recv()
        total = r2[m, 2]
        for a in range(1, nx):
            total = total + r2[m, 2 + a]
        r3[m, p2] = total
        for d in FAR:
            _, device = second_peer(d)
            second_sent[m].append(copy(r3.at[m, p2], r3.at[m, p2], device))
    edge += send_edges(slice(0, 2))
    unit = pl.ds(pl.multiple_of(p1 * thick + parity * 8, 8), 8)
    back_sent = []
    partner = ((x + 1 - 2 * parity) * nz + z, col)
    for m in streams:
        for c in second_sent[m]:
            c.wait_recv()
        total = r3[m, 0]
        for a in range(1, n1):
            total = total + r3[m, a]
        fresh[high + m, :, unit] = modes[high + m, :, unit] + total[:2] / (total[2:] + RELAX)
        here = fresh.at[high + m, :, unit]
        back_sent.append(copy(here, here, partner))
    gather = []
    for m in streams:
        back_sent[m].wait_recv()
        here = fresh.at[high + m, :, mine]
        to_peers = {}
        for d in FAR:
            _, device = first_peer(d)
            to_peers[d] = copy(here, here, device)
        gather.append(to_peers)
    late = [id(c) for to_peers in gather for c in to_peers.values()]
    early = [c for c in pending if id(c) not in late]
    here = fresh.at[high + 1, :, mine]
    pair = [copy(here, here, sibling)]

    for c in edge:
        c.wait_recv()
    west = unpack_low(ors[1] * ok(0, -1))
    east = unpack_high(ors[0] * ok(0, 1))
    for part, inner, vertical, lo, up in (
        (slice(0, 64), slice(64, 128), orv[1] * ok(-1, 0), orc[3] * ok(-1, -1), orc[2] * ok(-1, 1)),
        (slice(64, 128), slice(128, 192), orv[0] * ok(1, 0), orc[1] * ok(1, -1), orc[0] * ok(1, 1)),
    ):
        side = jnp.where(lanes_iota((3, 64, n)) < 64, west[:, part] + unpack_low(lo), east[:, part] + unpack_high(up))
        both_sums = centre(slice(0, 3), inner) + vertical + side
        new_object[:, part] = obj[:, part] + both_sums[:2] / (both_sums[2:] + RELAX)

    flush(early)
    for d in NEAR:
        gather[0][d].wait_recv()
    pair.append(copy(fresh.at[high], fresh.at[high], sibling))
    for d in NEAR:
        gather[1][d].wait_recv()
        here = fresh.at[high + 1, :, chunk(lax.rem(p1 + n1 - d, n1))]
        pair.append(copy(here, here, sibling))
    flush(list(gather[0].values()) + list(gather[1].values()))
    for c in pair:
        c.wait_recv()
    flush(list(pair))


def finish_kernel(object_in, fresh, object_out, modes_out, made, sem):
    first = pltpu.make_async_copy(object_in, object_out, sem.at[0])
    first.start()
    copies = [first]
    scale = 1.0 / (fresh.shape[2] * fresh.shape[3])

    def mean(v):
        return jnp.sum(jnp.sum(v, 0, keepdims=True), 1, keepdims=True) * scale

    basis = []
    coefs = {}
    for k in range(4):
        vr, vi = fresh[k, 0], fresh[k, 1]
        for j in range(k):
            cr, ci = coefs[j, k]
            br, bi = basis[j]
            vr = vr - (cr * br - ci * bi)
            vi = vi - (cr * bi + ci * br)
        inner = {}
        for later in range(k + 1, 4):
            fr, fi = fresh[later, 0], fresh[later, 1]
            inner[later] = (mean(vr * fr + vi * fi), mean(vr * fi - vi * fr))
        norm = 1.0 / jnp.sqrt(mean(vr * vr + vi * vi) + EPSILON)
        qr, qi = vr * norm, vi * norm
        for later in range(k + 1, 4):
            coefs[k, later] = (norm * inner[later][0], norm * inner[later][1])
        basis.append((qr, qi))
        made[k, 0] = qr
        made[k, 1] = qi
        write = pltpu.make_async_copy(made.at[k], modes_out.at[k], sem.at[k + 1])
        write.start()
        copies.append(write)
    for c in copies:
        c.wait()


def solution(mesh):
    rows, cols = mesh.shape["row"], mesh.shape["col"]
    nx = 4
    n1 = cols // 2
    f32, bf16, i32 = jnp.float32, jnp.bfloat16, jnp.int32

    def body(object_field, amplitudes, counts, offsets, mode_index, mix_table, probe_modes):
        cap, mixes = amplitudes.shape[2], mix_table.shape[0]
        number = 25 + 7 * (n1 - 1) + 3 * (nx - 1) + 2 + n1 + 1
        new_object, fresh = pl.pallas_call(
            functools.partial(kernel, rows, cols, nx, n1, cap, mixes),
            out_shape=(
                pltpu.VMEM((2, 128, 128), f32),
                pltpu.VMEM((4, 2, 128, 128), f32),
            ),
            in_specs=[HBM] * 8,
            out_specs=(VMEM, VMEM),
            scratch_shapes=[
                pltpu.VMEM((2, 128, 128), f32),
                pltpu.VMEM(amplitudes.shape, bf16),
                pltpu.SMEM((1, 1), i32),
                pltpu.SMEM((1, 1, 2, cap), i32),
                pltpu.SMEM((1, 1, cap), i32),
                pltpu.SMEM((4, mixes), f32),
                pltpu.VMEM((4, 2, 128, 128), f32),
                pltpu.VMEM((2, 256, 256), bf16),
                pltpu.VMEM((2, 2, 64, 128), f32),
                pltpu.VMEM((4, 2, 32, 128), f32),
                pltpu.VMEM((2, 2, 64, 128), f32),
                pltpu.VMEM((2, 2, 64, 128), f32),
                pltpu.VMEM((4, 2, 32, 128), f32),
                pltpu.VMEM((2, 2, 256, 128), f32),
                pltpu.VMEM((cap, 2, 128, 128), f32),
                pltpu.VMEM((cap, 2, 128, 128), f32),
                pltpu.VMEM((cap, 2, 128, 128), f32),
                pltpu.VMEM((cap, 8, 128), f32),
                pltpu.VMEM((4, 3, 128, 128), f32),
                pltpu.VMEM((GROUP, 3, 384, 128), f32),
                pltpu.VMEM((3, 2, 256, 128), f32),
                pltpu.VMEM((2, 3, 64, 128), f32),
                pltpu.VMEM((2, 3, 64, 128), f32),
                pltpu.VMEM((4, 3, 32, 128), f32),
                pltpu.VMEM((2, 3, 64, 128), f32),
                pltpu.VMEM((2, 3, 64, 128), f32),
                pltpu.VMEM((4, 3, 32, 128), f32),
                pltpu.VMEM((2, 3, 128, 128), f32),
                pltpu.VMEM((2, 3, 128, 128), f32),
                pltpu.VMEM((2, n1 - 1, 3, 128 // n1, 128), f32),
                pltpu.VMEM((2, 2 + nx, 3, 8, 128), f32),
                pltpu.VMEM((2, n1, 3, 8, 128), f32),
                pltpu.SemaphoreType.DMA((8,)),
                pltpu.SemaphoreType.DMA((number,)),
                pltpu.SemaphoreType.DMA((number,)),
                pltpu.SemaphoreType.DMA((n1,)),
                pltpu.SemaphoreType.DMA((n1,)),
            ],
            compiler_params=pltpu.CompilerParams(
                collective_id=0, has_side_effects=True, vmem_limit_bytes=56 * 1024 * 1024
            ),
            name="update",
        )(
            object_field, amplitudes, counts, jnp.swapaxes(offsets, 2, 3), mode_index, mix_table.T,
            probe_modes, jnp.asarray(tables(128)),
        )
        return pl.pallas_call(
            finish_kernel,
            out_shape=(
                jax.ShapeDtypeStruct((2, 128, 128), f32),
                jax.ShapeDtypeStruct((4, 2, 128, 128), f32),
            ),
            in_specs=[VMEM, VMEM],
            out_specs=(HBM, HBM),
            scratch_shapes=[pltpu.VMEM((4, 2, 128, 128), f32), pltpu.SemaphoreType.DMA((5,))],
            compiler_params=pltpu.CompilerParams(vmem_limit_bytes=8 * 1024 * 1024),
            name="finish",
        )(new_object, fresh)

    return jax.shard_map(
        body,
        mesh=mesh,
        in_specs=(
            P(None, "row", "col"),
            P("row", "col", None, None, None),
            P("row", "col"),
            P("row", "col", None, None),
            P("row", "col", None),
            P(),
            P(),
        ),
        out_specs=(P(None, "row", "col"), P()),
        check_vma=False,
    )
```

```python
import functools

import jax
import jax.numpy as jnp
import ml_dtypes
import numpy as np
from jax import lax
from jax.experimental import pallas as pl
from jax.experimental.pallas import tpu as pltpu
from jax.sharding import PartitionSpec as P

FLOOR = 0.25
RELAX = 0.5
EPSILON = 1e-06
GROUP = 2
TEAM = 12
FAR = (4, 3, 5, 2, 6, 1, 7)
NEAR = (1, 7, 2, 6, 3, 5, 4)
MESH = pl.DeviceIdType.MESH
VMEM = pl.BlockSpec(memory_space=pltpu.VMEM)
HBM = pl.BlockSpec(memory_space=pltpu.HBM)


def tables(size):
    index = np.arange(size)
    angle = (index[:, None] * index[None, :] % size).astype(np.float32) * np.float32(2.0 * np.pi / size)
    factor = np.float32(1.0 / np.sqrt(size))
    c = (np.cos(angle) * factor).astype(ml_dtypes.bfloat16)
    s = (np.sin(angle) * factor).astype(ml_dtypes.bfloat16)
    p = np.concatenate([np.concatenate([c, s], 1), np.concatenate([-s, c], 1)], 0)
    q = np.concatenate([np.concatenate([c, -s], 1), np.concatenate([s, c], 1)], 0)
    return np.stack([p, q])


def lanes_iota(shape):
    return lax.broadcasted_iota(jnp.int32, shape, len(shape) - 1)


def pack_low(x):
    n = x.shape[1] // 2
    a, b = x[:, :n], x[:, n:]
    return jnp.where(lanes_iota(a.shape) < 64, a, pltpu.roll(b, 64, 2))


def pack_high(x):
    n = x.shape[1] // 2
    a, b = x[:, :n], x[:, n:]
    return jnp.where(lanes_iota(a.shape) < 64, pltpu.roll(a, 64, 2), b)


def unpack_low(x):
    return jnp.concatenate([x, pltpu.roll(x, 64, 2)], 1)


def unpack_high(x):
    return jnp.concatenate([pltpu.roll(x, 64, 2), x], 1)


def place(rows, cols):
    row, col = lax.axis_index("row"), lax.axis_index("col")
    around = {}
    for dr in (-1, 0, 1):
        for dc in (-1, 0, 1):
            if dr or dc:
                around[dr, dc] = (lax.rem(row + dr + rows, rows), lax.rem(col + dc + cols, cols))
    return row, col, around


def inside(row, col, rows, cols, dr, dc):
    ok = jnp.float32(1.0)
    if dr == -1:
        ok = ok * (row > 0).astype(jnp.float32)
    if dr == 1:
        ok = ok * (row < rows - 1).astype(jnp.float32)
    if dc == -1:
        ok = ok * (col > 0).astype(jnp.float32)
    if dc == 1:
        ok = ok * (col < cols - 1).astype(jnp.float32)
    return ok


SIDES = [(-1, 0), (1, 0), (0, -1), (0, 1), (-1, -1), (-1, 1), (1, -1), (1, 1)]


def kernel(
    rows, cols, nx, n1, cap, mixes,
    o_hbm, a_hbm, counts_hbm, offs_hbm, index_hbm, mix_hbm, modes_hbm, tab_hbm,
    new_object, fresh,
    obj, amps, counts, offs, index, mix, modes, tab,
    ps, pc, rv, rs, rc, tiles, probes, patches, deltas, splats, sums, pad, marg,
    on, op, oc, orv, ors, orc, got, half, r1, r2, r3,
    load, send, recv, pair_send, pair_recv,
):
    n = 128
    nz = rows // nx
    row, col, around = place(rows, cols)
    x, z = row // nz, lax.rem(row, nz)
    y, core = col // 2, lax.rem(col, 2)
    p1 = z + core * (y - z)
    p2 = y + core * (z - y)
    sibling = (row, col + 1 - 2 * core)
    high = 2 * core
    other = 2 - high

    def first_peer(d):
        a = lax.rem(p1 + d, n1)
        return a, (x * nz + z + (1 - core) * (a - z), (y + core * (a - y)) * 2 + core)

    def second_peer(d):
        a = lax.rem(p2 + d, n1)
        return a, (x * nz + z + core * (a - z), (y + (1 - core) * (a - y)) * 2 + core)

    def x_peer(d):
        a = lax.rem(x + d, nx)
        return a, (a * nz + z, col)

    used = [0]
    pending = []

    def copy(src, dst, device):
        i = used[0]
        used[0] += 1
        made = pltpu.make_async_remote_copy(
            src_ref=src, dst_ref=dst, send_sem=send.at[i], recv_sem=recv.at[i],
            device_id=device, device_id_type=MESH,
        )
        made.start()
        pending.append(made)
        return made

    def flush(copies):
        for c in copies:
            c.wait_send()
        done = [id(c) for c in copies]
        pending[:] = [c for c in pending if id(c) not in done]

    def ok(dr, dc):
        return inside(row, col, rows, cols, dr, dc)

    barrier = pltpu.get_barrier_semaphore()
    partners = (
        [around[s] for s in SIDES]
        + [sibling]
        + [first_peer(d)[1] for d in range(1, n1)]
        + [second_peer(d)[1] for d in range(1, n1)]
        + [x_peer(d)[1] for d in range(1, nx)]
    )
    for device in partners:
        pl.semaphore_signal(barrier, inc=1, device_id=device, device_id_type=MESH)
    loads = [
        pltpu.make_async_copy(src, dst, load.at[i])
        for i, (src, dst) in enumerate(
            (
                (o_hbm, obj), (modes_hbm, modes), (mix_hbm, mix), (index_hbm, index), (counts_hbm, counts),
                (offs_hbm, offs), (tab_hbm, tab), (a_hbm, amps),
            )
        )
    ]
    for c in loads:
        c.start()

    loads[0].wait()
    ps[0] = pack_low(obj[...])
    ps[1] = pack_high(obj[...])
    pc[0] = pack_low(obj[:, :64])
    pc[1] = pack_high(obj[:, :64])
    pc[2] = pack_low(obj[:, 64:])
    pc[3] = pack_high(obj[:, 64:])
    pl.semaphore_wait(barrier, len(partners))
    halo = [
        copy(pc.at[0], rc.at[0], around[-1, -1]),
        copy(pc.at[1], rc.at[1], around[-1, 1]),
        copy(pc.at[2], rc.at[2], around[1, -1]),
        copy(pc.at[3], rc.at[3], around[1, 1]),
        copy(obj.at[:, 0:64], rv.at[0], around[-1, 0]),
        copy(obj.at[:, 64:128], rv.at[1], around[1, 0]),
        copy(ps.at[0], rs.at[0], around[0, -1]),
        copy(ps.at[1], rs.at[1], around[0, 1]),
    ]

    for c in loads[1:]:
        c.wait()
    marg[...] = jnp.zeros_like(marg)
    pad[...] = jnp.zeros_like(pad)
    count = counts[0, 0]

    def spot(slot):
        top = jnp.clip(offs[0, 0, 0, slot], 0, n - 1)
        left_px = jnp.clip(offs[0, 0, 1, slot], 0, n - 1)
        return top, left_px

    def weights_of(slot):
        pick = jnp.clip(index[0, 0, slot], 0, mixes - 1)
        return [jnp.where(slot < count, mix[k, pick], 0.0) for k in range(4)]

    def spread(frames, spots):
        for f in frames:
            for h in range(4):
                part = slice(h * 64, (h + 1) * 64)
                low, up = marg[f, 0, part], marg[f, 1, part]
                for i, (top, left_px) in enumerate(spots):
                    value = pad[i, f, pl.ds(n - top + h * 64, 64), :]
                    mask = lanes_iota((64, n)) >= left_px
                    low = low + jnp.where(mask, value, 0.0)
                    up = up + jnp.where(mask, 0.0, value)
                marg[f, 0, part] = low
                marg[f, 1, part] = up

    def centre(frames, part):
        own, end = marg[frames, 0, part], marg[frames, 1, part]
        return jnp.where(lanes_iota(own.shape) < 64, pltpu.roll(own, 64, 2), pltpu.roll(end, 64, 2))

    def send_edges(frames):
        top, middle, bottom = slice(0, 64), slice(64, 192), slice(192, 256)
        on[0, frames] = centre(frames, top)
        on[1, frames] = centre(frames, bottom)
        op[0, frames] = pack_low(marg[frames, 0, middle])
        op[1, frames] = pack_high(marg[frames, 1, middle])
        oc[0, frames] = pack_low(marg[frames, 0, top])
        oc[1, frames] = pack_high(marg[frames, 1, top])
        oc[2, frames] = pack_low(marg[frames, 0, bottom])
        oc[3, frames] = pack_high(marg[frames, 1, bottom])
        return [
            copy(oc.at[0, frames], orc.at[0, frames], around[-1, -1]),
            copy(oc.at[1, frames], orc.at[1, frames], around[-1, 1]),
            copy(oc.at[2, frames], orc.at[2, frames], around[1, -1]),
            copy(oc.at[3, frames], orc.at[3, frames], around[1, 1]),
            copy(on.at[0, frames], orv.at[0, frames], around[-1, 0]),
            copy(on.at[1, frames], orv.at[1, frames], around[1, 0]),
            copy(op.at[0, frames], ors.at[0, frames], around[0, -1]),
            copy(op.at[1, frames], ors.at[1, frames], around[0, 1]),
        ]

    def make_probes(step, carry):
        slots = [step * GROUP + i for i in range(GROUP)]
        spots = [spot(slot) for slot in slots]
        for i, slot in enumerate(slots):
            w = weights_of(slot)
            for k in range(4):
                splats[slot, k : k + 1] = jnp.broadcast_to(w[k], (1, n))
                splats[slot, 4 + k : 5 + k] = jnp.broadcast_to(w[k] * w[k], (1, n))
            probe = []
            for comp in range(2):
                total = w[0] * modes[0, comp]
                for k in range(1, 4):
                    total = total + w[k] * modes[k, comp]
                probes[slot, comp] = total
                probe.append(total)
            value = probe[0] * probe[0] + probe[1] * probe[1]
            pad[i, 2, n : 2 * n] = pltpu.roll(value, spots[i][1], 1)
        spread((2,), spots)
        return carry

    lax.fori_loop(0, cap // GROUP, make_probes, 0)
    edge = []
    for c in halo:
        c.wait_recv()

    def tile_rows(target, west, own, east):
        turned = pltpu.roll(own, 64, 2)
        low = lanes_iota(own.shape) < 64
        tiles[:, 0, target] = jnp.where(low, west, turned)
        tiles[:, 1, target] = jnp.where(low, turned, east)

    tile_rows(
        slice(0, 64), unpack_low(rc[3] * ok(-1, -1)), rv[1] * ok(-1, 0), unpack_high(rc[2] * ok(-1, 1))
    )
    tile_rows(slice(64, 192), unpack_low(rs[1] * ok(0, -1)), obj[...], unpack_high(rs[0] * ok(0, 1)))
    tile_rows(
        slice(192, 256), unpack_low(rc[1] * ok(1, -1)), rv[0] * ok(1, 0), unpack_high(rc[0] * ok(1, 1))
    )

    fwd, inv = tab[0], tab[1]

    def dot(a, b):
        return jnp.dot(a, b, preferred_element_type=jnp.float32)

    def left(table, res, ims):
        out = dot(table, jnp.concatenate([jnp.concatenate(res, 1), jnp.concatenate(ims, 1)], 0))
        return (
            [out[:n, i * n : (i + 1) * n] for i in range(len(res))],
            [out[n:, i * n : (i + 1) * n] for i in range(len(res))],
        )

    def right(table, res, ims):
        out = dot(jnp.concatenate([jnp.concatenate([a, b], 1) for a, b in zip(res, ims)], 0), table)
        return (
            [out[i * n : (i + 1) * n, :n] for i in range(len(res))],
            [out[i * n : (i + 1) * n, n:] for i in range(len(res))],
        )

    def lower(xs):
        return [v.astype(jnp.bfloat16) for v in xs]

    lane = lanes_iota((n, n))

    def visit(step, carry):
        slots = [step * TEAM + i for i in range(TEAM)]
        psi_r, psi_i = [], []
        for slot in slots:
            top, left_px = spot(slot)
            mask = lane >= left_px
            patch = []
            for comp in range(2):
                a = tiles[comp, 0, pl.ds(top, n), :]
                b = tiles[comp, 1, pl.ds(top, n), :]
                patch.append(pltpu.roll(jnp.where(mask, a, b), lax.rem(n - left_px, n), 1))
                patches[slot, comp] = patch[comp]
            pr, pi = probes[slot, 0], probes[slot, 1]
            real = pr * patch[0] - pi * patch[1]
            imag = pr * patch[1] + pi * patch[0]
            psi_r.append(real)
            psi_i.append(imag)
        re, im = left(fwd, lower(psi_r), lower(psi_i))
        re, im = right(inv, lower(re), lower(im))
        fixed_re, fixed_im = [], []
        for slot, a, b in zip(slots, re, im):
            ratio = amps[0, 0, slot].astype(jnp.float32) * lax.rsqrt(jnp.maximum(a * a + b * b, FLOOR * FLOOR))
            fixed_re.append((a * ratio).astype(jnp.bfloat16))
            fixed_im.append((b * ratio).astype(jnp.bfloat16))
        re, im = left(inv, fixed_re, fixed_im)
        re, im = right(fwd, lower(re), lower(im))
        for i, slot in enumerate(slots):
            deltas[slot, 0] = re[i] - psi_r[i]
            deltas[slot, 1] = im[i] - psi_i[i]
        return carry

    lax.fori_loop(0, cap // TEAM, visit, 0)

    thick = n // n1

    def chunk(a):
        return pl.ds(pl.multiple_of(a * thick, thick), thick)

    def pair_copy(i, d):
        piece = chunk(lax.rem(p2 + d, n1))
        return pltpu.make_async_remote_copy(
            src_ref=sums.at[pl.ds(other, 2), :, piece], dst_ref=got.at[:, :, piece],
            send_sem=pair_send.at[i], recv_sem=pair_recv.at[i], device_id=sibling, device_id_type=MESH,
        )

    def finish_rows(i, carry):
        d = n1 // 2 + (1 - 2 * lax.rem(i, 2)) * ((i + 1) // 2)
        rows_here = chunk(lax.rem(p2 + d, n1))
        totals = [[jnp.zeros((thick, n), jnp.float32) for _ in range(3)] for _ in range(4)]
        for slot in range(cap):
            dr, di = deltas[slot, 0, rows_here], deltas[slot, 1, rows_here]
            ar, ai = patches[slot, 0, rows_here], patches[slot, 1, rows_here]
            pieces = (ar * dr + ai * di, ar * di - ai * dr, ar * ar + ai * ai)
            for k in range(4):
                w, square = splats[slot, k : k + 1], splats[slot, 4 + k : 5 + k]
                totals[k][0] = totals[k][0] + w * pieces[0]
                totals[k][1] = totals[k][1] + w * pieces[1]
                totals[k][2] = totals[k][2] + square * pieces[2]
        for k in range(4):
            for f in range(3):
                sums[k, f, rows_here] = totals[k][f]
        pair_copy(i, d).start()
        return carry

    lax.fori_loop(0, n1, finish_rows, 0)
    order = FAR + (0,)
    pair_out = [pair_copy(i, d) for i, d in enumerate(order)]
    streams = (0, 1)
    sent = [[], []]

    def send_first(m, d):
        a, device = first_peer(d)
        sent[m].append(copy(half.at[m, :, chunk(a)], r1.at[m, d - 1], device))

    for d, c in zip(order, pair_out):
        c.wait_recv()
        a, _ = first_peer(d)
        half[:, :, chunk(a)] = sums[pl.ds(high, 2), :, chunk(a)] + got[:, :, chunk(a)]
        if d:
            send_first(0, d)
    for d in FAR:
        send_first(1, d)

    def numerators(step, carry):
        slots = [step * GROUP + i for i in range(GROUP)]
        spots = [spot(slot) for slot in slots]
        for i, slot in enumerate(slots):
            pr, pi = probes[slot, 0], probes[slot, 1]
            dr, di = deltas[slot, 0], deltas[slot, 1]
            for f, value in enumerate((pr * dr + pi * di, pr * di - pi * dr)):
                pad[i, f, n : 2 * n] = pltpu.roll(value, spots[i][1], 1)
        spread((0, 1), spots)
        return carry

    lax.fori_loop(0, cap // GROUP, numerators, 0)
    flush(pair_out + halo + edge)

    mine = chunk(p1)
    parity = lax.rem(x, 2)
    x_sent = [[], []]
    for m in streams:
        total = half[m, :, mine]
        for d, c in zip(FAR[::-1], sent[m][::-1]):
            c.wait_recv()
            total = total + r1[m, d - 1]
        for t in range(2):
            r2[m, t] = total[:, t * 8 : (t + 1) * 8]
        r2[m, 2 + x] = r2[m, parity]
        for d in range(1, nx):
            a, device = x_peer(d)
            x_sent[m].append(copy(r2.at[m, lax.rem(a, 2)], r2.at[m, 2 + x], device))
    second_sent = [[], []]
    for m in streams:
        for c in x_sent[m]:
            c.wait_recv()
        total = r2[m, 2]
        for a in range(1, nx):
            total = total + r2[m, 2 + a]
        r3[m, p2] = total
        for d in FAR:
            _, device = second_peer(d)
            second_sent[m].append(copy(r3.at[m, p2], r3.at[m, p2], device))
    edge += send_edges(slice(0, 3))
    unit = pl.ds(pl.multiple_of(p1 * thick + parity * 8, 8), 8)
    back_sent = []
    partner = ((x + 1 - 2 * parity) * nz + z, col)
    for m in streams:
        for c in second_sent[m]:
            c.wait_recv()
        total = r3[m, 0]
        for a in range(1, n1):
            total = total + r3[m, a]
        fresh[high + m, :, unit] = modes[high + m, :, unit] + total[:2] / (total[2:] + RELAX)
        here = fresh.at[high + m, :, unit]
        back_sent.append(copy(here, here, partner))
    gather = []
    for m in streams:
        back_sent[m].wait_recv()
        here = fresh.at[high + m, :, mine]
        to_peers = {}
        for d in FAR:
            _, device = first_peer(d)
            to_peers[d] = copy(here, here, device)
        gather.append(to_peers)
    late = [id(c) for to_peers in gather for c in to_peers.values()]
    early = [c for c in pending if id(c) not in late]
    here = fresh.at[high + 1, :, mine]
    pair = [copy(here, here, sibling)]

    for c in edge:
        c.wait_recv()
    west = unpack_low(ors[1] * ok(0, -1))
    east = unpack_high(ors[0] * ok(0, 1))
    for part, inner, vertical, lo, up in (
        (slice(0, 64), slice(64, 128), orv[1] * ok(-1, 0), orc[3] * ok(-1, -1), orc[2] * ok(-1, 1)),
        (slice(64, 128), slice(128, 192), orv[0] * ok(1, 0), orc[1] * ok(1, -1), orc[0] * ok(1, 1)),
    ):
        side = jnp.where(lanes_iota((3, 64, n)) < 64, west[:, part] + unpack_low(lo), east[:, part] + unpack_high(up))
        both_sums = centre(slice(0, 3), inner) + vertical + side
        new_object[:, part] = obj[:, part] + both_sums[:2] / (both_sums[2:] + RELAX)

    flush(early)
    for d in NEAR:
        gather[0][d].wait_recv()
    pair.append(copy(fresh.at[high], fresh.at[high], sibling))
    for d in NEAR:
        gather[1][d].wait_recv()
        here = fresh.at[high + 1, :, chunk(lax.rem(p1 + n1 - d, n1))]
        pair.append(copy(here, here, sibling))
    flush(list(gather[0].values()) + list(gather[1].values()))
    for c in pair:
        c.wait_recv()
    flush(list(pair))


def finish_kernel(object_in, fresh, object_out, modes_out, made, sem):
    first = pltpu.make_async_copy(object_in, object_out, sem.at[0])
    first.start()
    copies = [first]
    scale = 1.0 / (fresh.shape[2] * fresh.shape[3])

    def mean(v):
        return jnp.sum(jnp.sum(v, 0, keepdims=True), 1, keepdims=True) * scale

    basis = []
    coefs = {}
    for k in range(4):
        vr, vi = fresh[k, 0], fresh[k, 1]
        for j in range(k):
            cr, ci = coefs[j, k]
            br, bi = basis[j]
            vr = vr - (cr * br - ci * bi)
            vi = vi - (cr * bi + ci * br)
        inner = {}
        for later in range(k + 1, 4):
            fr, fi = fresh[later, 0], fresh[later, 1]
            inner[later] = (mean(vr * fr + vi * fi), mean(vr * fi - vi * fr))
        norm = 1.0 / jnp.sqrt(mean(vr * vr + vi * vi) + EPSILON)
        qr, qi = vr * norm, vi * norm
        for later in range(k + 1, 4):
            coefs[k, later] = (norm * inner[later][0], norm * inner[later][1])
        basis.append((qr, qi))
        made[k, 0] = qr
        made[k, 1] = qi
        write = pltpu.make_async_copy(made.at[k], modes_out.at[k], sem.at[k + 1])
        write.start()
        copies.append(write)
    for c in copies:
        c.wait()


def solution(mesh):
    rows, cols = mesh.shape["row"], mesh.shape["col"]
    nx = 4
    n1 = cols // 2
    f32, bf16, i32 = jnp.float32, jnp.bfloat16, jnp.int32

    def body(object_field, amplitudes, counts, offsets, mode_index, mix_table, probe_modes):
        cap, mixes = amplitudes.shape[2], mix_table.shape[0]
        number = 24 + 6 * (n1 - 1) + 2 * (nx - 1) + 2 + n1 + 1
        new_object, fresh = pl.pallas_call(
            functools.partial(kernel, rows, cols, nx, n1, cap, mixes),
            out_shape=(
                pltpu.VMEM((2, 128, 128), f32),
                pltpu.VMEM((4, 2, 128, 128), f32),
            ),
            in_specs=[HBM] * 8,
            out_specs=(VMEM, VMEM),
            scratch_shapes=[
                pltpu.VMEM((2, 128, 128), f32),
                pltpu.VMEM(amplitudes.shape, bf16),
                pltpu.SMEM((1, 1), i32),
                pltpu.SMEM((1, 1, 2, cap), i32),
                pltpu.SMEM((1, 1, cap), i32),
                pltpu.SMEM((4, mixes), f32),
                pltpu.VMEM((4, 2, 128, 128), f32),
                pltpu.VMEM((2, 256, 256), bf16),
                pltpu.VMEM((2, 2, 64, 128), f32),
                pltpu.VMEM((4, 2, 32, 128), f32),
                pltpu.VMEM((2, 2, 64, 128), f32),
                pltpu.VMEM((2, 2, 64, 128), f32),
                pltpu.VMEM((4, 2, 32, 128), f32),
                pltpu.VMEM((2, 2, 256, 128), f32),
                pltpu.VMEM((cap, 2, 128, 128), f32),
                pltpu.VMEM((cap, 2, 128, 128), f32),
                pltpu.VMEM((cap, 2, 128, 128), f32),
                pltpu.VMEM((cap, 8, 128), f32),
                pltpu.VMEM((4, 3, 128, 128), f32),
                pltpu.VMEM((GROUP, 3, 384, 128), f32),
                pltpu.VMEM((3, 2, 256, 128), f32),
                pltpu.VMEM((2, 3, 64, 128), f32),
                pltpu.VMEM((2, 3, 64, 128), f32),
                pltpu.VMEM((4, 3, 32, 128), f32),
                pltpu.VMEM((2, 3, 64, 128), f32),
                pltpu.VMEM((2, 3, 64, 128), f32),
                pltpu.VMEM((4, 3, 32, 128), f32),
                pltpu.VMEM((2, 3, 128, 128), f32),
                pltpu.VMEM((2, 3, 128, 128), f32),
                pltpu.VMEM((2, n1 - 1, 3, 128 // n1, 128), f32),
                pltpu.VMEM((2, 2 + nx, 3, 8, 128), f32),
                pltpu.VMEM((2, n1, 3, 8, 128), f32),
                pltpu.SemaphoreType.DMA((8,)),
                pltpu.SemaphoreType.DMA((number,)),
                pltpu.SemaphoreType.DMA((number,)),
                pltpu.SemaphoreType.DMA((n1,)),
                pltpu.SemaphoreType.DMA((n1,)),
            ],
            compiler_params=pltpu.CompilerParams(
                collective_id=0, has_side_effects=True, vmem_limit_bytes=56 * 1024 * 1024
            ),
            name="update",
        )(
            object_field, amplitudes, counts, jnp.swapaxes(offsets, 2, 3), mode_index, mix_table.T,
            probe_modes, jnp.asarray(tables(128)),
        )
        return pl.pallas_call(
            finish_kernel,
            out_shape=(
                jax.ShapeDtypeStruct((2, 128, 128), f32),
                jax.ShapeDtypeStruct((4, 2, 128, 128), f32),
            ),
            in_specs=[VMEM, VMEM],
            out_specs=(HBM, HBM),
            scratch_shapes=[pltpu.VMEM((4, 2, 128, 128), f32), pltpu.SemaphoreType.DMA((5,))],
            compiler_params=pltpu.CompilerParams(vmem_limit_bytes=8 * 1024 * 1024),
            name="finish",
        )(new_object, fresh)

    return jax.shard_map(
        body,
        mesh=mesh,
        in_specs=(
            P(None, "row", "col"),
            P("row", "col", None, None, None),
            P("row", "col"),
            P("row", "col", None, None),
            P("row", "col", None),
            P(),
            P(),
        ),
        out_specs=(P(None, "row", "col"), P()),
        check_vma=False,
    )
```

```python
import functools

import jax
import jax.numpy as jnp
import ml_dtypes
import numpy as np
from jax import lax
from jax.experimental import pallas as pl
from jax.experimental.pallas import tpu as pltpu
from jax.sharding import PartitionSpec as P

FLOOR = 0.25
RELAX = 0.5
EPSILON = 1e-06
GROUP = 2
TEAM = 12
FAR = (4, 3, 5, 2, 6, 1, 7)
NEAR = (1, 7, 2, 6, 3, 5, 4)
SIDE = (4, 3, 2, 5, 6, 1, 7)
MESH = pl.DeviceIdType.MESH
VMEM = pl.BlockSpec(memory_space=pltpu.VMEM)
HBM = pl.BlockSpec(memory_space=pltpu.HBM)


def tables(size):
    index = np.arange(size)
    angle = (index[:, None] * index[None, :] % size).astype(np.float32) * np.float32(2.0 * np.pi / size)
    factor = np.float32(1.0 / np.sqrt(size))
    c = (np.cos(angle) * factor).astype(ml_dtypes.bfloat16)
    s = (np.sin(angle) * factor).astype(ml_dtypes.bfloat16)
    p = np.concatenate([np.concatenate([c, s], 1), np.concatenate([-s, c], 1)], 0)
    q = np.concatenate([np.concatenate([c, -s], 1), np.concatenate([s, c], 1)], 0)
    return np.stack([p, q])


def lanes_iota(shape):
    return lax.broadcasted_iota(jnp.int32, shape, len(shape) - 1)


def pack_low(x):
    n = x.shape[1] // 2
    a, b = x[:, :n], x[:, n:]
    return jnp.where(lanes_iota(a.shape) < 64, a, pltpu.roll(b, 64, 2))


def pack_high(x):
    n = x.shape[1] // 2
    a, b = x[:, :n], x[:, n:]
    return jnp.where(lanes_iota(a.shape) < 64, pltpu.roll(a, 64, 2), b)


def unpack_low(x):
    return jnp.concatenate([x, pltpu.roll(x, 64, 2)], 1)


def unpack_high(x):
    return jnp.concatenate([pltpu.roll(x, 64, 2), x], 1)


def place(rows, cols):
    row, col = lax.axis_index("row"), lax.axis_index("col")
    around = {}
    for dr in (-1, 0, 1):
        for dc in (-1, 0, 1):
            if dr or dc:
                around[dr, dc] = (lax.rem(row + dr + rows, rows), lax.rem(col + dc + cols, cols))
    return row, col, around


def inside(row, col, rows, cols, dr, dc):
    ok = jnp.float32(1.0)
    if dr == -1:
        ok = ok * (row > 0).astype(jnp.float32)
    if dr == 1:
        ok = ok * (row < rows - 1).astype(jnp.float32)
    if dc == -1:
        ok = ok * (col > 0).astype(jnp.float32)
    if dc == 1:
        ok = ok * (col < cols - 1).astype(jnp.float32)
    return ok


SIDES = [(-1, 0), (1, 0), (0, -1), (0, 1), (-1, -1), (-1, 1), (1, -1), (1, 1)]


def kernel(
    rows, cols, nx, n1, cap, mixes,
    o_hbm, a_hbm, counts_hbm, offs_hbm, index_hbm, mix_hbm, modes_hbm, tab_hbm,
    new_object, fresh,
    obj, amps, counts, offs, index, mix, modes, tab,
    ps, pc, rv, rs, rc, tiles, probes, patches, deltas, splats, sums, pad, marg,
    on, op, oc, orv, ors, orc, got, half, r1, r2, r3,
    load, send, recv, pair_send, pair_recv,
):
    n = 128
    nz = rows // nx
    row, col, around = place(rows, cols)
    x, z = row // nz, lax.rem(row, nz)
    y, core = col // 2, lax.rem(col, 2)
    p1 = z + core * (y - z)
    p2 = y + core * (z - y)
    sibling = (row, col + 1 - 2 * core)
    high = 2 * core
    other = 2 - high

    def first_peer(d):
        a = lax.rem(p1 + d, n1)
        return a, (x * nz + z + (1 - core) * (a - z), (y + core * (a - y)) * 2 + core)

    def second_peer(d):
        a = lax.rem(p2 + d, n1)
        return a, (x * nz + z + core * (a - z), (y + (1 - core) * (a - y)) * 2 + core)

    def x_peer(d):
        a = lax.rem(x + d, nx)
        return a, (a * nz + z, col)

    used = [0]
    pending = []

    def copy(src, dst, device):
        i = used[0]
        used[0] += 1
        made = pltpu.make_async_remote_copy(
            src_ref=src, dst_ref=dst, send_sem=send.at[i], recv_sem=recv.at[i],
            device_id=device, device_id_type=MESH,
        )
        made.start()
        pending.append(made)
        return made

    def flush(copies):
        for c in copies:
            c.wait_send()
        done = [id(c) for c in copies]
        pending[:] = [c for c in pending if id(c) not in done]

    def ok(dr, dc):
        return inside(row, col, rows, cols, dr, dc)

    barrier = pltpu.get_barrier_semaphore()
    partners = (
        [around[s] for s in SIDES]
        + [sibling]
        + [first_peer(d)[1] for d in range(1, n1)]
        + [second_peer(d)[1] for d in range(1, n1)]
        + [x_peer(d)[1] for d in range(1, nx)]
    )
    for device in partners:
        pl.semaphore_signal(barrier, inc=1, device_id=device, device_id_type=MESH)
    loads = [
        pltpu.make_async_copy(src, dst, load.at[i])
        for i, (src, dst) in enumerate(
            (
                (o_hbm, obj), (modes_hbm, modes), (mix_hbm, mix), (index_hbm, index), (counts_hbm, counts),
                (offs_hbm, offs), (tab_hbm, tab), (a_hbm, amps),
            )
        )
    ]
    for c in loads:
        c.start()

    loads[0].wait()
    ps[0] = pack_low(obj[...])
    ps[1] = pack_high(obj[...])
    pc[0] = pack_low(obj[:, :64])
    pc[1] = pack_high(obj[:, :64])
    pc[2] = pack_low(obj[:, 64:])
    pc[3] = pack_high(obj[:, 64:])
    pl.semaphore_wait(barrier, len(partners))
    halo = [
        copy(pc.at[0], rc.at[0], around[-1, -1]),
        copy(pc.at[1], rc.at[1], around[-1, 1]),
        copy(pc.at[2], rc.at[2], around[1, -1]),
        copy(pc.at[3], rc.at[3], around[1, 1]),
        copy(obj.at[:, 0:64], rv.at[0], around[-1, 0]),
        copy(obj.at[:, 64:128], rv.at[1], around[1, 0]),
        copy(ps.at[0], rs.at[0], around[0, -1]),
        copy(ps.at[1], rs.at[1], around[0, 1]),
    ]

    for c in loads[1:]:
        c.wait()
    marg[...] = jnp.zeros_like(marg)
    pad[...] = jnp.zeros_like(pad)
    count = counts[0, 0]

    def spot(slot):
        top = jnp.clip(offs[0, 0, 0, slot], 0, n - 1)
        left_px = jnp.clip(offs[0, 0, 1, slot], 0, n - 1)
        return top, left_px

    def weights_of(slot):
        pick = jnp.clip(index[0, 0, slot], 0, mixes - 1)
        return [jnp.where(slot < count, mix[k, pick], 0.0) for k in range(4)]

    def spread(frames, spots):
        for f in frames:
            for h in range(4):
                part = slice(h * 64, (h + 1) * 64)
                low, up = marg[f, 0, part], marg[f, 1, part]
                for i, (top, left_px) in enumerate(spots):
                    value = pad[i, f, pl.ds(n - top + h * 64, 64), :]
                    mask = lanes_iota((64, n)) >= left_px
                    low = low + jnp.where(mask, value, 0.0)
                    up = up + jnp.where(mask, 0.0, value)
                marg[f, 0, part] = low
                marg[f, 1, part] = up

    def centre(frames, part):
        own, end = marg[frames, 0, part], marg[frames, 1, part]
        return jnp.where(lanes_iota(own.shape) < 64, pltpu.roll(own, 64, 2), pltpu.roll(end, 64, 2))

    def send_edges(frames):
        top, middle, bottom = slice(0, 64), slice(64, 192), slice(192, 256)
        on[0, frames] = centre(frames, top)
        on[1, frames] = centre(frames, bottom)
        op[0, frames] = pack_low(marg[frames, 0, middle])
        op[1, frames] = pack_high(marg[frames, 1, middle])
        oc[0, frames] = pack_low(marg[frames, 0, top])
        oc[1, frames] = pack_high(marg[frames, 1, top])
        oc[2, frames] = pack_low(marg[frames, 0, bottom])
        oc[3, frames] = pack_high(marg[frames, 1, bottom])
        return [
            copy(oc.at[0, frames], orc.at[0, frames], around[-1, -1]),
            copy(oc.at[1, frames], orc.at[1, frames], around[-1, 1]),
            copy(oc.at[2, frames], orc.at[2, frames], around[1, -1]),
            copy(oc.at[3, frames], orc.at[3, frames], around[1, 1]),
            copy(on.at[0, frames], orv.at[0, frames], around[-1, 0]),
            copy(on.at[1, frames], orv.at[1, frames], around[1, 0]),
            copy(op.at[0, frames], ors.at[0, frames], around[0, -1]),
            copy(op.at[1, frames], ors.at[1, frames], around[0, 1]),
        ]

    def make_probes(step, carry):
        slots = [step * GROUP + i for i in range(GROUP)]
        spots = [spot(slot) for slot in slots]
        for i, slot in enumerate(slots):
            w = weights_of(slot)
            for k in range(4):
                splats[slot, k : k + 1] = jnp.broadcast_to(w[k], (1, n))
                splats[slot, 4 + k : 5 + k] = jnp.broadcast_to(w[k] * w[k], (1, n))
            probe = []
            for comp in range(2):
                total = w[0] * modes[0, comp]
                for k in range(1, 4):
                    total = total + w[k] * modes[k, comp]
                probes[slot, comp] = total
                probe.append(total)
            value = probe[0] * probe[0] + probe[1] * probe[1]
            pad[i, 2, n : 2 * n] = pltpu.roll(value, spots[i][1], 1)
        spread((2,), spots)
        return carry

    lax.fori_loop(0, cap // GROUP, make_probes, 0)
    edge = []
    for c in halo:
        c.wait_recv()

    def tile_rows(target, west, own, east):
        turned = pltpu.roll(own, 64, 2)
        low = lanes_iota(own.shape) < 64
        tiles[:, 0, target] = jnp.where(low, west, turned)
        tiles[:, 1, target] = jnp.where(low, turned, east)

    tile_rows(
        slice(0, 64), unpack_low(rc[3] * ok(-1, -1)), rv[1] * ok(-1, 0), unpack_high(rc[2] * ok(-1, 1))
    )
    tile_rows(slice(64, 192), unpack_low(rs[1] * ok(0, -1)), obj[...], unpack_high(rs[0] * ok(0, 1)))
    tile_rows(
        slice(192, 256), unpack_low(rc[1] * ok(1, -1)), rv[0] * ok(1, 0), unpack_high(rc[0] * ok(1, 1))
    )

    fwd, inv = tab[0], tab[1]

    def dot(a, b):
        return jnp.dot(a, b, preferred_element_type=jnp.float32)

    def left(table, res, ims):
        out = dot(table, jnp.concatenate([jnp.concatenate(res, 1), jnp.concatenate(ims, 1)], 0))
        return (
            [out[:n, i * n : (i + 1) * n] for i in range(len(res))],
            [out[n:, i * n : (i + 1) * n] for i in range(len(res))],
        )

    def right(table, res, ims):
        out = dot(jnp.concatenate([jnp.concatenate([a, b], 1) for a, b in zip(res, ims)], 0), table)
        return (
            [out[i * n : (i + 1) * n, :n] for i in range(len(res))],
            [out[i * n : (i + 1) * n, n:] for i in range(len(res))],
        )

    def lower(xs):
        return [v.astype(jnp.bfloat16) for v in xs]

    lane = lanes_iota((n, n))

    def visit(step, carry):
        slots = [step * TEAM + i for i in range(TEAM)]
        psi_r, psi_i = [], []
        for slot in slots:
            top, left_px = spot(slot)
            mask = lane >= left_px
            patch = []
            for comp in range(2):
                a = tiles[comp, 0, pl.ds(top, n), :]
                b = tiles[comp, 1, pl.ds(top, n), :]
                patch.append(pltpu.roll(jnp.where(mask, a, b), lax.rem(n - left_px, n), 1))
                patches[slot, comp] = patch[comp]
            pr, pi = probes[slot, 0], probes[slot, 1]
            real = pr * patch[0] - pi * patch[1]
            imag = pr * patch[1] + pi * patch[0]
            psi_r.append(real)
            psi_i.append(imag)
        re, im = left(fwd, lower(psi_r), lower(psi_i))
        re, im = right(inv, lower(re), lower(im))
        fixed_re, fixed_im = [], []
        for slot, a, b in zip(slots, re, im):
            ratio = amps[0, 0, slot].astype(jnp.float32) * lax.rsqrt(jnp.maximum(a * a + b * b, FLOOR * FLOOR))
            fixed_re.append((a * ratio).astype(jnp.bfloat16))
            fixed_im.append((b * ratio).astype(jnp.bfloat16))
        re, im = left(inv, fixed_re, fixed_im)
        re, im = right(fwd, lower(re), lower(im))
        for i, slot in enumerate(slots):
            deltas[slot, 0] = re[i] - psi_r[i]
            deltas[slot, 1] = im[i] - psi_i[i]
        return carry

    lax.fori_loop(0, cap // TEAM, visit, 0)

    thick = n // n1

    def chunk(a):
        return pl.ds(pl.multiple_of(a * thick, thick), thick)

    def pair_copy(i, d):
        piece = chunk(lax.rem(p2 + d, n1))
        return pltpu.make_async_remote_copy(
            src_ref=sums.at[pl.ds(other, 2), :, piece], dst_ref=got.at[:, :, piece],
            send_sem=pair_send.at[i], recv_sem=pair_recv.at[i], device_id=sibling, device_id_type=MESH,
        )

    def finish_rows(i, carry):
        d = n1 // 2 + (1 - 2 * lax.rem(i, 2)) * ((i + 1) // 2)
        rows_here = chunk(lax.rem(p2 + d, n1))
        totals = [[jnp.zeros((thick, n), jnp.float32) for _ in range(3)] for _ in range(4)]
        for slot in range(cap):
            dr, di = deltas[slot, 0, rows_here], deltas[slot, 1, rows_here]
            ar, ai = patches[slot, 0, rows_here], patches[slot, 1, rows_here]
            pieces = (ar * dr + ai * di, ar * di - ai * dr, ar * ar + ai * ai)
            for k in range(4):
                w, square = splats[slot, k : k + 1], splats[slot, 4 + k : 5 + k]
                totals[k][0] = totals[k][0] + w * pieces[0]
                totals[k][1] = totals[k][1] + w * pieces[1]
                totals[k][2] = totals[k][2] + square * pieces[2]
        for k in range(4):
            for f in range(3):
                sums[k, f, rows_here] = totals[k][f]
        pair_copy(i, d).start()
        return carry

    lax.fori_loop(0, n1, finish_rows, 0)
    order = FAR + (0,)
    pair_out = [pair_copy(i, d) for i, d in enumerate(order)]
    streams = (0, 1)
    sent = [[], []]

    def send_first(m, d):
        a, device = first_peer(d)
        sent[m].append(copy(half.at[m, :, chunk(a)], r1.at[m, d - 1], device))

    for d, c in zip(order, pair_out):
        c.wait_recv()
        a, _ = first_peer(d)
        half[:, :, chunk(a)] = sums[pl.ds(high, 2), :, chunk(a)] + got[:, :, chunk(a)]
        if d:
            send_first(0, d)
    for d in SIDE:
        send_first(1, d)

    def numerators(step, carry):
        slots = [step * GROUP + i for i in range(GROUP)]
        spots = [spot(slot) for slot in slots]
        for i, slot in enumerate(slots):
            pr, pi = probes[slot, 0], probes[slot, 1]
            dr, di = deltas[slot, 0], deltas[slot, 1]
            for f, value in enumerate((pr * dr + pi * di, pr * di - pi * dr)):
                pad[i, f, n : 2 * n] = pltpu.roll(value, spots[i][1], 1)
        spread((0, 1), spots)
        return carry

    lax.fori_loop(0, cap // GROUP, numerators, 0)
    flush(pair_out + halo + edge)

    mine = chunk(p1)
    parity = lax.rem(x, 2)
    x_sent = [[], []]
    for m in streams:
        total = half[m, :, mine]
        for d, c in zip((FAR, SIDE)[m][::-1], sent[m][::-1]):
            c.wait_recv()
            total = total + r1[m, d - 1]
        for t in range(2):
            r2[m, t] = total[:, t * 8 : (t + 1) * 8]
        r2[m, 2 + x] = r2[m, parity]
        for d in range(1, nx):
            a, device = x_peer(d)
            x_sent[m].append(copy(r2.at[m, lax.rem(a, 2)], r2.at[m, 2 + x], device))
    second_sent = [[], []]
    for m in streams:
        for c in x_sent[m]:
            c.wait_recv()
        total = r2[m, 2]
        for a in range(1, nx):
            total = total + r2[m, 2 + a]
        r3[m, p2] = total
        for d in SIDE:
            _, device = second_peer(d)
            second_sent[m].append(copy(r3.at[m, p2], r3.at[m, p2], device))
    edge += send_edges(slice(0, 3))
    unit = pl.ds(pl.multiple_of(p1 * thick + parity * 8, 8), 8)
    back_sent = []
    partner = ((x + 1 - 2 * parity) * nz + z, col)
    for m in streams:
        for c in second_sent[m]:
            c.wait_recv()
        total = r3[m, 0]
        for a in range(1, n1):
            total = total + r3[m, a]
        fresh[high + m, :, unit] = modes[high + m, :, unit] + total[:2] / (total[2:] + RELAX)
        here = fresh.at[high + m, :, unit]
        back_sent.append(copy(here, here, partner))
    gather = []
    for m in streams:
        back_sent[m].wait_recv()
        here = fresh.at[high + m, :, mine]
        to_peers = {}
        for d in SIDE:
            _, device = first_peer(d)
            to_peers[d] = copy(here, here, device)
        gather.append(to_peers)
    late = [id(c) for to_peers in gather for c in to_peers.values()]
    early = [c for c in pending if id(c) not in late]
    here = fresh.at[high + 1, :, mine]
    pair = [copy(here, here, sibling)]

    for c in edge:
        c.wait_recv()
    west = unpack_low(ors[1] * ok(0, -1))
    east = unpack_high(ors[0] * ok(0, 1))
    for part, inner, vertical, lo, up in (
        (slice(0, 64), slice(64, 128), orv[1] * ok(-1, 0), orc[3] * ok(-1, -1), orc[2] * ok(-1, 1)),
        (slice(64, 128), slice(128, 192), orv[0] * ok(1, 0), orc[1] * ok(1, -1), orc[0] * ok(1, 1)),
    ):
        side = jnp.where(lanes_iota((3, 64, n)) < 64, west[:, part] + unpack_low(lo), east[:, part] + unpack_high(up))
        both_sums = centre(slice(0, 3), inner) + vertical + side
        new_object[:, part] = obj[:, part] + both_sums[:2] / (both_sums[2:] + RELAX)

    flush(early)
    for d in NEAR:
        gather[0][d].wait_recv()
    pair.append(copy(fresh.at[high], fresh.at[high], sibling))
    for d in NEAR:
        gather[1][d].wait_recv()
        here = fresh.at[high + 1, :, chunk(lax.rem(p1 + n1 - d, n1))]
        pair.append(copy(here, here, sibling))
    flush(list(gather[0].values()) + list(gather[1].values()))
    for c in pair:
        c.wait_recv()
    flush(list(pair))


def finish_kernel(object_in, fresh, object_out, modes_out, made, sem):
    first = pltpu.make_async_copy(object_in, object_out, sem.at[0])
    first.start()
    copies = [first]
    scale = 1.0 / (fresh.shape[2] * fresh.shape[3])

    def mean(v):
        return jnp.sum(jnp.sum(v, 0, keepdims=True), 1, keepdims=True) * scale

    basis = []
    coefs = {}
    for k in range(4):
        vr, vi = fresh[k, 0], fresh[k, 1]
        for j in range(k):
            cr, ci = coefs[j, k]
            br, bi = basis[j]
            vr = vr - (cr * br - ci * bi)
            vi = vi - (cr * bi + ci * br)
        inner = {}
        for later in range(k + 1, 4):
            fr, fi = fresh[later, 0], fresh[later, 1]
            inner[later] = (mean(vr * fr + vi * fi), mean(vr * fi - vi * fr))
        norm = 1.0 / jnp.sqrt(mean(vr * vr + vi * vi) + EPSILON)
        qr, qi = vr * norm, vi * norm
        for later in range(k + 1, 4):
            coefs[k, later] = (norm * inner[later][0], norm * inner[later][1])
        basis.append((qr, qi))
        made[k, 0] = qr
        made[k, 1] = qi
        write = pltpu.make_async_copy(made.at[k], modes_out.at[k], sem.at[k + 1])
        write.start()
        copies.append(write)
    for c in copies:
        c.wait()


def solution(mesh):
    rows, cols = mesh.shape["row"], mesh.shape["col"]
    nx = 4
    n1 = cols // 2
    f32, bf16, i32 = jnp.float32, jnp.bfloat16, jnp.int32

    def body(object_field, amplitudes, counts, offsets, mode_index, mix_table, probe_modes):
        cap, mixes = amplitudes.shape[2], mix_table.shape[0]
        number = 24 + 6 * (n1 - 1) + 2 * (nx - 1) + 2 + n1 + 1
        new_object, fresh = pl.pallas_call(
            functools.partial(kernel, rows, cols, nx, n1, cap, mixes),
            out_shape=(
                pltpu.VMEM((2, 128, 128), f32),
                pltpu.VMEM((4, 2, 128, 128), f32),
            ),
            in_specs=[HBM] * 8,
            out_specs=(VMEM, VMEM),
            scratch_shapes=[
                pltpu.VMEM((2, 128, 128), f32),
                pltpu.VMEM(amplitudes.shape, bf16),
                pltpu.SMEM((1, 1), i32),
                pltpu.SMEM((1, 1, 2, cap), i32),
                pltpu.SMEM((1, 1, cap), i32),
                pltpu.SMEM((4, mixes), f32),
                pltpu.VMEM((4, 2, 128, 128), f32),
                pltpu.VMEM((2, 256, 256), bf16),
                pltpu.VMEM((2, 2, 64, 128), f32),
                pltpu.VMEM((4, 2, 32, 128), f32),
                pltpu.VMEM((2, 2, 64, 128), f32),
                pltpu.VMEM((2, 2, 64, 128), f32),
                pltpu.VMEM((4, 2, 32, 128), f32),
                pltpu.VMEM((2, 2, 256, 128), f32),
                pltpu.VMEM((cap, 2, 128, 128), f32),
                pltpu.VMEM((cap, 2, 128, 128), f32),
                pltpu.VMEM((cap, 2, 128, 128), f32),
                pltpu.VMEM((cap, 8, 128), f32),
                pltpu.VMEM((4, 3, 128, 128), f32),
                pltpu.VMEM((GROUP, 3, 384, 128), f32),
                pltpu.VMEM((3, 2, 256, 128), f32),
                pltpu.VMEM((2, 3, 64, 128), f32),
                pltpu.VMEM((2, 3, 64, 128), f32),
                pltpu.VMEM((4, 3, 32, 128), f32),
                pltpu.VMEM((2, 3, 64, 128), f32),
                pltpu.VMEM((2, 3, 64, 128), f32),
                pltpu.VMEM((4, 3, 32, 128), f32),
                pltpu.VMEM((2, 3, 128, 128), f32),
                pltpu.VMEM((2, 3, 128, 128), f32),
                pltpu.VMEM((2, n1 - 1, 3, 128 // n1, 128), f32),
                pltpu.VMEM((2, 2 + nx, 3, 8, 128), f32),
                pltpu.VMEM((2, n1, 3, 8, 128), f32),
                pltpu.SemaphoreType.DMA((8,)),
                pltpu.SemaphoreType.DMA((number,)),
                pltpu.SemaphoreType.DMA((number,)),
                pltpu.SemaphoreType.DMA((n1,)),
                pltpu.SemaphoreType.DMA((n1,)),
            ],
            compiler_params=pltpu.CompilerParams(
                collective_id=0, has_side_effects=True, vmem_limit_bytes=56 * 1024 * 1024
            ),
            name="update",
        )(
            object_field, amplitudes, counts, jnp.swapaxes(offsets, 2, 3), mode_index, mix_table.T,
            probe_modes, jnp.asarray(tables(128)),
        )
        return pl.pallas_call(
            finish_kernel,
            out_shape=(
                jax.ShapeDtypeStruct((2, 128, 128), f32),
                jax.ShapeDtypeStruct((4, 2, 128, 128), f32),
            ),
            in_specs=[VMEM, VMEM],
            out_specs=(HBM, HBM),
            scratch_shapes=[pltpu.VMEM((4, 2, 128, 128), f32), pltpu.SemaphoreType.DMA((5,))],
            compiler_params=pltpu.CompilerParams(vmem_limit_bytes=8 * 1024 * 1024),
            name="finish",
        )(new_object, fresh)

    return jax.shard_map(
        body,
        mesh=mesh,
        in_specs=(
            P(None, "row", "col"),
            P("row", "col", None, None, None),
            P("row", "col"),
            P("row", "col", None, None),
            P("row", "col", None),
            P(),
            P(),
        ),
        out_specs=(P(None, "row", "col"), P()),
        check_vma=False,
    )
```
